32 devices in a mesh: req: 16 (over z, y, x), head: 2 (over core).
Axes of the slice: x: 2, y: 2, z: 4, core: 2. Of those that a mesh axis runs over, the one named last changes fastest.
Arguments:
- hidden_in: bfloat16 [768, 1536], P('req', 'head'), may hold values from -6 to 6
- norm_gain: float32 [1536], replicated, may hold values from 0.5 to 1.5
- proj_gate: bfloat16 [1536, 3072], P(None, 'head'), may hold values from -0.15625 to 0.15625
- proj_inner: bfloat16 [1536, 3072], P(None, 'head'), may hold values from -0.15625 to 0.15625
- proj_ssm: bfloat16 [1536, 256], P(None, 'head'), may hold values from -0.15625 to 0.15625
- proj_step: bfloat16 [1536, 48], P(None, 'head'), may hold values from -0.15625 to 0.15625
- step_bias: float32 [48], P('head'), may hold values from -6 to -1
- decay_log: float32 [48], P('head'), may hold values from 0 to 2.77
- skip_gain: float32 [48], P('head'), may hold values from 0.5 to 1.5
- conv_inner: bfloat16 [4, 3072], P(None, 'head'), may hold values from -3 to 3
- conv_inner_bias: float32 [3072], P('head'), may hold values from -3 to 3
- conv_ssm: bfloat16 [4, 256], replicated, may hold values from -3 to 3
- conv_ssm_bias: float32 [256], replicated, may hold values from -3 to 3
- gate_gain: float32 [3072], P('head'), may hold values from 0.5 to 1.5
- proj_out: bfloat16 [3072, 1536], P('head'), may hold values from -0.109375 to 0.109375
- states_in: bfloat16 [96, 48, 64, 128], P('req', 'head'), may hold values from -6 to 6
- edge_inner: bfloat16 [96, 3, 3072], P('req', None, 'head'), may hold values from -6 to 6
- edge_ssm: bfloat16 [96, 3, 256], P('req'), may hold values from -6 to 6
- draft_lengths: int32 [96], P('req'), may hold values from 1 to 8, as said below
- accepted: int32 [96], P('req'), may hold values from 0 to 8, as said below
- destination: int32 [96], P('req'), may hold values from 0 to 95, as said below
Outputs:
- hidden_out: bfloat16 [768, 1536], P('req', 'head')
- kept_state: bfloat16 [96, 48, 64, 128], P('req', 'head')
- kept_edge_inner: bfloat16 [96, 3, 3072], P('req', None, 'head')
- kept_edge_ssm: bfloat16 [96, 3, 256], P('req')
The draws below stay inside these ranges and needn't reach their ends.
Inputs may be any that keep to these rules, and one draw needn't show every extreme that they name: `draft_lengths`: in every draw some request has a draft of 8 tokens. accepted[r] <= draft_lengths[r]; in every draw some request accepts none and some accepts 8. `destination`: a permutation of the 96 output rows; row d lies on index d // 6 of req; a request on index i of req goes to index (i + k) mod 16 for some k of 0 .. 7; the 6 requests of one index use 6 different k, the same set of k on every index, so every index receives exactly one request from each of 6 senders.
All inputs are finite; a program needn't handle non-finite values.
Results may differ from the reference program's by a relative error of at most 0.015.
Values may be sent and summed in bfloat16 or wider, within the bound.
No kernel may reach another device: no remote copies, remote signals or barrier semaphores. Data moves between devices by JAX's collectives and lax.ppermute only.
A program may use at most 128 MiB of HBM per device.

```python
import jax
import jax.numpy as jnp
from jax import lax

D = 1536
HEADS = 48
HEAD_DIM = 64
NSTATE = 128
KCONV = 4
DRAFT = 8
WINDOW = 8
REQ_DEV = 6
DINNER = 3072
REQUESTS = 96
TOKENS = 768
N_REQ = 16


def draft_plan(key):
    base = jax.random.fold_in(key, 11)
    first, second, third, fourth = jax.random.split(base, 4)
    ceilings = jax.random.randint(first, (N_REQ, 1), 1, DRAFT + 1)
    raw_lengths = jax.random.randint(second, (N_REQ, REQ_DEV), 0, 1 << 20)
    lengths_all = (1 + raw_lengths % ceilings).reshape(-1)
    chosen = jax.random.randint(third, (), 0, REQUESTS)
    other = (chosen + 1) % REQUESTS
    rows = jnp.arange(REQUESTS, dtype=jnp.int32)
    lengths_all = jnp.where(rows == chosen, DRAFT, lengths_all)
    raw_accept = jax.random.randint(fourth, (REQUESTS,), 0, 1 << 20)
    accept_all = raw_accept % (lengths_all + 1)
    accept_all = jnp.where(rows == chosen, DRAFT, accept_all)
    accept_all = jnp.where(rows == other, 0, accept_all)
    return (lengths_all.astype(jnp.int32), accept_all.astype(jnp.int32))


def draw_draft_lengths(key, part):
    return draft_plan(key)[0]


def draw_accepted(key, part):
    return draft_plan(key)[1]


def draw_destination(key, part):
    base = jax.random.fold_in(key, 23)
    first, second = jax.random.split(base, 2)
    offsets = jax.random.permutation(first, WINDOW)[:REQ_DEV].astype(jnp.int32)
    order = jax.random.permutation(second, REQ_DEV).astype(jnp.int32)
    senders = jnp.arange(N_REQ, dtype=jnp.int32)[:, None]
    owners = (senders + offsets[None, :]) % N_REQ
    slots = (order[None, :] + owners) % REQ_DEV
    return (owners * REQ_DEV + slots).reshape(-1).astype(jnp.int32)


def steps_of(rng, extent, cuts, low, high):
    def one(dim, blocks):
        steps = jax.random.uniform(jax.random.fold_in(jax.random.fold_in(rng, 6), dim), (blocks,), jnp.float32, low / len(cuts), high / len(cuts))
        return jnp.repeat(jnp.exp(steps), extent[dim] // blocks).reshape((-1,) + (1,) * (len(extent) - dim - 1))

    level = one(*cuts[0])
    for cut in cuts[1:]:
        level = level * one(*cut)
    return level


def normal_values(key, dims, scale, limit, pieces=(), kind=jnp.bfloat16):
    drawn = jax.random.normal(key, dims, jnp.float32) * scale
    if len(pieces) > 0:
        drawn = steps_of(key, dims, pieces, -0.22, 0.18) * drawn
    return jnp.clip(drawn, min=-limit, max=limit).astype(kind)


def setup_inputs(seed: int = 0) -> dict:
    seeds = jax.random.split(jax.random.key(seed), 22)
    hidden_in = normal_values(seeds[0], (TOKENS, D), 1.0, 6.0, ((0, 16), (1, 2)))
    norm_gain = jnp.clip(1.0 + 0.1 * jax.random.normal(seeds[1], (D,), jnp.float32), 0.5, 1.5)
    proj_gate = normal_values(seeds[2], (D, DINNER), D ** -0.5, 0.15625, ((1, 2),))
    proj_inner = normal_values(seeds[3], (D, DINNER), D ** -0.5, 0.15625, ((1, 2),))
    proj_ssm = normal_values(seeds[4], (D, 2 * NSTATE), D ** -0.5, 0.15625, ((1, 2),))
    proj_step = normal_values(seeds[5], (D, HEADS), D ** -0.5, 0.15625, ((1, 2),))
    step_bias = jnp.clip(-6.0 + 5.0 * jax.random.uniform(seeds[6], (HEADS,), jnp.float32) ** steps_of(seeds[6], (HEADS,), ((0, 2),), -0.2, 0.2), -6.0, -1.0)
    decay_log = jnp.clip(2.77 * jax.random.uniform(seeds[7], (HEADS,), jnp.float32) ** steps_of(seeds[7], (HEADS,), ((0, 2),), -0.2, 0.2), 0.0, 2.77)
    skip_gain = jnp.clip(0.5 + 1.0 * jax.random.uniform(seeds[8], (HEADS,), jnp.float32) ** steps_of(seeds[8], (HEADS,), ((0, 2),), -0.2, 0.2), 0.5, 1.5)
    conv_inner = normal_values(seeds[9], (KCONV, DINNER), KCONV ** -0.5, 3.0, ((1, 2),))
    conv_inner_bias = normal_values(seeds[10], (DINNER,), 0.5, 3.0, ((0, 2),), jnp.float32)
    conv_ssm = normal_values(seeds[11], (KCONV, 2 * NSTATE), KCONV ** -0.5, 3.0)
    conv_ssm_bias = normal_values(seeds[12], (2 * NSTATE,), 0.5, 3.0, (), jnp.float32)
    gate_gain = jnp.clip(1.0 + 0.1 * jax.random.normal(seeds[13], (DINNER,), jnp.float32), 0.5, 1.5)
    proj_out = normal_values(seeds[14], (DINNER, D), DINNER ** -0.5, 0.109375, ((0, 2),))
    states_in = normal_values(seeds[15], (REQUESTS, HEADS, HEAD_DIM, NSTATE), 1.0, 6.0, ((0, 16), (1, 2)))
    edge_inner = normal_values(seeds[16], (REQUESTS, KCONV - 1, DINNER), 1.0, 6.0, ((0, 16), (2, 2)))
    edge_ssm = normal_values(seeds[17], (REQUESTS, KCONV - 1, 2 * NSTATE), 1.0, 6.0, ((0, 16),))
    draft_lengths = draw_draft_lengths(jax.random.fold_in(seeds[21], 71), 0)
    accepted = draw_accepted(jax.random.fold_in(seeds[21], 71), 0)
    destination = draw_destination(jax.random.fold_in(seeds[21], 71), 0)
    return dict(hidden_in=hidden_in, norm_gain=norm_gain, proj_gate=proj_gate, proj_inner=proj_inner, proj_ssm=proj_ssm, proj_step=proj_step, step_bias=step_bias, decay_log=decay_log, skip_gain=skip_gain, conv_inner=conv_inner, conv_inner_bias=conv_inner_bias, conv_ssm=conv_ssm, conv_ssm_bias=conv_ssm_bias, gate_gain=gate_gain, proj_out=proj_out, states_in=states_in, edge_inner=edge_inner, edge_ssm=edge_ssm, draft_lengths=draft_lengths, accepted=accepted, destination=destination)


epsilon = 1e-05

def causal_conv(edge, rows, weight, bias):
    full = jnp.concatenate([edge, rows], axis=1)
    total = jnp.zeros(rows.shape, jnp.float32) + bias.astype(jnp.float32)
    for offset in range(KCONV):
        total = total + full[:, offset:offset + DRAFT, :].astype(jnp.float32) * weight[offset].astype(jnp.float32)
    return (jax.nn.silu(total).astype(jnp.bfloat16), full)

def edge_rows(full, accepted):
    index = accepted[:, None] + jnp.arange(KCONV - 1, dtype=jnp.int32)[None, :]
    return jnp.take_along_axis(full, index[:, :, None].astype(jnp.int32), axis=1)

def advance(state, kept, step_now, inner_now, bmat, cmat, rates, skip_gain, accepted, position):
    state = jnp.exp(step_now * rates)[:, :, None, None] * state + (step_now[:, :, None] * inner_now)[:, :, :, None] * bmat[:, None, None, :]
    output = jnp.einsum('rhpn,rn->rhp', state, cmat, precision=lax.Precision.HIGHEST) + skip_gain[None, :, None] * inner_now
    kept = jnp.where((accepted == position + 1)[:, None, None, None], state, kept)
    return (state, kept, output)

def reference(hidden_in, norm_gain, proj_gate, proj_inner, proj_ssm, proj_step, step_bias, decay_log, skip_gain, conv_inner, conv_inner_bias, conv_ssm, conv_ssm_bias, gate_gain, proj_out, states_in, edge_inner, edge_ssm, draft_lengths, accepted, destination):
    wide = hidden_in.astype(jnp.float32)
    normed = (wide * lax.rsqrt(lax.optimization_barrier(jnp.mean(wide * wide, axis=-1, keepdims=True)) + epsilon) * norm_gain).astype(jnp.bfloat16)
    gate = jnp.dot(normed, proj_gate, preferred_element_type=jnp.float32).astype(jnp.bfloat16)
    inner = jnp.dot(normed, proj_inner, preferred_element_type=jnp.float32).astype(jnp.bfloat16)
    ssm_rows = jnp.dot(normed, proj_ssm, preferred_element_type=jnp.float32).astype(jnp.bfloat16)
    step_raw = jnp.dot(normed, proj_step, preferred_element_type=jnp.float32).astype(jnp.bfloat16)
    conv_x, full_inner = causal_conv(edge_inner, inner.reshape(REQUESTS, DRAFT, DINNER), conv_inner, conv_inner_bias)
    conv_s, full_ssm = causal_conv(edge_ssm, ssm_rows.reshape(REQUESTS, DRAFT, 2 * NSTATE), conv_ssm, conv_ssm_bias)
    live = (jnp.arange(DRAFT, dtype=jnp.int32)[None, :] < draft_lengths[:, None]).astype(jnp.float32)
    step_size = jax.nn.softplus(step_raw.astype(jnp.float32).reshape(REQUESTS, DRAFT, HEADS) + step_bias) * live[:, :, None]
    rates = -jnp.exp(decay_log)

    def one_block(block):
        start_state, inner_block, ssm_block, step_block, accepted_block = block
        state = start_state.astype(jnp.float32)
        kept = jnp.where((accepted_block == 0)[:, None, None, None], state, jnp.zeros_like(state))
        outputs = []
        for position in range(DRAFT):
            state, kept, output = advance(state, kept, step_block[:, position], inner_block[:, position].astype(jnp.float32), ssm_block[:, position, :NSTATE].astype(jnp.float32), ssm_block[:, position, NSTATE:].astype(jnp.float32), rates, skip_gain, accepted_block, position)
            outputs.append(output)
        return (jnp.stack(outputs, axis=1).astype(jnp.bfloat16), kept.astype(jnp.bfloat16))
    blocks = (states_in.reshape(N_REQ, REQ_DEV, HEADS, HEAD_DIM, NSTATE), conv_x.reshape(N_REQ, REQ_DEV, DRAFT, HEADS, HEAD_DIM), conv_s.reshape(N_REQ, REQ_DEV, DRAFT, 2 * NSTATE), step_size.reshape(N_REQ, REQ_DEV, DRAFT, HEADS), accepted.reshape(N_REQ, REQ_DEV))
    ssm_out, kept = lax.map(one_block, blocks)
    ssm_out = ssm_out.reshape(TOKENS, DINNER)
    kept = kept.reshape(REQUESTS, HEADS, HEAD_DIM, NSTATE)
    gated = ssm_out.astype(jnp.float32) * jax.nn.silu(gate.astype(jnp.float32))
    gated_norm = (gated * lax.rsqrt(lax.optimization_barrier(jnp.mean(gated * gated, axis=-1, keepdims=True)) + epsilon) * gate_gain).astype(jnp.bfloat16)
    mixed = jnp.dot(gated_norm, proj_out, preferred_element_type=jnp.float32)
    hidden_out = (wide + mixed).astype(jnp.bfloat16)
    kept_state = jnp.zeros_like(kept).at[destination].set(kept)
    kept_edge_inner = jnp.zeros_like(edge_inner).at[destination].set(edge_rows(full_inner, accepted))
    kept_edge_ssm = jnp.zeros_like(edge_ssm).at[destination].set(edge_rows(full_ssm, accepted))
    return (hidden_out, kept_state, kept_edge_inner, kept_edge_ssm)
```

```python
import functools

import jax
import jax.numpy as jnp
from jax import lax
from jax.experimental import pallas as pl
from jax.experimental.pallas import tpu as pltpu
from jax.sharding import PartitionSpec as P

HEAD_DIM = 64
NSTATE = 128
KCONV = 4
DRAFT = 8
WINDOW = 8
DINNER = 3072
TILE = 256
EXTRA = 2 * NSTATE

epsilon = 1e-05
HIGH = lax.Precision.HIGHEST
F32 = jnp.float32
BF16 = jnp.bfloat16


def iota(shape, axis):
    return lax.broadcasted_iota(jnp.int32, shape, axis)


def mm(a, b, precision=None):
    return jnp.dot(a, b, preferred_element_type=F32, precision=precision)


def mm_t(a, b):
    return lax.dot_general(a, b, (((1,), (1,)), ((), ())), preferred_element_type=F32)


def silu(x):
    return x * (1.0 / (1.0 + jnp.exp(-x)))


def conv_rows(rows, edges, taps, bias):
    slot = iota(rows.shape, 1)
    total = bias + taps[KCONV - 1 : KCONV] * rows
    for back in range(1, KCONV):
        mixed = jnp.where(slot >= DRAFT - back, edges, rows)
        total = total + taps[KCONV - 1 - back : KCONV - back] * pltpu.roll(mixed, back, 1)
    return total


def front_kernel(
    count,
    heads,
    ints,
    hidden,
    norm_gain,
    w_gate,
    w_inner,
    w_out,
    w_ssm,
    w_step,
    head_rows,
    taps_inner,
    bias_inner,
    taps_ssm,
    bias_ssm,
    gate_gain,
    states,
    edge_inner,
    edge_ssm,
    mine,
    theirs,
    *rest,
):
    corr = rest[:WINDOW]
    normed, acc, squares, quant, gmat, cmat, select, boxes = rest[WINDOW:]
    step = pl.program_id(0)
    last = pl.num_programs(0) - 1
    rows = count * DRAFT
    width = acc.shape[1]
    half = width // 2

    @pl.when(step == 0)
    def _():
        wide = jnp.concatenate([hidden[0], hidden[1]], axis=1).astype(F32)
        scale = lax.rsqrt(jnp.mean(wide * wide, axis=-1, keepdims=True) + epsilon)
        norm = (wide * scale * norm_gain[...]).astype(BF16)
        normed[...] = norm
        acc[...] = jnp.zeros_like(acc)
        squares[...] = jnp.zeros_like(squares)
        boxes[...] = jnp.zeros_like(boxes)
        for k in range(WINDOW):
            corr[k][...] = jnp.zeros_like(corr[k])
        row = iota((rows, rows), 0)
        col = iota((rows, rows), 1)
        request = row >> 3
        taken = jnp.zeros((rows, rows), jnp.int32)
        for r in range(count):
            taken = jnp.where(request == r, ints[1, r], taken)
        same = request == (col >> 3)
        lower = same & ((col & 7) <= (row & 7))
        before = same & ((col & 7) < taken)
        raw = mm(norm, w_step[...]).astype(BF16).astype(F32) + head_rows[0:1]
        lengths = jnp.zeros((rows, heads), jnp.int32)
        chosen = jnp.zeros((rows, heads), jnp.int32)
        hrow = iota((rows, heads), 0)
        for r in range(count):
            lengths = jnp.where((hrow >> 3) == r, ints[0, r], lengths)
            chosen = jnp.where((hrow >> 3) == r, ints[1, r], chosen)
        soft = jnp.maximum(raw, 0.0) + jnp.log1p(jnp.exp(-jnp.abs(raw)))
        size = jnp.where((hrow & 7) < lengths, soft, 0.0)
        rate = -jnp.exp(head_rows[1:2])
        cum = mm(lower.astype(F32), size, HIGH)
        upto = mm(before.astype(F32), size, HIGH)
        weight = jnp.where(
            (hrow & 7) < chosen, jnp.exp(jnp.minimum(rate * (upto - cum), 0.0)) * size, 0.0
        )
        stacked = jnp.concatenate(
            [
                rate * cum,
                size,
                weight,
                jnp.exp(rate * upto),
                jnp.broadcast_to(head_rows[2:3], (16, heads)),
            ],
            axis=0,
        )
        for part in range(3):
            piece = stacked.astype(BF16)
            quant[part] = piece
            stacked = stacked - piece.astype(F32)
        sel_rows = jnp.where(
            same & ((row & 7) < KCONV - 1),
            ((col & 7) == (row & 7) + taken - 3).astype(F32),
            0.0,
        ).astype(BF16)
        sel_edge = jnp.where(
            same & ((row & 7) < KCONV - 1),
            ((col & 7) == (row & 7) + taken + 5).astype(F32),
            0.0,
        ).astype(BF16)
        select[0] = sel_rows
        select[1] = sel_edge
        ssm = jnp.concatenate([mm(norm, w_ssm[0]), mm(norm, w_ssm[1])], axis=1).astype(BF16)
        before_ssm = edge_ssm[...].astype(F32)
        conv = conv_rows(
            ssm.astype(F32).reshape(count, DRAFT, 2 * NSTATE),
            before_ssm,
            taps_ssm[...].astype(F32),
            bias_ssm[...],
        )
        both = silu(conv).reshape(rows, 2 * NSTATE).astype(BF16)
        bmat = both[:, :NSTATE]
        cvec = both[:, NSTATE:]
        cmat[...] = cvec.astype(F32)
        pair = jnp.where(lower, mm_t(cvec, bmat), 0.0)
        fold = ((iota((rows, NSTATE), 0) & 7) == iota((rows, NSTATE), 1)).astype(F32)
        gmat[...] = mm(pair, fold, HIGH)
        kept = mm(sel_rows, ssm) + mm(
            sel_edge, before_ssm.reshape(rows, 2 * NSTATE).astype(BF16)
        )
        wide_b = bmat.astype(F32)
        place = iota((DRAFT, NSTATE), 0)
        for r in range(count):
            own = kept[r * DRAFT : (r + 1) * DRAFT]
            slot = jnp.full((DRAFT, NSTATE), (ints[3, r] + 1).astype(F32))
            packed = jnp.where(
                place < 3,
                own[:, :NSTATE],
                jnp.where(place < 6, pltpu.roll(own[:, NSTATE:], 3, 0), slot),
            )
            top = jnp.concatenate([wide_b[r * DRAFT : (r + 1) * DRAFT], packed], axis=1)
            low = jnp.concatenate([jnp.zeros((DRAFT, NSTATE), F32), slot], axis=1)
            boxes[ints[2, r]] = jnp.concatenate([top, low], axis=0).astype(BF16)
        for k in range(WINDOW):
            corr[k][:, width : width + EXTRA] = boxes[k]

    norm = normed[...]
    inner = mm(norm, w_inner[...]).astype(BF16)
    gate = mm(norm, w_gate[...]).astype(BF16).astype(F32)
    edges = edge_inner[...].astype(F32)
    conv = conv_rows(
        inner.astype(F32).reshape(count, DRAFT, TILE),
        edges,
        taps_inner[...].astype(F32),
        bias_inner[...],
    )
    x = silu(conv).reshape(rows, TILE).astype(BF16).astype(F32)
    first_head = step * (TILE // HEAD_DIM)
    spread = (
        iota((heads, TILE), 0) == first_head + (iota((heads, TILE), 1) >> 6)
    ).astype(BF16)
    expanded = mm(quant[0], spread) + mm(quant[1], spread) + mm(quant[2], spread)
    level = expanded[:rows]
    weighted = expanded[rows : 2 * rows] * x
    past = jnp.concatenate(
        [
            mm_t(cmat[r * DRAFT : (r + 1) * DRAFT].astype(BF16), states[r])
            for r in range(count)
        ],
        axis=0,
    )
    out = jnp.exp(level) * past + expanded[4 * rows : 4 * rows + 1] * x
    level3 = level.reshape(count, DRAFT, TILE)
    weighted3 = weighted.reshape(count, DRAFT, TILE)
    total = jnp.zeros((count, DRAFT, TILE), F32)
    for u in range(DRAFT):
        factor = jnp.exp(jnp.minimum(level3 - level3[:, u : u + 1], 0.0))
        share = gmat[:, u : u + 1].reshape(count, DRAFT, 1)
        total = total + share * factor * weighted3[:, u : u + 1]
    out = (out + total.reshape(rows, TILE)).astype(BF16).astype(F32)
    gated = out * silu(gate)
    squared = gated * gated
    squares[...] += squared[:, :128] + squared[:, 128:]
    acc[...] += mm((gated * gate_gain[...]).astype(BF16), w_out[...])
    delta = expanded[2 * rows : 3 * rows] * x
    decay = expanded[3 * rows : 4 * rows]
    decay_hi = decay.astype(BF16).astype(F32)
    second = mm(select[0], inner) + mm(select[1], edges.reshape(rows, TILE).astype(BF16))
    place = iota((rows, TILE), 0) & 7
    second = jnp.where(
        place == 3, decay_hi, jnp.where(place == 4, decay - decay_hi, second)
    )
    for r in range(count):
        span = slice(r * DRAFT, (r + 1) * DRAFT)
        boxes[ints[2, r]] = jnp.concatenate([delta[span], second[span]], axis=0).astype(BF16)
    here = pl.ds(pl.multiple_of(step * TILE, TILE), TILE)
    for k in range(WINDOW):
        corr[k][:, here] = boxes[k]

    @pl.when(step == last)
    def _():
        total_square = jnp.broadcast_to(
            jnp.sum(squares[...], axis=1, keepdims=True), squares.shape
        )
        mine[:, half:] = total_square
        theirs[:, half:] = total_square

        @pl.when(ints[4, 0] == 0)
        def _():
            mine[:, :half] = acc[:, :half]
            theirs[:, :half] = acc[:, half:]

        @pl.when(ints[4, 0] != 0)
        def _():
            mine[:, :half] = acc[:, half:]
            theirs[:, :half] = acc[:, :half]


def front(count, heads, width, depth, args):
    rows = count * DRAFT
    tiles = width // TILE

    def whole(shape):
        return pl.BlockSpec(shape, lambda j: (0,) * len(shape))

    in_specs = [
        pl.BlockSpec(memory_space=pltpu.SMEM),
        whole((2, rows, depth // 2)),
        whole((1, depth)),
        pl.BlockSpec((depth, TILE), lambda j: (0, j)),
        pl.BlockSpec((depth, TILE), lambda j: (0, j)),
        pl.BlockSpec((TILE, depth), lambda j: (j, 0)),
        whole((2, depth, NSTATE)),
        whole((depth, heads)),
        whole((3, heads)),
        pl.BlockSpec((KCONV, TILE), lambda j: (0, j)),
        pl.BlockSpec((1, TILE), lambda j: (0, j)),
        whole((KCONV, 2 * NSTATE)),
        whole((1, 2 * NSTATE)),
        pl.BlockSpec((1, TILE), lambda j: (0, j)),
        pl.BlockSpec((count, TILE, NSTATE), lambda j: (0, j, 0)),
        pl.BlockSpec((count, DRAFT, TILE), lambda j: (0, 0, j)),
        whole((count, DRAFT, 2 * NSTATE)),
    ]
    out_width = depth // 2 + 128
    out_shape = [jax.ShapeDtypeStruct((rows, out_width), F32)] * 2 + [
        jax.ShapeDtypeStruct((2 * DRAFT, width + EXTRA), BF16)
    ] * WINDOW
    out_specs = [whole((rows, out_width))] * 2 + [whole((2 * DRAFT, width + EXTRA))] * WINDOW
    return pl.pallas_call(
        functools.partial(front_kernel, count, heads),
        grid=(tiles,),
        in_specs=in_specs,
        out_specs=out_specs,
        out_shape=out_shape,
        scratch_shapes=[
            pltpu.VMEM((rows, depth), BF16),
            pltpu.VMEM((rows, depth), F32),
            pltpu.VMEM((rows, 128), F32),
            pltpu.VMEM((3, 4 * rows + 16, heads), BF16),
            pltpu.VMEM((rows, NSTATE), F32),
            pltpu.VMEM((rows, NSTATE), F32),
            pltpu.VMEM((2, rows, rows), BF16),
            pltpu.VMEM((WINDOW, 2 * DRAFT, TILE), BF16),
        ],
        compiler_params=pltpu.CompilerParams(
            dimension_semantics=("arbitrary",), vmem_limit_bytes=40 * 1024 * 1024
        ),
        cost_estimate=pl.CostEstimate(
            flops=2 * rows * depth * width * 3,
            bytes_accessed=3 * depth * width * 2 + count * width * NSTATE * 2,
            transcendentals=rows * width * 12,
        ),
        name="front",
    )(*args)


def merge_kernel(offsets, local_first, *refs):
    n = len(offsets)
    ints = refs[0]
    sources = refs[1 : 1 + n]
    corr = refs[1 + n : 1 + 2 * n]
    kept, out_inner, out_ssm = refs[1 + 2 * n : 4 + 2 * n]
    loaded, merged, sem_in, sem_out = refs[4 + 2 * n :]
    width = loaded.shape[1]

    def source(i):
        if local_first and i == 0:
            return sources[0].at[ints[0]]
        return sources[i].at[0]

    def fetch(i):
        return pltpu.make_async_copy(source(i), loaded.at[i], sem_in.at[i])

    for i in range(n):
        fetch(i).start()
    slots = []
    for i in range(n):
        mark = corr[i][:, width + NSTATE : width + 2 * NSTATE].astype(F32)
        slot = jnp.max(mark[DRAFT:]).astype(jnp.int32) - 1
        slots.append(slot)
        fetch(i).wait()

        @pl.when(slot >= 0)
        def _(i=i, slot=slot, mark=mark):
            ones = jnp.where(
                (iota((2 * DRAFT, NSTATE), 0) == 11) | (iota((2 * DRAFT, NSTATE), 0) == 12),
                1.0,
                0.0,
            ).astype(BF16)
            right = jnp.concatenate([corr[i][:, width : width + NSTATE], ones], axis=1)

            @pl.loop(0, width // TILE)
            def _(c):
                span = pl.ds(pl.multiple_of(c * TILE, TILE), TILE)
                both = lax.dot_general(
                    corr[i][:, span],
                    right,
                    (((0,), (0,)), ((), ())),
                    preferred_element_type=F32,
                )
                state = loaded[i, span].astype(F32)
                merged[i, span] = (both[:, NSTATE:] * state + both[:, :NSTATE]).astype(BF16)

            pltpu.make_async_copy(merged.at[i], kept.at[slot], sem_out.at[i]).start()
            rows = corr[i][:, :width].astype(F32)[DRAFT : DRAFT + 3]
            out_inner[slot] = rows.astype(BF16)
            high = pltpu.roll(mark[:DRAFT], DRAFT - 3, 0)
            out_ssm[slot] = jnp.concatenate([mark[:3], high[:3]], axis=1).astype(BF16)

    for i in range(n):

        @pl.when(slots[i] >= 0)
        def _(i=i):
            pltpu.make_async_copy(merged.at[i], kept.at[slots[i]], sem_out.at[i]).wait()


def merge(count, width, first, sources, corr):
    n = len(sources)
    hbm = pl.BlockSpec(memory_space=pl.ANY)
    vmem = pl.BlockSpec(memory_space=pltpu.VMEM)
    return pl.pallas_call(
        functools.partial(merge_kernel, tuple(range(n)), True),
        in_specs=[pl.BlockSpec(memory_space=pltpu.SMEM)] + [hbm] * n + [vmem] * n,
        out_specs=[hbm, vmem, vmem],
        out_shape=[
            jax.ShapeDtypeStruct((count, width, NSTATE), BF16),
            jax.ShapeDtypeStruct((count, KCONV - 1, width), BF16),
            jax.ShapeDtypeStruct((count, KCONV - 1, 2 * NSTATE), BF16),
        ],
        scratch_shapes=[
            pltpu.VMEM((n, width, NSTATE), BF16),
            pltpu.VMEM((n, width, NSTATE), BF16),
            pltpu.SemaphoreType.DMA((n,)),
            pltpu.SemaphoreType.DMA((n,)),
        ],
        compiler_params=pltpu.CompilerParams(vmem_limit_bytes=40 * 1024 * 1024),
        cost_estimate=pl.CostEstimate(
            flops=2 * n * width * 16 * 256,
            bytes_accessed=2 * n * width * NSTATE * 2,
            transcendentals=0,
        ),
        name="merge",
    )(first, *sources, *corr)


def passed_along(array, axis, by):
    length = lax.axis_size(axis)
    return lax.ppermute(array, axis, [(i, (i + by) % length) for i in range(length)])


def local(
    hidden_in,
    norm_gain,
    proj_gate,
    proj_inner,
    proj_ssm,
    proj_step,
    step_bias,
    decay_log,
    skip_gain,
    conv_inner,
    conv_inner_bias,
    conv_ssm,
    conv_ssm_bias,
    gate_gain,
    proj_out,
    states_in,
    edge_inner,
    edge_ssm,
    draft_lengths,
    accepted,
    destination,
):
    count, heads = states_in.shape[:2]
    depth, width = proj_inner.shape
    peers = lax.axis_size("req")
    here = lax.axis_index("req")
    side = lax.axis_index("head")
    reach = (destination // count - here) % peers
    slot = destination % count
    match = reach[None, :] == jnp.arange(WINDOW, dtype=jnp.int32)[:, None]
    index = jnp.sum(jnp.where(match, jnp.arange(count, dtype=jnp.int32)[None, :], 0), axis=1)
    flat = states_in.reshape(count, width, NSTATE)
    sources = [flat]
    for k in range(1, WINDOW):
        picked = lax.dynamic_slice_in_dim(flat, index[k], 1, 0)
        sources.append(passed_along(picked, "req", k))

    hidden = lax.all_gather(hidden_in, "head", axis=0, tiled=False)
    w_ssm = lax.all_gather(proj_ssm, "head", axis=0, tiled=False)
    ints = jnp.stack(
        [draft_lengths, accepted, reach, slot, jnp.broadcast_to(side, (count,))]
    ).astype(jnp.int32)
    pad = ((0, 0), (DRAFT - KCONV + 1, 0), (0, 0))
    results = front(
        count,
        heads,
        width,
        depth,
        (
            ints,
            hidden,
            norm_gain.reshape(1, depth),
            proj_gate,
            proj_inner,
            proj_out,
            w_ssm,
            proj_step,
            jnp.stack([step_bias, decay_log, skip_gain]),
            conv_inner,
            conv_inner_bias.reshape(1, width),
            conv_ssm,
            conv_ssm_bias.reshape(1, 2 * NSTATE),
            gate_gain.reshape(1, width),
            flat,
            jnp.pad(edge_inner, pad),
            jnp.pad(edge_ssm, pad),
        ),
    )
    mine, theirs = results[:2]
    corr = list(results[2:])
    other = passed_along(theirs, "head", 1)
    half = depth // 2
    total = mine + other
    scale = lax.rsqrt(total[:, half : half + 1] / DINNER + epsilon)
    hidden_out = (hidden_in.astype(F32) + total[:, :half] * scale).astype(BF16)
    for k in range(1, WINDOW):
        corr[k] = passed_along(corr[k], "req", k)
    kept, kept_inner, kept_ssm = merge(count, width, index[:1], sources, corr)
    return (hidden_out, kept.reshape(states_in.shape), kept_inner, kept_ssm)


def solution(mesh):
    in_specs = (
        P("req", "head"),
        P(),
        P(None, "head"),
        P(None, "head"),
        P(None, "head"),
        P(None, "head"),
        P("head"),
        P("head"),
        P("head"),
        P(None, "head"),
        P("head"),
        P(),
        P(),
        P("head"),
        P("head", None),
        P("req", "head", None, None),
        P("req", None, "head"),
        P("req", None, None),
        P("req"),
        P("req"),
        P("req"),
    )
    out_specs = (
        P("req", "head"),
        P("req", "head", None, None),
        P("req", None, "head"),
        P("req", None, None),
    )
    return jax.shard_map(local, mesh=mesh, in_specs=in_specs, out_specs=out_specs, check_vma=False)
```

```python
import functools

import jax
import jax.numpy as jnp
from jax import lax
from jax.experimental import pallas as pl
from jax.experimental.pallas import tpu as pltpu
from jax.sharding import PartitionSpec as P

HEAD_DIM = 64
NSTATE = 128
KCONV = 4
DRAFT = 8
WINDOW = 8
DINNER = 3072
TILE = 256
EXTRA = 2 * NSTATE

epsilon = 1e-05
HIGH = lax.Precision.HIGHEST
F32 = jnp.float32
BF16 = jnp.bfloat16


def iota(shape, axis):
    return lax.broadcasted_iota(jnp.int32, shape, axis)


def mm(a, b, precision=None):
    return jnp.dot(a, b, preferred_element_type=F32, precision=precision)


def mm_t(a, b):
    return lax.dot_general(a, b, (((1,), (1,)), ((), ())), preferred_element_type=F32)


def silu(x):
    return x * (1.0 / (1.0 + jnp.exp(-x)))


def conv_rows(rows, edges, taps, bias):
    slot = iota(rows.shape, 1)
    total = bias + taps[KCONV - 1 : KCONV] * rows
    for back in range(1, KCONV):
        mixed = jnp.where(slot >= DRAFT - back, edges, rows)
        total = total + taps[KCONV - 1 - back : KCONV - back] * pltpu.roll(mixed, back, 1)
    return total


def front_kernel(
    count,
    heads,
    table,
    lengths_in,
    accepted_in,
    hidden,
    norm_gain,
    w_gate,
    w_inner,
    w_out,
    w_ssm,
    w_step,
    head_rows,
    taps_inner,
    bias_inner,
    taps_ssm,
    bias_ssm,
    gate_gain,
    states,
    edge_inner,
    edge_ssm,
    mine,
    theirs,
    *rest,
):
    corr = rest[:count]
    normed, acc, squares, quant, gmat, cmat, select, boxes = rest[count:]
    step = pl.program_id(0)
    last = pl.num_programs(0) - 1
    rows = count * DRAFT
    width = acc.shape[1]
    half = width // 2

    @pl.when(step == 0)
    def _():
        wide = jnp.concatenate([hidden[0], hidden[1]], axis=1).astype(F32)
        scale = lax.rsqrt(jnp.mean(wide * wide, axis=-1, keepdims=True) + epsilon)
        norm = (wide * scale * norm_gain[...]).astype(BF16)
        normed[...] = norm
        acc[...] = jnp.zeros_like(acc)
        squares[...] = jnp.zeros_like(squares)
        row = iota((rows, rows), 0)
        col = iota((rows, rows), 1)
        request = row >> 3
        taken = jnp.zeros((rows, rows), jnp.int32)
        for r in range(count):
            taken = jnp.where(request == r, accepted_in[r], taken)
        same = request == (col >> 3)
        lower = same & ((col & 7) <= (row & 7))
        before = same & ((col & 7) < taken)
        raw = mm(norm, w_step[...]).astype(BF16).astype(F32) + head_rows[0:1]
        lengths = jnp.zeros((rows, heads), jnp.int32)
        chosen = jnp.zeros((rows, heads), jnp.int32)
        hrow = iota((rows, heads), 0)
        for r in range(count):
            lengths = jnp.where((hrow >> 3) == r, lengths_in[r], lengths)
            chosen = jnp.where((hrow >> 3) == r, accepted_in[r], chosen)
        soft = jnp.maximum(raw, 0.0) + jnp.log1p(jnp.exp(-jnp.abs(raw)))
        size = jnp.where((hrow & 7) < lengths, soft, 0.0)
        rate = -jnp.exp(head_rows[1:2])
        cum = mm(lower.astype(F32), size, HIGH)
        upto = mm(before.astype(F32), size, HIGH)
        weight = jnp.where(
            (hrow & 7) < chosen, jnp.exp(jnp.minimum(rate * (upto - cum), 0.0)) * size, 0.0
        )
        stacked = jnp.concatenate(
            [
                rate * cum,
                size,
                weight,
                jnp.exp(rate * upto),
                jnp.broadcast_to(head_rows[2:3], (16, heads)),
            ],
            axis=0,
        )
        for part in range(3):
            piece = stacked.astype(BF16)
            quant[part] = piece
            stacked = stacked - piece.astype(F32)
        sel_rows = jnp.where(
            same & ((row & 7) < KCONV - 1),
            ((col & 7) == (row & 7) + taken - 3).astype(F32),
            0.0,
        ).astype(BF16)
        sel_edge = jnp.where(
            same & ((row & 7) < KCONV - 1),
            ((col & 7) == (row & 7) + taken + 5).astype(F32),
            0.0,
        ).astype(BF16)
        select[0] = sel_rows
        select[1] = sel_edge
        ssm = jnp.concatenate([mm(norm, w_ssm[0]), mm(norm, w_ssm[1])], axis=1).astype(BF16)
        before_ssm = edge_ssm[...].astype(F32)
        conv = conv_rows(
            ssm.astype(F32).reshape(count, DRAFT, 2 * NSTATE),
            before_ssm,
            taps_ssm[...].astype(F32),
            bias_ssm[...],
        )
        both = silu(conv).reshape(rows, 2 * NSTATE).astype(BF16)
        bmat = both[:, :NSTATE]
        cvec = both[:, NSTATE:]
        cmat[...] = cvec.astype(F32)
        pair = jnp.where(lower, mm_t(cvec, bmat), 0.0)
        fold = ((iota((rows, NSTATE), 0) & 7) == iota((rows, NSTATE), 1)).astype(F32)
        gmat[...] = mm(pair, fold, HIGH)
        kept = mm(sel_rows, ssm) + mm(
            sel_edge, before_ssm.reshape(rows, 2 * NSTATE).astype(BF16)
        )
        wide_b = bmat.astype(F32)
        place = iota((DRAFT, NSTATE), 0)
        for r in range(count):
            own = kept[r * DRAFT : (r + 1) * DRAFT]
            slot = jnp.full((DRAFT, NSTATE), (table[1, r] + 1).astype(F32))
            packed = jnp.where(
                place < 3,
                own[:, :NSTATE],
                jnp.where(place < 6, pltpu.roll(own[:, NSTATE:], 3, 0), slot),
            )
            top = jnp.concatenate([wide_b[r * DRAFT : (r + 1) * DRAFT], packed], axis=1)
            low = jnp.concatenate([jnp.zeros((DRAFT, NSTATE), F32), slot], axis=1)
            boxes[table[0, r]] = jnp.concatenate([top, low], axis=0).astype(BF16)
        for k in range(count):
            corr[k][:, width : width + EXTRA] = boxes[k]

    norm = normed[...]
    inner = mm(norm, w_inner[...]).astype(BF16)
    gate = mm(norm, w_gate[...]).astype(BF16).astype(F32)
    edges = edge_inner[...].astype(F32)
    conv = conv_rows(
        inner.astype(F32).reshape(count, DRAFT, TILE),
        edges,
        taps_inner[...].astype(F32),
        bias_inner[...],
    )
    x = silu(conv).reshape(rows, TILE).astype(BF16).astype(F32)
    first_head = step * (TILE // HEAD_DIM)
    spread = (
        iota((heads, TILE), 0) == first_head + (iota((heads, TILE), 1) >> 6)
    ).astype(BF16)
    expanded = mm(quant[0], spread) + mm(quant[1], spread) + mm(quant[2], spread)
    level = expanded[:rows]
    weighted = expanded[rows : 2 * rows] * x
    past = jnp.concatenate(
        [
            mm_t(cmat[r * DRAFT : (r + 1) * DRAFT].astype(BF16), states[r])
            for r in range(count)
        ],
        axis=0,
    )
    out = jnp.exp(level) * past + expanded[4 * rows : 4 * rows + 1] * x
    level3 = level.reshape(count, DRAFT, TILE)
    weighted3 = weighted.reshape(count, DRAFT, TILE)
    total = jnp.zeros((count, DRAFT, TILE), F32)
    for u in range(DRAFT):
        factor = jnp.exp(jnp.minimum(level3 - level3[:, u : u + 1], 0.0))
        share = gmat[:, u : u + 1].reshape(count, DRAFT, 1)
        total = total + share * factor * weighted3[:, u : u + 1]
    out = (out + total.reshape(rows, TILE)).astype(BF16).astype(F32)
    gated = out * silu(gate)
    squared = gated * gated
    squares[...] += squared[:, :128] + squared[:, 128:]
    acc[...] += mm((gated * gate_gain[...]).astype(BF16), w_out[...])
    delta = expanded[2 * rows : 3 * rows] * x
    decay = expanded[3 * rows : 4 * rows]
    decay_hi = decay.astype(BF16).astype(F32)
    second = mm(select[0], inner) + mm(select[1], edges.reshape(rows, TILE).astype(BF16))
    place = iota((rows, TILE), 0) & 7
    second = jnp.where(
        place == 3, decay_hi, jnp.where(place == 4, decay - decay_hi, second)
    )
    for r in range(count):
        span = slice(r * DRAFT, (r + 1) * DRAFT)
        boxes[table[0, r]] = jnp.concatenate([delta[span], second[span]], axis=0).astype(BF16)
    here = pl.ds(pl.multiple_of(step * TILE, TILE), TILE)
    for k in range(count):
        corr[k][:, here] = boxes[k]

    @pl.when(step == last)
    def _():
        total_square = jnp.broadcast_to(
            jnp.sum(squares[...], axis=1, keepdims=True), squares.shape
        )
        mine[:, half:] = total_square
        theirs[:, half:] = total_square

        @pl.when(table[2, 0] == 0)
        def _():
            mine[:, :half] = acc[:, :half]
            theirs[:, :half] = acc[:, half:]

        @pl.when(table[2, 0] != 0)
        def _():
            mine[:, :half] = acc[:, half:]
            theirs[:, :half] = acc[:, :half]


def front(count, heads, width, depth, args):
    rows = count * DRAFT
    tiles = width // TILE

    def whole(shape):
        return pl.BlockSpec(shape, lambda j: (0,) * len(shape))

    in_specs = [
        *[pl.BlockSpec(memory_space=pltpu.SMEM)] * 3,
        whole((2, rows, depth // 2)),
        whole((1, depth)),
        pl.BlockSpec((depth, TILE), lambda j: (0, j)),
        pl.BlockSpec((depth, TILE), lambda j: (0, j)),
        pl.BlockSpec((TILE, depth), lambda j: (j, 0)),
        whole((2, depth, NSTATE)),
        whole((depth, heads)),
        whole((3, heads)),
        pl.BlockSpec((KCONV, TILE), lambda j: (0, j)),
        pl.BlockSpec((1, TILE), lambda j: (0, j)),
        whole((KCONV, 2 * NSTATE)),
        whole((1, 2 * NSTATE)),
        pl.BlockSpec((1, TILE), lambda j: (0, j)),
        pl.BlockSpec((count, TILE, NSTATE), lambda j: (0, j, 0)),
        pl.BlockSpec((count, DRAFT, TILE), lambda j: (0, 0, j)),
        whole((count, DRAFT, 2 * NSTATE)),
    ]
    out_width = depth // 2 + 128
    out_shape = [jax.ShapeDtypeStruct((rows, out_width), F32)] * 2 + [
        jax.ShapeDtypeStruct((2 * DRAFT, width + EXTRA), BF16)
    ] * count
    out_specs = [whole((rows, out_width))] * 2 + [whole((2 * DRAFT, width + EXTRA))] * count
    return pl.pallas_call(
        functools.partial(front_kernel, count, heads),
        grid=(tiles,),
        in_specs=in_specs,
        out_specs=out_specs,
        out_shape=out_shape,
        scratch_shapes=[
            pltpu.VMEM((rows, depth), BF16),
            pltpu.VMEM((rows, depth), F32),
            pltpu.VMEM((rows, 128), F32),
            pltpu.VMEM((3, 4 * rows + 16, heads), BF16),
            pltpu.VMEM((rows, NSTATE), F32),
            pltpu.VMEM((rows, NSTATE), F32),
            pltpu.VMEM((2, rows, rows), BF16),
            pltpu.VMEM((count, 2 * DRAFT, TILE), BF16),
        ],
        compiler_params=pltpu.CompilerParams(dimension_semantics=("arbitrary",)),
        cost_estimate=pl.CostEstimate(
            flops=2 * rows * depth * width * 3,
            bytes_accessed=3 * depth * width * 2 + count * width * NSTATE * 2,
            transcendentals=rows * width * 12,
        ),
        name="front",
    )(*args)


def pick_kernel(count, peers, destination, states, *outs):
    picked = outs[:count]
    table, branch, sems = outs[count:]
    here = lax.axis_index("req")
    reach = [
        lax.rem(lax.div(destination[r], count) - here + peers, peers) for r in range(count)
    ]
    rank = []
    for r in range(count):
        below = [(reach[q] < reach[r]).astype(jnp.int32) for q in range(count) if q != r]
        rank.append(sum(below))
        table[0, r] = rank[r]
        table[1, r] = lax.rem(destination[r], count)
        table[2, r] = lax.axis_index("head")
    copies = []
    for j in range(count):
        source = sum((rank[r] == j).astype(jnp.int32) * r for r in range(count))
        copy = pltpu.make_async_copy(states.at[source], picked[j].at[0], sems.at[j])
        copy.start()
        copies.append(copy)
    low = jnp.int32(0)
    run = jnp.int32(1)
    for b in range(WINDOW):
        found = sum((reach[r] == b).astype(jnp.int32) for r in range(count))
        run = run * found
        low = low + run
    high = WINDOW * (WINDOW - 1) // 2 - sum(reach) - low
    branch[0] = lax.div(low * (2 * WINDOW - 1 - low), 2) + high - low - 1
    for copy in copies:
        copy.wait()


def pick(count, width, peers, destination, states):
    hbm = pl.BlockSpec(memory_space=pl.ANY)
    smem = pl.BlockSpec(memory_space=pltpu.SMEM)
    return pl.pallas_call(
        functools.partial(pick_kernel, count, peers),
        in_specs=[smem, hbm],
        out_specs=[hbm] * count + [smem] * 2,
        out_shape=[jax.ShapeDtypeStruct((1, width, NSTATE), BF16)] * count
        + [
            jax.ShapeDtypeStruct((3, count), jnp.int32),
            jax.ShapeDtypeStruct((1,), jnp.int32),
        ],
        scratch_shapes=[pltpu.SemaphoreType.DMA((count,))],
        name="pick",
    )(destination, states)


MERGE_PARTS = 3


def merge_kernel(count, final, *refs):
    source = refs[0]
    corr = refs[1]
    n = 2 + (count - 1 if final else 0)
    others = refs[2:n]
    refs = refs[n:]
    if len(refs) == (8 if final else 6):
        refs = refs[1:]
    kept = refs[0]
    loaded, merged, sem_in, sem_out = refs[-4:]
    width = loaded.shape[0]
    part = width // MERGE_PARTS

    def span(c):
        return slice(c * part, (c + 1) * part)

    def fetch(c):
        return pltpu.make_async_copy(source.at[0, span(c)], loaded.at[span(c)], sem_in.at[c])

    def mark_of(ref):
        mark = ref[:, width + NSTATE : width + 2 * NSTATE].astype(F32)
        return mark, jnp.max(mark[DRAFT:]).astype(jnp.int32) - 1

    for c in range(MERGE_PARTS):
        fetch(c).start()
    slot = mark_of(corr)[1]

    def put(c):
        return pltpu.make_async_copy(
            merged.at[span(c)], kept.at[slot, span(c)], sem_out.at[c]
        )

    line = iota((2 * DRAFT, NSTATE), 0)
    ones = jnp.where((line == 11) | (line == 12), 1.0, 0.0).astype(BF16)
    right = jnp.concatenate([corr[:, width : width + NSTATE], ones], axis=1)
    for c in range(MERGE_PARTS):
        both = lax.dot_general(
            corr[:, span(c)], right, (((0,), (0,)), ((), ())), preferred_element_type=F32
        )
        fetch(c).wait()
        state = loaded[span(c)].astype(F32)
        merged[span(c)] = (both[:, NSTATE:] * state + both[:, :NSTATE]).astype(BF16)
        put(c).start()
    if final:
        out_inner, out_ssm = refs[1:3]
        for ref in (corr, *others):
            mark, target = mark_of(ref)
            rows = ref[:, :width].astype(F32)[DRAFT : DRAFT + 3]
            out_inner[target] = rows.astype(BF16)
            high = pltpu.roll(mark[:DRAFT], DRAFT - 3, 0)
            out_ssm[target] = jnp.concatenate([mark[:3], high[:3]], axis=1).astype(BF16)
    for c in range(MERGE_PARTS):
        put(c).wait()


def merge(count, width, kept, source, corr, others=()):
    hbm = pl.BlockSpec(memory_space=pl.ANY)
    vmem = pl.BlockSpec(memory_space=pltpu.VMEM)
    final = len(others) > 0
    inputs = [source, corr, *others] + ([] if kept is None else [kept])
    out_shape = [jax.ShapeDtypeStruct((count, width, NSTATE), BF16)]
    if final:
        out_shape += [
            jax.ShapeDtypeStruct((count, KCONV - 1, width), BF16),
            jax.ShapeDtypeStruct((count, KCONV - 1, 2 * NSTATE), BF16),
        ]
    return pl.pallas_call(
        functools.partial(merge_kernel, count, final),
        in_specs=[hbm]
        + [vmem] * (1 + len(others))
        + ([] if kept is None else [hbm]),
        out_specs=[hbm] + [vmem] * (len(out_shape) - 1),
        out_shape=out_shape,
        input_output_aliases={} if kept is None else {len(inputs) - 1: 0},
        scratch_shapes=[
            pltpu.VMEM((width, NSTATE), BF16),
            pltpu.VMEM((width, NSTATE), BF16),
            pltpu.SemaphoreType.DMA((MERGE_PARTS,)),
            pltpu.SemaphoreType.DMA((MERGE_PARTS,)),
        ],
        cost_estimate=pl.CostEstimate(
            flops=2 * width * 16 * 256,
            bytes_accessed=2 * width * NSTATE * 2,
            transcendentals=0,
        ),
        name="merge",
    )(*inputs)


def passed_along(array, axis, by):
    length = lax.axis_size(axis)
    return lax.ppermute(array, axis, [(i, (i + by) % length) for i in range(length)])


def local(
    hidden_in,
    norm_gain,
    proj_gate,
    proj_inner,
    proj_ssm,
    proj_step,
    step_bias,
    decay_log,
    skip_gain,
    conv_inner,
    conv_inner_bias,
    conv_ssm,
    conv_ssm_bias,
    gate_gain,
    proj_out,
    states_in,
    edge_inner,
    edge_ssm,
    draft_lengths,
    accepted,
    destination,
):
    count, heads = states_in.shape[:2]
    depth, width = proj_inner.shape
    peers = lax.axis_size("req")
    flat = states_in.reshape(count, width, NSTATE)
    results = pick(count, width, peers, destination, flat)
    picked = list(results[:count])
    table, branch = results[count:]
    half = depth // 2
    given = (
        norm_gain,
        proj_gate,
        proj_inner,
        proj_out,
        proj_step,
        step_bias,
        decay_log,
        skip_gain,
        conv_inner,
        conv_inner_bias,
        conv_ssm,
        conv_ssm_bias,
        gate_gain,
        flat,
        edge_inner,
        edge_ssm,
        draft_lengths,
        accepted,
    )

    def layer(table, hidden_in, proj_ssm, given):
        (
            norm_gain,
            proj_gate,
            proj_inner,
            proj_out,
            proj_step,
            step_bias,
            decay_log,
            skip_gain,
            conv_inner,
            conv_inner_bias,
            conv_ssm,
            conv_ssm_bias,
            gate_gain,
            flat,
            edge_inner,
            edge_ssm,
            draft_lengths,
            accepted,
        ) = given
        pad = ((0, 0), (DRAFT - KCONV + 1, 0), (0, 0))
        return front(
            count,
            heads,
            width,
            depth,
            (
                table,
                draft_lengths,
                accepted,
                lax.all_gather(hidden_in, "head", axis=0, tiled=False),
                norm_gain.reshape(1, depth),
                proj_gate,
                proj_inner,
                proj_out,
                lax.all_gather(proj_ssm, "head", axis=0, tiled=False),
                proj_step,
                jnp.stack([step_bias, decay_log, skip_gain]),
                conv_inner,
                conv_inner_bias.reshape(1, width),
                conv_ssm,
                conv_ssm_bias.reshape(1, 2 * NSTATE),
                gate_gain.reshape(1, width),
                flat,
                jnp.pad(edge_inner, pad),
                jnp.pad(edge_ssm, pad),
            ),
        )

    def run(offsets, operands):
        table, picked, hidden_in, proj_ssm, given = operands
        results = layer(table, hidden_in, proj_ssm, given)
        mine, theirs = results[:2]
        corr = list(results[2:])
        arrived = list(picked)
        for j, k in enumerate(offsets):
            if k > 0:
                state = picked[j]
                if j == 0:
                    state, corr[j] = lax.optimization_barrier((state, corr[j]))
                arrived[j] = passed_along(state, "req", k)
        pair = lax.all_gather(theirs, "head", axis=0, tiled=False)
        other = jnp.where(lax.axis_index("head") == 0, pair[1], pair[0])
        total = mine + other
        scale = lax.rsqrt(total[:, half : half + 1] / DINNER + epsilon)
        hidden_out = (hidden_in.astype(F32) + total[:, :half] * scale).astype(BF16)
        for j, k in enumerate(offsets):
            if k > 0:
                arrived[j], corr[j] = lax.optimization_barrier((arrived[j], corr[j]))
                corr[j] = passed_along(corr[j], "req", k)
        kept = None
        for j in range(count - 1):
            (kept,) = merge(count, width, kept, arrived[j], corr[j])
        kept, kept_inner, kept_ssm = merge(
            count, width, kept, arrived[-1], corr[-1], tuple(corr[:-1])
        )
        return hidden_out, kept, kept_inner, kept_ssm

    sets = [
        tuple(k for k in range(WINDOW) if k not in (low, high))
        for low in range(WINDOW)
        for high in range(low + 1, WINDOW)
    ]
    hidden_out, kept, kept_inner, kept_ssm = lax.switch(
        branch[0],
        [functools.partial(run, offsets) for offsets in sets],
        (table, picked, hidden_in, proj_ssm, given),
    )
    return (hidden_out, kept.reshape(states_in.shape), kept_inner, kept_ssm)


def solution(mesh):
    in_specs = (
        P("req", "head"),
        P(),
        P(None, "head"),
        P(None, "head"),
        P(None, "head"),
        P(None, "head"),
        P("head"),
        P("head"),
        P("head"),
        P(None, "head"),
        P("head"),
        P(),
        P(),
        P("head"),
        P("head", None),
        P("req", "head", None, None),
        P("req", None, "head"),
        P("req", None, None),
        P("req"),
        P("req"),
        P("req"),
    )
    out_specs = (
        P("req", "head"),
        P("req", "head", None, None),
        P("req", None, "head"),
        P("req", None, None),
    )
    return jax.shard_map(local, mesh=mesh, in_specs=in_specs, out_specs=out_specs, check_vma=False)
```

```python
import functools

import jax
import jax.numpy as jnp
from jax import lax
from jax.experimental import pallas as pl
from jax.experimental.pallas import tpu as pltpu
from jax.sharding import PartitionSpec as P

HEAD_DIM = 64
NSTATE = 128
KCONV = 4
DRAFT = 8
WINDOW = 8
DINNER = 3072
TILE = 256
EXTRA = NSTATE
PLANE = 4
RAW = (7, 6, 5)
PARTS = 3
SMALL = pl.CostEstimate(flops=1024, bytes_accessed=1024, transcendentals=0)

epsilon = 1e-05
HIGH = lax.Precision.HIGHEST
F32 = jnp.float32
BF16 = jnp.bfloat16


def iota(shape, axis):
    return lax.broadcasted_iota(jnp.int32, shape, axis)


def mm(a, b, precision=None):
    return jnp.dot(a, b, preferred_element_type=F32, precision=precision)


def mm_t(a, b):
    return lax.dot_general(a, b, (((1,), (1,)), ((), ())), preferred_element_type=F32)


def silu(x):
    return x * (1.0 / (1.0 + jnp.exp(-x)))


def conv_rows(rows, edges, taps, bias):
    slot = iota(rows.shape, 1)
    total = bias + taps[KCONV - 1 : KCONV] * rows
    for back in range(1, KCONV):
        mixed = jnp.where(slot >= DRAFT - back, edges, rows)
        total = total + taps[KCONV - 1 - back : KCONV - back] * pltpu.roll(mixed, back, 1)
    return total


def front_kernel(
    count,
    heads,
    table,
    lengths_in,
    accepted_in,
    hidden,
    vectors,
    w_gate,
    w_inner,
    w_out,
    w_ssm,
    w_step,
    head_rows,
    taps_inner,
    vector_tile,
    taps_ssm,
    bias_ssm,
    states,
    edge_inner,
    edge_ssm,
    mine,
    theirs,
    *rest,
):
    corr = rest[:WINDOW]
    normed, acc, squares, quant, gmat, cmat, select, boxes, edge_pad = rest[WINDOW:]
    step = pl.program_id(0)
    last = pl.num_programs(0) - 1
    rows = count * DRAFT
    width = acc.shape[1]
    half = width // 2

    @pl.when(step == 0)
    def _():
        wide = jnp.concatenate([hidden[0], hidden[1]], axis=1).astype(F32)
        scale = lax.rsqrt(jnp.mean(wide * wide, axis=-1, keepdims=True) + epsilon)
        norm = (wide * scale * vectors[0:1]).astype(BF16)
        normed[...] = norm
        acc[...] = jnp.zeros_like(acc)
        squares[...] = jnp.zeros_like(squares)
        boxes[...] = jnp.zeros_like(boxes)
        edge_pad[...] = jnp.zeros_like(edge_pad)
        edge_pad[:, DRAFT - KCONV + 1 :] = edge_ssm[...].astype(F32)
        row = iota((rows, rows), 0)
        col = iota((rows, rows), 1)
        request = row >> 3
        taken = jnp.zeros((rows, rows), jnp.int32)
        for r in range(count):
            taken = jnp.where(request == r, accepted_in[r], taken)
        same = request == (col >> 3)
        lower = same & ((col & 7) <= (row & 7))
        before = same & ((col & 7) < taken)
        raw = mm_t(norm, w_step[...]).astype(BF16).astype(F32) + head_rows[0:1]
        lengths = jnp.zeros((rows, heads), jnp.int32)
        chosen = jnp.zeros((rows, heads), jnp.int32)
        hrow = iota((rows, heads), 0)
        for r in range(count):
            lengths = jnp.where((hrow >> 3) == r, lengths_in[r], lengths)
            chosen = jnp.where((hrow >> 3) == r, accepted_in[r], chosen)
        soft = jnp.maximum(raw, 0.0) + jnp.log1p(jnp.exp(-jnp.abs(raw)))
        size = jnp.where((hrow & 7) < lengths, soft, 0.0)
        rate = -jnp.exp(head_rows[1:2])
        cum = mm(lower.astype(F32), size, HIGH)
        upto = mm(before.astype(F32), size, HIGH)
        weight = jnp.where(
            (hrow & 7) < chosen, jnp.exp(jnp.minimum(rate * (upto - cum), 0.0)) * size, 0.0
        )
        stacked = jnp.concatenate(
            [
                rate * cum,
                size,
                weight,
                jnp.exp(rate * upto),
                jnp.broadcast_to(head_rows[2:3], (16, heads)),
            ],
            axis=0,
        )
        for part in range(3):
            piece = stacked.astype(BF16)
            quant[part] = piece
            stacked = stacked - piece.astype(F32)
        sel_rows = jnp.where(
            same & ((row & 7) < KCONV - 1),
            ((col & 7) == (row & 7) + taken - 3).astype(F32),
            0.0,
        ).astype(BF16)
        sel_edge = jnp.where(
            same & ((row & 7) < KCONV - 1),
            ((col & 7) == (row & 7) + taken + 5).astype(F32),
            0.0,
        ).astype(BF16)
        select[0] = sel_rows
        select[1] = sel_edge
        ssm = jnp.concatenate([mm(norm, w_ssm[0]), mm(norm, w_ssm[1])], axis=1).astype(BF16)
        before_ssm = edge_pad[...]
        conv = conv_rows(
            ssm.astype(F32).reshape(count, DRAFT, 2 * NSTATE),
            before_ssm,
            taps_ssm[...].astype(F32),
            bias_ssm[...],
        )
        both = silu(conv).reshape(rows, 2 * NSTATE).astype(BF16)
        bmat = both[:, :NSTATE]
        cvec = both[:, NSTATE:]
        cmat[...] = cvec.astype(F32)
        pair = jnp.where(lower, mm_t(cvec, bmat), 0.0)
        fold = ((iota((rows, NSTATE), 0) & 7) == iota((rows, NSTATE), 1)).astype(F32)
        gmat[...] = mm(pair, fold, HIGH)
        kept = mm(sel_rows, ssm) + mm(
            sel_edge, before_ssm.reshape(rows, 2 * NSTATE).astype(BF16)
        )
        wide_b = bmat.astype(F32)
        place = iota((DRAFT, NSTATE), 0)
        for r in range(count):
            own = kept[r * DRAFT : (r + 1) * DRAFT]
            packed = jnp.where(
                place < 3,
                own[:, :NSTATE],
                jnp.where(
                    place < 6,
                    pltpu.roll(own[:, NSTATE:], 3, 0),
                    jnp.full((DRAFT, NSTATE), (table[1, r] + 1).astype(F32)),
                ),
            )
            boxes[table[0, r], :, :NSTATE] = jnp.concatenate(
                [wide_b[r * DRAFT : (r + 1) * DRAFT], packed], axis=0
            ).astype(BF16)
        for k in range(WINDOW):
            corr[k][:, width:] = boxes[k, :, :NSTATE]

    norm = normed[...]
    inner = mm(norm, w_inner[...]).astype(BF16)
    gate = mm(norm, w_gate[...]).astype(BF16).astype(F32)
    edge_pad[:, DRAFT - KCONV + 1 :] = edge_inner[...].astype(F32)
    edges = edge_pad[...]
    conv = conv_rows(
        inner.astype(F32).reshape(count, DRAFT, TILE),
        edges,
        taps_inner[...].astype(F32),
        vector_tile[1:2],
    )
    x = silu(conv).reshape(rows, TILE).astype(BF16).astype(F32)
    first_head = step * (TILE // HEAD_DIM)
    spread = (
        iota((heads, TILE), 0) == first_head + (iota((heads, TILE), 1) >> 6)
    ).astype(BF16)
    expanded = mm(quant[0], spread) + mm(quant[1], spread) + mm(quant[2], spread)
    level = expanded[:rows]
    weighted = expanded[rows : 2 * rows] * x
    past = jnp.concatenate(
        [
            mm_t(cmat[r * DRAFT : (r + 1) * DRAFT].astype(BF16), states[r])
            for r in range(count)
        ],
        axis=0,
    )
    out = jnp.exp(level) * past + expanded[4 * rows : 4 * rows + 1] * x
    level3 = level.reshape(count, DRAFT, TILE)
    weighted3 = weighted.reshape(count, DRAFT, TILE)
    total = jnp.zeros((count, DRAFT, TILE), F32)
    for u in range(DRAFT):
        factor = jnp.exp(jnp.minimum(level3 - level3[:, u : u + 1], 0.0))
        share = gmat[:, u : u + 1].reshape(count, DRAFT, 1)
        total = total + share * factor * weighted3[:, u : u + 1]
    out = (out + total.reshape(rows, TILE)).astype(BF16).astype(F32)
    gated = out * silu(gate)
    squared = gated * gated
    squares[...] += squared[:, :128] + squared[:, 128:]
    acc[...] += mm((gated * vector_tile[2:3]).astype(BF16), w_out[...])
    delta = expanded[2 * rows : 3 * rows] * x
    decay = expanded[3 * rows : 4 * rows]
    decay_hi = decay.astype(BF16).astype(F32)
    second = mm(select[0], inner) + mm(select[1], edges.reshape(rows, TILE).astype(BF16))
    place = iota((rows, TILE), 0) & 7
    second = jnp.where(
        place == 3, decay_hi, jnp.where(place == 4, decay - decay_hi, second)
    )
    for r in range(count):
        span = slice(r * DRAFT, (r + 1) * DRAFT)
        boxes[table[0, r]] = jnp.concatenate([delta[span], second[span]], axis=0).astype(BF16)
    here = pl.ds(pl.multiple_of(step * TILE, TILE), TILE)
    for k in range(WINDOW):
        corr[k][:, here] = boxes[k]

    @pl.when(step == last)
    def _():
        total_square = jnp.broadcast_to(
            jnp.sum(squares[...], axis=1, keepdims=True), squares.shape
        )
        mine[:, half:] = total_square
        theirs[:, half:] = total_square

        @pl.when(table[2, 0] == 0)
        def _():
            mine[:, :half] = acc[:, :half]
            theirs[:, :half] = acc[:, half:]

        @pl.when(table[2, 0] != 0)
        def _():
            mine[:, :half] = acc[:, half:]
            theirs[:, :half] = acc[:, :half]


def front(count, heads, width, depth, args):
    rows = count * DRAFT
    tiles = width // TILE

    def whole(shape):
        return pl.BlockSpec(shape, lambda j: (0,) * len(shape))

    in_specs = [
        *[pl.BlockSpec(memory_space=pltpu.SMEM)] * 3,
        whole((2, rows, depth // 2)),
        whole((3, depth)),
        pl.BlockSpec((depth, TILE), lambda j: (0, j)),
        pl.BlockSpec((depth, TILE), lambda j: (0, j)),
        pl.BlockSpec((TILE, depth), lambda j: (j, 0)),
        whole((2, depth, NSTATE)),
        whole((heads, depth)),
        whole((3, heads)),
        pl.BlockSpec((KCONV, TILE), lambda j: (0, j)),
        pl.BlockSpec((3, TILE), lambda j: (0, j)),
        whole((KCONV, 2 * NSTATE)),
        whole((1, 2 * NSTATE)),
        pl.BlockSpec((count, TILE, NSTATE), lambda j: (0, j, 0)),
        pl.BlockSpec((count, KCONV - 1, TILE), lambda j: (0, 0, j)),
        whole((count, KCONV - 1, 2 * NSTATE)),
    ]
    out_width = depth // 2 + 128
    out_shape = [jax.ShapeDtypeStruct((rows, out_width), F32)] * 2 + [
        jax.ShapeDtypeStruct((2 * DRAFT, width + EXTRA), BF16)
    ] * WINDOW
    out_specs = [whole((rows, out_width))] * 2 + [whole((2 * DRAFT, width + EXTRA))] * WINDOW
    return pl.pallas_call(
        functools.partial(front_kernel, count, heads),
        grid=(tiles,),
        in_specs=in_specs,
        out_specs=out_specs,
        out_shape=out_shape,
        scratch_shapes=[
            pltpu.VMEM((rows, depth), BF16),
            pltpu.VMEM((rows, depth), F32),
            pltpu.VMEM((rows, 128), F32),
            pltpu.VMEM((3, 4 * rows + 16, heads), BF16),
            pltpu.VMEM((rows, NSTATE), F32),
            pltpu.VMEM((rows, NSTATE), F32),
            pltpu.VMEM((2, rows, rows), BF16),
            pltpu.VMEM((WINDOW, 2 * DRAFT, TILE), BF16),
            pltpu.VMEM((count, DRAFT, TILE), F32),
        ],
        compiler_params=pltpu.CompilerParams(dimension_semantics=("arbitrary",)),
        cost_estimate=SMALL,
        name="front",
    )(*args)


def pick_kernel(count, peers, destination, states, *outs):
    picked = outs[: len(RAW)]
    table, sems = outs[len(RAW) :]
    here = lax.axis_index("req")
    reach = [
        lax.rem(lax.div(destination[r], count) - here + peers, peers) for r in range(count)
    ]
    index = []
    for k in range(WINDOW):
        index.append(sum((reach[r] == k).astype(jnp.int32) * r for r in range(count)))
        table[3, k] = index[k]
    copies = []
    for n, k in enumerate(RAW):
        copy = pltpu.make_async_copy(states.at[index[k]], picked[n], sems.at[n])
        copy.start()
        copies.append(copy)
    for r in range(count):
        table[0, r] = reach[r]
        table[1, r] = lax.rem(destination[r], count)
        table[2, r] = lax.axis_index("head")
    for copy in copies:
        copy.wait()


def in_hbm():
    return pl.BlockSpec(memory_space=pl.ANY)


def in_vmem():
    return pl.BlockSpec(memory_space=pltpu.VMEM)


def in_smem():
    return pl.BlockSpec(memory_space=pltpu.SMEM)


def pick(count, width, peers, destination, states):
    return pl.pallas_call(
        functools.partial(pick_kernel, count, peers),
        in_specs=[in_smem(), in_hbm()],
        out_specs=[in_vmem()] * len(RAW) + [in_smem()],
        out_shape=[jax.ShapeDtypeStruct((width, NSTATE), BF16)] * len(RAW)
        + [jax.ShapeDtypeStruct((4, max(count, WINDOW)), jnp.int32)],
        scratch_shapes=[pltpu.SemaphoreType.DMA((len(RAW),))],
        cost_estimate=SMALL,
        name="pick",
    )(destination, states)


def advance(corr, state, out):
    width = state.shape[0]
    line = iota((2 * DRAFT, NSTATE), 0)
    bmat = jnp.where(line < DRAFT, corr[:, width:].astype(F32), 0.0)
    ones = jnp.where((line == 11) | (line == 12), 1.0, 0.0)
    right = jnp.concatenate([bmat, ones], axis=1).astype(BF16)
    part = width // PARTS
    for c in range(PARTS):
        span = slice(c * part, (c + 1) * part)
        both = lax.dot_general(
            corr[:, span], right, (((0,), (0,)), ((), ())), preferred_element_type=F32
        )
        out[span] = (both[:, NSTATE:] * state[span].astype(F32) + both[:, :NSTATE]).astype(BF16)


def tail_rows(width):
    pairs = (width // NSTATE + 2) // 2
    return pairs, pairs * 2 * DRAFT


def column():
    return lax.rem(lax.axis_index("req"), PLANE)


def finish_kernel(offsets, aside, *refs):
    n = len(offsets)
    table, states = refs[:2]
    corr = refs[2 : 2 + n]
    outs = refs[2 + n : 2 + 2 * n]
    loaded, sems = refs[-2:]
    width = loaded.shape[1]
    pairs, _ = tail_rows(width)
    copies = []
    for i, k in enumerate(offsets):
        copy = pltpu.make_async_copy(states.at[table[3, k]], loaded.at[i], sems.at[i])
        copy.start()
        copies.append(copy)
    for i in range(n):
        low = corr[i][...].astype(F32)[DRAFT:]
        low = jnp.concatenate(
            [low, jnp.zeros((DRAFT, 2 * pairs * NSTATE - low.shape[1]), F32)], axis=1
        )
        for t in range(pairs):
            block = jnp.concatenate(
                [
                    low[:, t * NSTATE : (t + 1) * NSTATE],
                    low[:, (t + pairs) * NSTATE : (t + pairs + 1) * NSTATE],
                ],
                axis=0,
            )
            outs[i][width + t * 2 * DRAFT : width + (t + 1) * 2 * DRAFT] = block.astype(BF16)
        copies[i].wait()
        advance(corr[i], loaded.at[i], outs[i])
    if aside:
        other = refs[2 + 2 * n]

        @pl.when(column() == 3)
        def _():
            other[...] = outs[offsets.index(1)][...]

        @pl.when(column() != 3)
        def _():
            other[...] = outs[offsets.index(3)][...]


def finish(offsets, aside, table, states, corr):
    n = len(offsets)
    width = states.shape[1]
    shape = jax.ShapeDtypeStruct((width + tail_rows(width)[1], NSTATE), BF16)
    outs = n + (1 if aside else 0)
    return pl.pallas_call(
        functools.partial(finish_kernel, offsets, aside),
        in_specs=[in_smem(), in_hbm()] + [in_vmem()] * n,
        out_specs=[in_vmem()] * outs,
        out_shape=[shape] * outs,
        scratch_shapes=[
            pltpu.VMEM((n, width, NSTATE), BF16),
            pltpu.SemaphoreType.DMA((n,)),
        ],
        cost_estimate=SMALL,
        name="finish",
    )(table, states, *[corr[k] for k in offsets])


def mark_of(low):
    return jnp.max(low[6:7]).astype(jnp.int32) - 1


def merge_kernel(table, states, raw7, raw6, raw5, raw5_aside, *refs):
    corr = refs[:4]
    kept, loaded, merged, sem_in, sem_out = refs[4:]
    width = loaded.shape[1]

    def fetch(i, source):
        return pltpu.make_async_copy(source, loaded.at[i], sem_in.at[i])

    fetch(0, states.at[table[3, 0]]).start()
    fetch(1, raw7).start()
    fetch(2, raw6).start()

    @pl.when(column() == 0)
    def _():
        fetch(3, raw5_aside).start()

    @pl.when(column() != 0)
    def _():
        fetch(3, raw5).start()

    slots = [mark_of(ref[:, width:].astype(F32)[DRAFT:]) for ref in corr]

    def put(i):
        return pltpu.make_async_copy(merged.at[i], kept.at[slots[i]], sem_out.at[i])

    for i in range(4):
        fetch(i, raw7).wait()

        @pl.when(slots[i] >= 0)
        def _(i=i):
            advance(corr[i], loaded.at[i], merged.at[i])
            put(i).start()

    for i in range(4):

        @pl.when(slots[i] >= 0)
        def _(i=i):
            put(i).wait()


def merge(count, table, states, raws, corr):
    width = states.shape[1]
    return pl.pallas_call(
        merge_kernel,
        in_specs=[in_smem()] + [in_hbm()] * 5 + [in_vmem()] * 4,
        out_specs=in_hbm(),
        out_shape=jax.ShapeDtypeStruct((count, width, NSTATE), BF16),
        scratch_shapes=[
            pltpu.VMEM((4, width, NSTATE), BF16),
            pltpu.VMEM((4, width, NSTATE), BF16),
            pltpu.SemaphoreType.DMA((4,)),
            pltpu.SemaphoreType.DMA((4,)),
        ],
        cost_estimate=SMALL,
        name="merge",
    )(table, states, *raws, *corr)


def place_kernel(first, second, third, fourth, aside, *refs):
    corr = refs[:4]
    _, kept, out_inner, out_ssm, loaded, sem_in, sem_out = refs[4:]
    width = out_inner.shape[2]
    pairs, _ = tail_rows(width)

    def fetch(i, source):
        return pltpu.make_async_copy(source, loaded.at[i], sem_in.at[i])

    fetch(3, fourth).start()
    fetch(1, second).start()
    for i, source, turned in ((0, first, 0), (2, third, 1)):

        @pl.when(column() == turned)
        def _(i=i):
            fetch(i, aside).start()

        @pl.when(column() != turned)
        def _(i=i, source=source):
            fetch(i, source).start()

    def write_edges(slot, inner, low):
        out_inner[slot] = inner[: KCONV - 1].astype(BF16)
        high = pltpu.roll(low, DRAFT - 3, 0)
        out_ssm[slot] = jnp.concatenate([low[:3], high[:3]], axis=1).astype(BF16)

    for ref in corr:
        low = ref[...].astype(F32)[DRAFT:]
        slot = mark_of(low[:, width:])

        @pl.when(slot >= 0)
        def _(slot=slot, low=low):
            write_edges(slot, low[:, :width], low[:, width:])

    def put(i, slot):
        return pltpu.make_async_copy(
            loaded.at[i, pl.ds(0, width)], kept.at[slot], sem_out.at[i]
        )

    slots = []
    for i in (3, 1, 2, 0):
        fetch(i, fourth).wait()
        parts = [
            loaded[i, width + t * 2 * DRAFT : width + (t + 1) * 2 * DRAFT].astype(F32)
            for t in range(pairs)
        ]
        lows = [part[:DRAFT] for part in parts] + [part[DRAFT:] for part in parts]
        tiles = width // NSTATE
        slot = mark_of(lows[tiles])
        slots.append((i, slot))

        @pl.when(slot >= 0)
        def _(i=i, slot=slot, lows=lows):
            put(i, slot).start()
            write_edges(slot, jnp.concatenate(lows[:tiles], axis=1), lows[tiles])

    for i, slot in slots:

        @pl.when(slot >= 0)
        def _(i=i, slot=slot):
            put(i, slot).wait()


def place(count, width, messages, corr, kept):
    rows = width + tail_rows(width)[1]
    return pl.pallas_call(
        place_kernel,
        in_specs=[in_hbm()] * 5 + [in_vmem()] * 4 + [in_hbm()],
        out_specs=[in_hbm(), in_vmem(), in_vmem()],
        out_shape=[
            jax.ShapeDtypeStruct((count, width, NSTATE), BF16),
            jax.ShapeDtypeStruct((count, KCONV - 1, width), BF16),
            jax.ShapeDtypeStruct((count, KCONV - 1, 2 * NSTATE), BF16),
        ],
        input_output_aliases={9: 0},
        scratch_shapes=[
            pltpu.VMEM((4, rows, NSTATE), BF16),
            pltpu.SemaphoreType.DMA((4,)),
            pltpu.SemaphoreType.DMA((4,)),
        ],
        cost_estimate=SMALL,
        name="place",
    )(*messages, *corr, kept)


def moved(array, by, columns=range(PLANE)):
    length = lax.axis_size("req")
    pairs = [(i, (i + by[i % PLANE]) % length) for i in range(length) if i % PLANE in columns]
    return lax.ppermute(array, "req", pairs)


def local(
    hidden_in,
    norm_gain,
    proj_gate,
    proj_inner,
    proj_ssm,
    proj_step,
    step_bias,
    decay_log,
    skip_gain,
    conv_inner,
    conv_inner_bias,
    conv_ssm,
    conv_ssm_bias,
    gate_gain,
    proj_out,
    states_in,
    edge_inner,
    edge_ssm,
    draft_lengths,
    accepted,
    destination,
):
    count, heads = states_in.shape[:2]
    depth, width = proj_inner.shape
    peers = lax.axis_size("req")
    flat = states_in.reshape(count, width, NSTATE)
    raw7, raw6, raw5, table = pick(count, width, peers, destination, flat)
    raw5_z = moved(raw5, [8] * PLANE, (3,))
    raw7 = moved(raw7, [7] * PLANE)
    raw6 = moved(raw6, [6] * PLANE)
    raw5 = moved(raw5, [5] * PLANE, (0, 1, 2))
    results = front(
        count,
        heads,
        width,
        depth,
        (
            table,
            draft_lengths,
            accepted,
            lax.all_gather(hidden_in, "head", axis=0, tiled=False),
            jnp.stack([norm_gain, conv_inner_bias, gate_gain]),
            proj_gate,
            proj_inner,
            proj_out,
            lax.all_gather(proj_ssm, "head", axis=0, tiled=False),
            proj_step.T,
            jnp.stack([step_bias, decay_log, skip_gain]),
            conv_inner,
            jnp.stack([norm_gain, conv_inner_bias, gate_gain]),
            conv_ssm,
            conv_ssm_bias.reshape(1, 2 * NSTATE),
            flat,
            edge_inner,
            edge_ssm,
        ),
    )
    mine, theirs = results[:2]
    corr = list(results[2:])
    (fourth,) = finish((4,), False, table, flat, corr)
    fourth = moved(fourth, [4] * PLANE)
    first, second, third, aside = finish((1, 2, 3), True, table, flat, corr)

    pair = lax.all_gather(theirs, "head", axis=0, tiled=False)
    other = jnp.where(lax.axis_index("head") == 0, pair[1], pair[0])
    total = mine + other
    half = depth // 2
    scale = lax.rsqrt(total[:, half : half + 1] / DINNER + epsilon)
    hidden_out = (hidden_in.astype(F32) + total[:, :half] * scale).astype(BF16)

    raw7, raw6, raw5, raw5_z, fourth, aside, third, second, first, *late = (
        lax.optimization_barrier(
            (raw7, raw6, raw5, raw5_z, fourth, aside, third, second, first, *corr[5:])
        )
    )
    corr[5:] = late
    raw5_turned = moved(raw5_z, [-3] * PLANE, (3,))
    aside = moved(aside, [4] * PLANE, (2, 3))
    third = moved(third, [3] * PLANE, (0, 1, 3))
    second = moved(second, [2] * PLANE)
    turned = moved(aside, [0, 0, -1, -3], (2, 3))
    third, first = lax.optimization_barrier((third, first))
    first = moved(first, [1] * PLANE, (0, 1, 2))
    raw5_turned, corr[7] = lax.optimization_barrier((raw5_turned, corr[7]))
    corr[7] = moved(corr[7], [7] * PLANE)
    corr[7], corr[6] = lax.optimization_barrier((corr[7], corr[6]))
    corr[6] = moved(corr[6], [6] * PLANE)
    corr[6], corr[5] = lax.optimization_barrier((corr[6], corr[5]))
    corr[5] = moved(corr[5], [5] * PLANE)
    sent = [corr[0], corr[7], corr[6], corr[5]]
    kept = merge(count, table, flat, (raw7, raw6, raw5, raw5_turned), sent)
    kept, kept_inner, kept_ssm = place(
        count, width, (first, second, third, fourth, turned), sent, kept
    )
    return (hidden_out, kept.reshape(states_in.shape), kept_inner, kept_ssm)


def solution(mesh):
    in_specs = (
        P("req", "head"),
        P(),
        P(None, "head"),
        P(None, "head"),
        P(None, "head"),
        P(None, "head"),
        P("head"),
        P("head"),
        P("head"),
        P(None, "head"),
        P("head"),
        P(),
        P(),
        P("head"),
        P("head", None),
        P("req", "head", None, None),
        P("req", None, "head"),
        P("req", None, None),
        P("req"),
        P("req"),
        P("req"),
    )
    out_specs = (
        P("req", "head"),
        P("req", "head", None, None),
        P("req", None, "head"),
        P("req", None, None),
    )
    return jax.shard_map(local, mesh=mesh, in_specs=in_specs, out_specs=out_specs, check_vma=False)
```

```python
import functools

import jax
import jax.numpy as jnp
from jax import lax
from jax.experimental import pallas as pl
from jax.experimental.pallas import tpu as pltpu
from jax.sharding import PartitionSpec as P

HEAD_DIM = 64
NSTATE = 128
KCONV = 4
DRAFT = 8
WINDOW = 8
DINNER = 3072
TILE = 256
EXTRA = NSTATE
PLANE = 4
RAW = (4, 5, 6, 7)
PARTS = 3
SMALL = pl.CostEstimate(flops=1024, bytes_accessed=1024, transcendentals=0)
STEP = pl.CostEstimate(flops=1024, bytes_accessed=40_000_000, transcendentals=0)

epsilon = 1e-05
HIGH = lax.Precision.HIGHEST
F32 = jnp.float32
BF16 = jnp.bfloat16


def iota(shape, axis):
    return lax.broadcasted_iota(jnp.int32, shape, axis)


def mm(a, b, precision=None):
    return jnp.dot(a, b, preferred_element_type=F32, precision=precision)


def mm_t(a, b):
    return lax.dot_general(a, b, (((1,), (1,)), ((), ())), preferred_element_type=F32)


def silu(x):
    return x * (1.0 / (1.0 + jnp.exp(-x)))


def conv_rows(rows, edges, taps, bias):
    slot = iota(rows.shape, 1)
    total = bias + taps[KCONV - 1 : KCONV] * rows
    for back in range(1, KCONV):
        mixed = jnp.where(slot >= DRAFT - back, edges, rows)
        total = total + taps[KCONV - 1 - back : KCONV - back] * pltpu.roll(mixed, back, 1)
    return total


def front_kernel(
    count,
    heads,
    table,
    lengths_in,
    accepted_in,
    hidden,
    vectors,
    w_gate,
    w_inner,
    w_out,
    w_ssm,
    w_step,
    head_rows,
    taps_inner,
    vector_tile,
    taps_ssm,
    bias_ssm,
    states,
    edge_inner,
    edge_ssm,
    mine,
    theirs,
    *rest,
):
    corr = rest[:WINDOW]
    normed, acc, squares, quant, gmat, cmat, select, boxes, edge_pad = rest[WINDOW:]
    step = pl.program_id(0)
    last = pl.num_programs(0) - 1
    rows = count * DRAFT
    width = acc.shape[1]
    half = width // 2

    @pl.when(step == 0)
    def _():
        wide = jnp.concatenate([hidden[0], hidden[1]], axis=1).astype(F32)
        scale = lax.rsqrt(jnp.mean(wide * wide, axis=-1, keepdims=True) + epsilon)
        norm = (wide * scale * vectors[0:1]).astype(BF16)
        normed[...] = norm
        acc[...] = jnp.zeros_like(acc)
        squares[...] = jnp.zeros_like(squares)
        boxes[...] = jnp.zeros_like(boxes)
        edge_pad[...] = jnp.zeros_like(edge_pad)
        edge_pad[:, DRAFT - KCONV + 1 :] = edge_ssm[...].astype(F32)
        row = iota((rows, rows), 0)
        col = iota((rows, rows), 1)
        request = row >> 3
        taken = jnp.zeros((rows, rows), jnp.int32)
        for r in range(count):
            taken = jnp.where(request == r, accepted_in[r], taken)
        same = request == (col >> 3)
        lower = same & ((col & 7) <= (row & 7))
        before = same & ((col & 7) < taken)
        raw = mm_t(norm, w_step[...]).astype(BF16).astype(F32) + head_rows[0:1]
        lengths = jnp.zeros((rows, heads), jnp.int32)
        chosen = jnp.zeros((rows, heads), jnp.int32)
        hrow = iota((rows, heads), 0)
        for r in range(count):
            lengths = jnp.where((hrow >> 3) == r, lengths_in[r], lengths)
            chosen = jnp.where((hrow >> 3) == r, accepted_in[r], chosen)
        soft = jnp.maximum(raw, 0.0) + jnp.log1p(jnp.exp(-jnp.abs(raw)))
        size = jnp.where((hrow & 7) < lengths, soft, 0.0)
        rate = -jnp.exp(head_rows[1:2])
        cum = mm(lower.astype(F32), size, HIGH)
        upto = mm(before.astype(F32), size, HIGH)
        weight = jnp.where(
            (hrow & 7) < chosen, jnp.exp(jnp.minimum(rate * (upto - cum), 0.0)) * size, 0.0
        )
        stacked = jnp.concatenate(
            [
                rate * cum,
                size,
                weight,
                jnp.exp(rate * upto),
                jnp.broadcast_to(head_rows[2:3], (16, heads)),
            ],
            axis=0,
        )
        for part in range(3):
            piece = stacked.astype(BF16)
            quant[part] = piece
            stacked = stacked - piece.astype(F32)
        sel_rows = jnp.where(
            same & ((row & 7) < KCONV - 1),
            ((col & 7) == (row & 7) + taken - 3).astype(F32),
            0.0,
        ).astype(BF16)
        sel_edge = jnp.where(
            same & ((row & 7) < KCONV - 1),
            ((col & 7) == (row & 7) + taken + 5).astype(F32),
            0.0,
        ).astype(BF16)
        select[0] = sel_rows
        select[1] = sel_edge
        ssm = jnp.concatenate([mm(norm, w_ssm[0]), mm(norm, w_ssm[1])], axis=1).astype(BF16)
        before_ssm = edge_pad[...]
        conv = conv_rows(
            ssm.astype(F32).reshape(count, DRAFT, 2 * NSTATE),
            before_ssm,
            taps_ssm[...].astype(F32),
            bias_ssm[...],
        )
        both = silu(conv).reshape(rows, 2 * NSTATE).astype(BF16)
        bmat = both[:, :NSTATE]
        cvec = both[:, NSTATE:]
        cmat[...] = cvec.astype(F32)
        pair = jnp.where(lower, mm_t(cvec, bmat), 0.0)
        fold = ((iota((rows, NSTATE), 0) & 7) == iota((rows, NSTATE), 1)).astype(F32)
        gmat[...] = mm(pair, fold, HIGH)
        kept = mm(sel_rows, ssm) + mm(
            sel_edge, before_ssm.reshape(rows, 2 * NSTATE).astype(BF16)
        )
        wide_b = bmat.astype(F32)
        place = iota((DRAFT, NSTATE), 0)
        for r in range(count):
            own = kept[r * DRAFT : (r + 1) * DRAFT]
            packed = jnp.where(
                place < 3,
                own[:, :NSTATE],
                jnp.where(
                    place < 6,
                    pltpu.roll(own[:, NSTATE:], 3, 0),
                    jnp.full((DRAFT, NSTATE), (table[1, r] + 1).astype(F32)),
                ),
            )
            boxes[table[0, r], :, :NSTATE] = jnp.concatenate(
                [wide_b[r * DRAFT : (r + 1) * DRAFT], packed], axis=0
            ).astype(BF16)
        for k in range(WINDOW):
            corr[k][:, width:] = boxes[k, :, :NSTATE]

    norm = normed[...]
    inner = mm(norm, w_inner[...]).astype(BF16)
    gate = mm(norm, w_gate[...]).astype(BF16).astype(F32)
    edge_pad[:, DRAFT - KCONV + 1 :] = edge_inner[...].astype(F32)
    edges = edge_pad[...]
    conv = conv_rows(
        inner.astype(F32).reshape(count, DRAFT, TILE),
        edges,
        taps_inner[...].astype(F32),
        vector_tile[1:2],
    )
    x = silu(conv).reshape(rows, TILE).astype(BF16).astype(F32)
    first_head = step * (TILE // HEAD_DIM)
    spread = (
        iota((heads, TILE), 0) == first_head + (iota((heads, TILE), 1) >> 6)
    ).astype(BF16)
    expanded = mm(quant[0], spread) + mm(quant[1], spread) + mm(quant[2], spread)
    level = expanded[:rows]
    weighted = expanded[rows : 2 * rows] * x
    past = jnp.concatenate(
        [
            mm_t(cmat[r * DRAFT : (r + 1) * DRAFT].astype(BF16), states[r])
            for r in range(count)
        ],
        axis=0,
    )
    out = jnp.exp(level) * past + expanded[4 * rows : 4 * rows + 1] * x
    level3 = level.reshape(count, DRAFT, TILE)
    weighted3 = weighted.reshape(count, DRAFT, TILE)
    total = jnp.zeros((count, DRAFT, TILE), F32)
    for u in range(DRAFT):
        factor = jnp.exp(jnp.minimum(level3 - level3[:, u : u + 1], 0.0))
        share = gmat[:, u : u + 1].reshape(count, DRAFT, 1)
        total = total + share * factor * weighted3[:, u : u + 1]
    out = (out + total.reshape(rows, TILE)).astype(BF16).astype(F32)
    gated = out * silu(gate)
    squared = gated * gated
    squares[...] += squared[:, :128] + squared[:, 128:]
    acc[...] += mm((gated * vector_tile[2:3]).astype(BF16), w_out[...])
    delta = expanded[2 * rows : 3 * rows] * x
    decay = expanded[3 * rows : 4 * rows]
    decay_hi = decay.astype(BF16).astype(F32)
    second = mm(select[0], inner) + mm(select[1], edges.reshape(rows, TILE).astype(BF16))
    place = iota((rows, TILE), 0) & 7
    second = jnp.where(
        place == 3, decay_hi, jnp.where(place == 4, decay - decay_hi, second)
    )
    for r in range(count):
        span = slice(r * DRAFT, (r + 1) * DRAFT)
        boxes[table[0, r]] = jnp.concatenate([delta[span], second[span]], axis=0).astype(BF16)
    here = pl.ds(pl.multiple_of(step * TILE, TILE), TILE)
    for k in range(WINDOW):
        corr[k][:, here] = boxes[k]

    @pl.when(step == last)
    def _():
        total_square = jnp.broadcast_to(
            jnp.sum(squares[...], axis=1, keepdims=True), squares.shape
        )
        mine[:, half:] = total_square
        theirs[:, half:] = total_square

        @pl.when(table[2, 0] == 0)
        def _():
            mine[:, :half] = acc[:, :half]
            theirs[:, :half] = acc[:, half:]

        @pl.when(table[2, 0] != 0)
        def _():
            mine[:, :half] = acc[:, half:]
            theirs[:, :half] = acc[:, :half]


def front(count, heads, width, depth, args):
    rows = count * DRAFT
    tiles = width // TILE

    def whole(shape):
        return pl.BlockSpec(shape, lambda j: (0,) * len(shape))

    in_specs = [
        *[pl.BlockSpec(memory_space=pltpu.SMEM)] * 3,
        whole((2, rows, depth // 2)),
        whole((3, depth)),
        pl.BlockSpec((depth, TILE), lambda j: (0, j)),
        pl.BlockSpec((depth, TILE), lambda j: (0, j)),
        pl.BlockSpec((TILE, depth), lambda j: (j, 0)),
        whole((2, depth, NSTATE)),
        whole((heads, depth)),
        whole((3, heads)),
        pl.BlockSpec((KCONV, TILE), lambda j: (0, j)),
        pl.BlockSpec((3, TILE), lambda j: (0, j)),
        whole((KCONV, 2 * NSTATE)),
        whole((1, 2 * NSTATE)),
        pl.BlockSpec((count, TILE, NSTATE), lambda j: (0, j, 0)),
        pl.BlockSpec((count, KCONV - 1, TILE), lambda j: (0, 0, j)),
        whole((count, KCONV - 1, 2 * NSTATE)),
    ]
    out_width = depth // 2 + 128
    out_shape = [jax.ShapeDtypeStruct((rows, out_width), F32)] * 2 + [
        jax.ShapeDtypeStruct((2 * DRAFT, width + EXTRA), BF16)
    ] * WINDOW
    out_specs = [whole((rows, out_width))] * 2 + [whole((2 * DRAFT, width + EXTRA))] * WINDOW
    return pl.pallas_call(
        functools.partial(front_kernel, count, heads),
        grid=(tiles,),
        in_specs=in_specs,
        out_specs=out_specs,
        out_shape=out_shape,
        scratch_shapes=[
            pltpu.VMEM((rows, depth), BF16),
            pltpu.VMEM((rows, depth), F32),
            pltpu.VMEM((rows, 128), F32),
            pltpu.VMEM((3, 4 * rows + 16, heads), BF16),
            pltpu.VMEM((rows, NSTATE), F32),
            pltpu.VMEM((rows, NSTATE), F32),
            pltpu.VMEM((2, rows, rows), BF16),
            pltpu.VMEM((WINDOW, 2 * DRAFT, TILE), BF16),
            pltpu.VMEM((count, DRAFT, TILE), F32),
        ],
        compiler_params=pltpu.CompilerParams(dimension_semantics=("arbitrary",)),
        cost_estimate=SMALL,
        name="front",
    )(*args)


def pick_kernel(count, peers, destination, states, *outs):
    picked = outs[: len(RAW)]
    table, sems = outs[len(RAW) :]
    here = lax.axis_index("req")
    reach = [
        lax.rem(lax.div(destination[r], count) - here + peers, peers) for r in range(count)
    ]
    index = []
    for k in range(WINDOW):
        index.append(sum((reach[r] == k).astype(jnp.int32) * r for r in range(count)))
        table[3, k] = index[k]
    copies = []
    for n, k in enumerate(RAW):
        copy = pltpu.make_async_copy(states.at[index[k]], picked[n], sems.at[n])
        copy.start()
        copies.append(copy)
    for r in range(count):
        table[0, r] = reach[r]
        table[1, r] = lax.rem(destination[r], count)
        table[2, r] = lax.axis_index("head")
    for copy in copies:
        copy.wait()


def in_hbm():
    return pl.BlockSpec(memory_space=pl.ANY)


def in_vmem():
    return pl.BlockSpec(memory_space=pltpu.VMEM)


def in_smem():
    return pl.BlockSpec(memory_space=pltpu.SMEM)


def pick(count, width, peers, destination, states):
    return pl.pallas_call(
        functools.partial(pick_kernel, count, peers),
        in_specs=[in_smem(), in_hbm()],
        out_specs=[in_vmem()] * len(RAW) + [in_smem()],
        out_shape=[jax.ShapeDtypeStruct((width, NSTATE), BF16)] * len(RAW)
        + [jax.ShapeDtypeStruct((4, max(count, WINDOW)), jnp.int32)],
        scratch_shapes=[pltpu.SemaphoreType.DMA((len(RAW),))],
        cost_estimate=SMALL,
        name="pick",
    )(destination, states)


def advance(corr, state, out):
    width = state.shape[0]
    line = iota((2 * DRAFT, NSTATE), 0)
    bmat = jnp.where(line < DRAFT, corr[:, width:].astype(F32), 0.0)
    ones = jnp.where((line == 11) | (line == 12), 1.0, 0.0)
    right = jnp.concatenate([bmat, ones], axis=1).astype(BF16)
    part = width // PARTS
    for c in range(PARTS):
        span = slice(c * part, (c + 1) * part)
        both = lax.dot_general(
            corr[:, span], right, (((0,), (0,)), ((), ())), preferred_element_type=F32
        )
        out[span] = (both[:, NSTATE:] * state[span].astype(F32) + both[:, :NSTATE]).astype(BF16)


def tail_rows(width):
    pairs = (width // NSTATE + 2) // 2
    return pairs, pairs * 2 * DRAFT


def column():
    return lax.rem(lax.axis_index("req"), PLANE)


def finish_kernel(offsets, *refs):
    n = len(offsets)
    table, states = refs[:2]
    corr = refs[2 : 2 + n]
    outs = refs[2 + n : 2 + 2 * n]
    loaded, sems = refs[-2:]
    width = loaded.shape[1]
    pairs, _ = tail_rows(width)
    copies = []
    for i, k in enumerate(offsets):
        copy = pltpu.make_async_copy(states.at[table[3, k]], loaded.at[i], sems.at[i])
        copy.start()
        copies.append(copy)
    for i in range(n):
        low = corr[i][...].astype(F32)[DRAFT:]
        low = jnp.concatenate(
            [low, jnp.zeros((DRAFT, 2 * pairs * NSTATE - low.shape[1]), F32)], axis=1
        )
        for t in range(pairs):
            block = jnp.concatenate(
                [
                    low[:, t * NSTATE : (t + 1) * NSTATE],
                    low[:, (t + pairs) * NSTATE : (t + pairs + 1) * NSTATE],
                ],
                axis=0,
            )
            outs[i][width + t * 2 * DRAFT : width + (t + 1) * 2 * DRAFT] = block.astype(BF16)
        copies[i].wait()
        advance(corr[i], loaded.at[i], outs[i])


def finish(offsets, table, states, corr):
    n = len(offsets)
    width = states.shape[1]
    shape = jax.ShapeDtypeStruct((width + tail_rows(width)[1], NSTATE), BF16)
    return pl.pallas_call(
        functools.partial(finish_kernel, offsets),
        in_specs=[in_smem(), in_hbm()] + [in_vmem()] * n,
        out_specs=[in_vmem()] * n,
        out_shape=[shape] * n,
        scratch_shapes=[
            pltpu.VMEM((n, width, NSTATE), BF16),
            pltpu.SemaphoreType.DMA((n,)),
        ],
        cost_estimate=SMALL,
        name="finish",
    )(table, states, *[corr[k] for k in offsets])


def mark_of(low):
    return jnp.max(low[6:7]).astype(jnp.int32) - 1


def merge_kernel(table, states, *refs):
    n = 1 + len(RAW)
    raws = refs[: n - 1]
    turned = refs[n - 1]
    corr = refs[n : 2 * n]
    _, kept, loaded, merged, sem_in, sem_out = refs[2 * n :]
    width = loaded.shape[0]
    own = pltpu.make_async_copy(states.at[table[3, 0]], loaded, sem_in)
    own.start()
    slots = [mark_of(ref[:, width:].astype(F32)[DRAFT:]) for ref in corr]

    def put(i):
        return pltpu.make_async_copy(merged.at[i], kept.at[slots[i]], sem_out.at[i])

    for i in range(n):
        if i == 0:
            own.wait()

        @pl.when(slots[i] >= 0)
        def _(i=i):
            if i == 0:
                advance(corr[i], loaded, merged.at[i])
            elif RAW[i - 1] == 5:

                @pl.when(column() == 0)
                def _():
                    advance(corr[i], turned, merged.at[i])

                @pl.when(column() != 0)
                def _():
                    advance(corr[i], raws[i - 1], merged.at[i])

            else:
                advance(corr[i], raws[i - 1], merged.at[i])
            put(i).start()

    for i in range(n):

        @pl.when(slots[i] >= 0)
        def _(i=i):
            put(i).wait()


def merge(count, table, states, raws, turned, corr, kept):
    width = states.shape[1]
    n = 1 + len(RAW)
    return pl.pallas_call(
        merge_kernel,
        in_specs=[in_smem(), in_hbm()] + [in_vmem()] * (2 * n) + [in_hbm()],
        out_specs=in_hbm(),
        out_shape=jax.ShapeDtypeStruct((count, width, NSTATE), BF16),
        scratch_shapes=[
            pltpu.VMEM((width, NSTATE), BF16),
            pltpu.VMEM((n, width, NSTATE), BF16),
            pltpu.SemaphoreType.DMA,
            pltpu.SemaphoreType.DMA((n,)),
        ],
        input_output_aliases={2 + 2 * n: 0},
        cost_estimate=STEP,
        name="merge",
    )(table, states, *raws, turned, *corr, kept)


def halves(ref, width):
    parts = [
        ref[row : row + 2 * DRAFT].astype(F32)
        for row in range(width, ref.shape[0], 2 * DRAFT)
    ]
    return [part[:DRAFT] for part in parts] + [part[DRAFT:] for part in parts]


def place_kernel(width, message, *refs):
    kept, sem = refs[-2:]
    slot = mark_of(halves(message, width)[width // NSTATE])

    @pl.when(slot >= 0)
    def _():
        copy = pltpu.make_async_copy(message.at[pl.ds(0, width)], kept.at[slot], sem)
        copy.start()
        copy.wait()


def place(count, width, message, kept=None):
    return pl.pallas_call(
        functools.partial(place_kernel, width),
        in_specs=[in_vmem()] + ([] if kept is None else [in_hbm()]),
        out_specs=in_hbm(),
        out_shape=jax.ShapeDtypeStruct((count, width, NSTATE), BF16),
        input_output_aliases={} if kept is None else {1: 0},
        scratch_shapes=[pltpu.SemaphoreType.DMA],
        cost_estimate=STEP,
        name="place",
    )(message, *([] if kept is None else [kept]))


def close_kernel(n, *refs):
    messages = refs[:n]
    corr = refs[n : n + 1 + len(RAW)]
    _, kept, out_inner, out_ssm, sem = refs[n + 1 + len(RAW) :]
    width = out_inner.shape[2]
    tiles = width // NSTATE
    marks = []
    for ref in messages:
        lows = halves(ref, width)
        marks.append((mark_of(lows[tiles]), lows))
    last = marks[0][0]

    def put():
        return pltpu.make_async_copy(messages[0].at[pl.ds(0, width)], kept.at[last], sem)

    @pl.when(last >= 0)
    def _():
        put().start()

    def write_edges(slot, inner, low):
        out_inner[slot] = inner[: KCONV - 1].astype(BF16)
        high = pltpu.roll(low, DRAFT - 3, 0)
        out_ssm[slot] = jnp.concatenate([low[:3], high[:3]], axis=1).astype(BF16)

    for ref in corr:
        low = ref[...].astype(F32)[DRAFT:]
        slot = mark_of(low[:, width:])

        @pl.when(slot >= 0)
        def _(slot=slot, low=low):
            write_edges(slot, low[:, :width], low[:, width:])

    for slot, lows in marks:

        @pl.when(slot >= 0)
        def _(slot=slot, lows=lows):
            write_edges(slot, jnp.concatenate(lows[:tiles], axis=1), lows[tiles])

    @pl.when(last >= 0)
    def _():
        put().wait()


def close(count, width, messages, corr, kept):
    n = len(messages)
    return pl.pallas_call(
        functools.partial(close_kernel, n),
        in_specs=[in_vmem()] * (n + len(corr)) + [in_hbm()],
        out_specs=[in_hbm(), in_vmem(), in_vmem()],
        out_shape=[
            jax.ShapeDtypeStruct((count, width, NSTATE), BF16),
            jax.ShapeDtypeStruct((count, KCONV - 1, width), BF16),
            jax.ShapeDtypeStruct((count, KCONV - 1, 2 * NSTATE), BF16),
        ],
        input_output_aliases={n + len(corr): 0},
        scratch_shapes=[pltpu.SemaphoreType.DMA],
        cost_estimate=SMALL,
        name="close",
    )(*messages, *corr, kept)


def moved(array, by, columns=tuple(range(PLANE))):
    length = lax.axis_size("req")
    pairs = [(i, (i + by) % length) for i in range(length) if i % PLANE in columns]
    return lax.ppermute(array, "req", pairs)


def local(
    hidden_in,
    norm_gain,
    proj_gate,
    proj_inner,
    proj_ssm,
    proj_step,
    step_bias,
    decay_log,
    skip_gain,
    conv_inner,
    conv_inner_bias,
    conv_ssm,
    conv_ssm_bias,
    gate_gain,
    proj_out,
    states_in,
    edge_inner,
    edge_ssm,
    draft_lengths,
    accepted,
    destination,
):
    count, heads = states_in.shape[:2]
    depth, width = proj_inner.shape
    peers = lax.axis_size("req")
    flat = states_in.reshape(count, width, NSTATE)
    *raws, table = pick(count, width, peers, destination, flat)
    raw5_z = moved(raws[1], 8, (3,))
    raws = [
        moved(raw, k, (0, 1, 2) if k == 5 else (0, 1, 2, 3)) for raw, k in zip(raws, RAW)
    ]
    table, ready, ready_ssm = lax.optimization_barrier((table, hidden_in, proj_ssm))
    vectors = jnp.stack([norm_gain, conv_inner_bias, gate_gain])
    results = front(
        count,
        heads,
        width,
        depth,
        (
            table,
            draft_lengths,
            accepted,
            lax.all_gather(ready, "head", axis=0, tiled=False),
            vectors,
            proj_gate,
            proj_inner,
            proj_out,
            lax.all_gather(ready_ssm, "head", axis=0, tiled=False),
            proj_step.T,
            jnp.stack([step_bias, decay_log, skip_gain]),
            conv_inner,
            vectors,
            conv_ssm,
            conv_ssm_bias.reshape(1, 2 * NSTATE),
            flat,
            edge_inner,
            edge_ssm,
        ),
    )
    mine, theirs = results[:2]
    corr = list(results[2:])
    first, second, third = finish((1, 2, 3), table, flat, corr)

    pair = lax.all_gather(theirs, "head", axis=0, tiled=False)
    other = jnp.where(lax.axis_index("head") == 0, pair[1], pair[0])
    total = mine + other
    half = depth // 2
    scale = lax.rsqrt(total[:, half : half + 1] / DINNER + epsilon)
    hidden_out = (hidden_in.astype(F32) + total[:, :half] * scale).astype(BF16)

    raw4, raw5, raw6, raw7 = raws
    raw5_z, third = lax.optimization_barrier((raw5_z, third))
    turned = moved(raw5_z, -3, (3,))
    raw4, third = lax.optimization_barrier((raw4, third))
    third = moved(third, 3)
    raw5, second = lax.optimization_barrier((raw5, second))
    second = moved(second, 2)
    raw6, first = lax.optimization_barrier((raw6, first))
    first = moved(first, 1)
    raw7, *late = lax.optimization_barrier((raw7, *corr[4:]))
    corr[7] = moved(late[3], 7)
    raw4, raw5, raw6, raw7, raw5_z, *late = lax.optimization_barrier(
        (raw4, raw5, raw6, raw7, raw5_z, *late[:3])
    )
    corr[4:7] = [moved(array, k) for array, k in zip(late, (4, 5, 6))]
    sent = [corr[0], *corr[4:]]
    kept = place(count, width, third)
    kept = place(count, width, second, kept)
    kept = merge(count, table, flat, (raw4, raw5, raw6, raw7), turned, sent, kept)
    kept, kept_inner, kept_ssm = close(count, width, (first, second, third), sent, kept)
    return (hidden_out, kept.reshape(states_in.shape), kept_inner, kept_ssm)


def solution(mesh):
    in_specs = (
        P("req", "head"),
        P(),
        P(None, "head"),
        P(None, "head"),
        P(None, "head"),
        P(None, "head"),
        P("head"),
        P("head"),
        P("head"),
        P(None, "head"),
        P("head"),
        P(),
        P(),
        P("head"),
        P("head", None),
        P("req", "head", None, None),
        P("req", None, "head"),
        P("req", None, None),
        P("req"),
        P("req"),
        P("req"),
    )
    out_specs = (
        P("req", "head"),
        P("req", "head", None, None),
        P("req", None, "head"),
        P("req", None, None),
    )
    return jax.shard_map(local, mesh=mesh, in_specs=in_specs, out_specs=out_specs, check_vma=False)
```

```python
import functools

import jax
import jax.numpy as jnp
from jax import lax
from jax.experimental import pallas as pl
from jax.experimental.pallas import tpu as pltpu
from jax.sharding import PartitionSpec as P

HEAD_DIM = 64
NSTATE = 128
KCONV = 4
DRAFT = 8
WINDOW = 8
DINNER = 3072
TILE = 256
EXTRA = NSTATE
RAW = (7,)
PARTS = 3
SMALL = pl.CostEstimate(flops=1024, bytes_accessed=1024, transcendentals=0)
STEP = pl.CostEstimate(flops=1024, bytes_accessed=8_000_000, transcendentals=0)

epsilon = 1e-05
HIGH = lax.Precision.HIGHEST
F32 = jnp.float32
BF16 = jnp.bfloat16


def iota(shape, axis):
    return lax.broadcasted_iota(jnp.int32, shape, axis)


def mm(a, b, precision=None):
    return jnp.dot(a, b, preferred_element_type=F32, precision=precision)


def mm_t(a, b):
    return lax.dot_general(a, b, (((1,), (1,)), ((), ())), preferred_element_type=F32)


def silu(x):
    return x * (1.0 / (1.0 + jnp.exp(-x)))


def conv_rows(rows, edges, taps, bias):
    slot = iota(rows.shape, 1)
    total = bias + taps[KCONV - 1 : KCONV] * rows
    for back in range(1, KCONV):
        mixed = jnp.where(slot >= DRAFT - back, edges, rows)
        total = total + taps[KCONV - 1 - back : KCONV - back] * pltpu.roll(mixed, back, 1)
    return total


def front_kernel(
    count,
    heads,
    table,
    lengths_in,
    accepted_in,
    hidden,
    vectors,
    w_gate,
    w_inner,
    w_out,
    w_ssm,
    w_step,
    head_rows,
    taps_inner,
    vector_tile,
    taps_ssm,
    bias_ssm,
    states,
    edge_inner,
    edge_ssm,
    mine,
    theirs,
    *rest,
):
    corr = rest[:WINDOW]
    normed, acc, squares, quant, gmat, cmat, select, boxes, edge_pad = rest[WINDOW:]
    step = pl.program_id(0)
    last = pl.num_programs(0) - 1
    rows = count * DRAFT
    width = acc.shape[1]
    half = width // 2

    @pl.when(step == 0)
    def _():
        wide = jnp.concatenate([hidden[0], hidden[1]], axis=1).astype(F32)
        scale = lax.rsqrt(jnp.mean(wide * wide, axis=-1, keepdims=True) + epsilon)
        norm = (wide * scale * vectors[0:1]).astype(BF16)
        normed[...] = norm
        acc[...] = jnp.zeros_like(acc)
        squares[...] = jnp.zeros_like(squares)
        boxes[...] = jnp.zeros_like(boxes)
        edge_pad[...] = jnp.zeros_like(edge_pad)
        edge_pad[:, DRAFT - KCONV + 1 :] = edge_ssm[...].astype(F32)
        row = iota((rows, rows), 0)
        col = iota((rows, rows), 1)
        request = row >> 3
        taken = jnp.zeros((rows, rows), jnp.int32)
        for r in range(count):
            taken = jnp.where(request == r, accepted_in[r], taken)
        same = request == (col >> 3)
        lower = same & ((col & 7) <= (row & 7))
        before = same & ((col & 7) < taken)
        raw = mm_t(norm, w_step[...]).astype(BF16).astype(F32) + head_rows[0:1]
        lengths = jnp.zeros((rows, heads), jnp.int32)
        chosen = jnp.zeros((rows, heads), jnp.int32)
        hrow = iota((rows, heads), 0)
        for r in range(count):
            lengths = jnp.where((hrow >> 3) == r, lengths_in[r], lengths)
            chosen = jnp.where((hrow >> 3) == r, accepted_in[r], chosen)
        soft = jnp.maximum(raw, 0.0) + jnp.log1p(jnp.exp(-jnp.abs(raw)))
        size = jnp.where((hrow & 7) < lengths, soft, 0.0)
        rate = -jnp.exp(head_rows[1:2])
        cum = mm(lower.astype(F32), size, HIGH)
        upto = mm(before.astype(F32), size, HIGH)
        weight = jnp.where(
            (hrow & 7) < chosen, jnp.exp(jnp.minimum(rate * (upto - cum), 0.0)) * size, 0.0
        )
        stacked = jnp.concatenate(
            [
                rate * cum,
                size,
                weight,
                jnp.exp(rate * upto),
                jnp.broadcast_to(head_rows[2:3], (16, heads)),
            ],
            axis=0,
        )
        for part in range(3):
            piece = stacked.astype(BF16)
            quant[part] = piece
            stacked = stacked - piece.astype(F32)
        sel_rows = jnp.where(
            same & ((row & 7) < KCONV - 1),
            ((col & 7) == (row & 7) + taken - 3).astype(F32),
            0.0,
        ).astype(BF16)
        sel_edge = jnp.where(
            same & ((row & 7) < KCONV - 1),
            ((col & 7) == (row & 7) + taken + 5).astype(F32),
            0.0,
        ).astype(BF16)
        select[0] = sel_rows
        select[1] = sel_edge
        ssm = jnp.concatenate([mm(norm, w_ssm[0]), mm(norm, w_ssm[1])], axis=1).astype(BF16)
        before_ssm = edge_pad[...]
        conv = conv_rows(
            ssm.astype(F32).reshape(count, DRAFT, 2 * NSTATE),
            before_ssm,
            taps_ssm[...].astype(F32),
            bias_ssm[...],
        )
        both = silu(conv).reshape(rows, 2 * NSTATE).astype(BF16)
        bmat = both[:, :NSTATE]
        cvec = both[:, NSTATE:]
        cmat[...] = cvec.astype(F32)
        pair = jnp.where(lower, mm_t(cvec, bmat), 0.0)
        fold = ((iota((rows, NSTATE), 0) & 7) == iota((rows, NSTATE), 1)).astype(F32)
        gmat[...] = mm(pair, fold, HIGH)
        kept = mm(sel_rows, ssm) + mm(
            sel_edge, before_ssm.reshape(rows, 2 * NSTATE).astype(BF16)
        )
        wide_b = bmat.astype(F32)
        place = iota((DRAFT, NSTATE), 0)
        for r in range(count):
            own = kept[r * DRAFT : (r + 1) * DRAFT]
            packed = jnp.where(
                place < 3,
                own[:, :NSTATE],
                jnp.where(
                    place < 6,
                    pltpu.roll(own[:, NSTATE:], 3, 0),
                    jnp.full((DRAFT, NSTATE), (table[1, r] + 1).astype(F32)),
                ),
            )
            boxes[table[0, r], :, :NSTATE] = jnp.concatenate(
                [wide_b[r * DRAFT : (r + 1) * DRAFT], packed], axis=0
            ).astype(BF16)
        for k in range(WINDOW):
            corr[k][:, width:] = boxes[k, :, :NSTATE]

    norm = normed[...]
    inner = mm(norm, w_inner[...]).astype(BF16)
    gate = mm(norm, w_gate[...]).astype(BF16).astype(F32)
    edge_pad[:, DRAFT - KCONV + 1 :] = edge_inner[...].astype(F32)
    edges = edge_pad[...]
    conv = conv_rows(
        inner.astype(F32).reshape(count, DRAFT, TILE),
        edges,
        taps_inner[...].astype(F32),
        vector_tile[1:2],
    )
    x = silu(conv).reshape(rows, TILE).astype(BF16).astype(F32)
    first_head = step * (TILE // HEAD_DIM)
    spread = (
        iota((heads, TILE), 0) == first_head + (iota((heads, TILE), 1) >> 6)
    ).astype(BF16)
    expanded = mm(quant[0], spread) + mm(quant[1], spread) + mm(quant[2], spread)
    level = expanded[:rows]
    weighted = expanded[rows : 2 * rows] * x
    past = jnp.concatenate(
        [
            mm_t(cmat[r * DRAFT : (r + 1) * DRAFT].astype(BF16), states[r])
            for r in range(count)
        ],
        axis=0,
    )
    out = jnp.exp(level) * past + expanded[4 * rows : 4 * rows + 1] * x
    level3 = level.reshape(count, DRAFT, TILE)
    weighted3 = weighted.reshape(count, DRAFT, TILE)
    total = jnp.zeros((count, DRAFT, TILE), F32)
    for u in range(DRAFT):
        factor = jnp.exp(jnp.minimum(level3 - level3[:, u : u + 1], 0.0))
        share = gmat[:, u : u + 1].reshape(count, DRAFT, 1)
        total = total + share * factor * weighted3[:, u : u + 1]
    out = (out + total.reshape(rows, TILE)).astype(BF16).astype(F32)
    gated = out * silu(gate)
    squared = gated * gated
    squares[...] += squared[:, :128] + squared[:, 128:]
    acc[...] += mm((gated * vector_tile[2:3]).astype(BF16), w_out[...])
    delta = expanded[2 * rows : 3 * rows] * x
    decay = expanded[3 * rows : 4 * rows]
    decay_hi = decay.astype(BF16).astype(F32)
    second = mm(select[0], inner) + mm(select[1], edges.reshape(rows, TILE).astype(BF16))
    place = iota((rows, TILE), 0) & 7
    second = jnp.where(
        place == 3, decay_hi, jnp.where(place == 4, decay - decay_hi, second)
    )
    for r in range(count):
        span = slice(r * DRAFT, (r + 1) * DRAFT)
        boxes[table[0, r]] = jnp.concatenate([delta[span], second[span]], axis=0).astype(BF16)
    here = pl.ds(pl.multiple_of(step * TILE, TILE), TILE)
    for k in range(WINDOW):
        corr[k][:, here] = boxes[k]

    @pl.when(step == last)
    def _():
        total_square = jnp.broadcast_to(
            jnp.sum(squares[...], axis=1, keepdims=True), squares.shape
        )
        mine[:, half:] = total_square
        theirs[:, half:] = total_square

        @pl.when(table[2, 0] == 0)
        def _():
            mine[:, :half] = acc[:, :half]
            theirs[:, :half] = acc[:, half:]

        @pl.when(table[2, 0] != 0)
        def _():
            mine[:, :half] = acc[:, half:]
            theirs[:, :half] = acc[:, :half]


def front(count, heads, width, depth, args):
    rows = count * DRAFT
    tiles = width // TILE

    def whole(shape):
        return pl.BlockSpec(shape, lambda j: (0,) * len(shape))

    in_specs = [
        *[pl.BlockSpec(memory_space=pltpu.SMEM)] * 3,
        whole((2, rows, depth // 2)),
        whole((3, depth)),
        pl.BlockSpec((depth, TILE), lambda j: (0, j)),
        pl.BlockSpec((depth, TILE), lambda j: (0, j)),
        pl.BlockSpec((TILE, depth), lambda j: (j, 0)),
        whole((2, depth, NSTATE)),
        whole((heads, depth)),
        whole((3, heads)),
        pl.BlockSpec((KCONV, TILE), lambda j: (0, j)),
        pl.BlockSpec((3, TILE), lambda j: (0, j)),
        whole((KCONV, 2 * NSTATE)),
        whole((1, 2 * NSTATE)),
        pl.BlockSpec((count, TILE, NSTATE), lambda j: (0, j, 0)),
        pl.BlockSpec((count, KCONV - 1, TILE), lambda j: (0, 0, j)),
        whole((count, KCONV - 1, 2 * NSTATE)),
    ]
    out_width = depth // 2 + 128
    out_shape = [jax.ShapeDtypeStruct((rows, out_width), F32)] * 2 + [
        jax.ShapeDtypeStruct((2 * DRAFT, width + EXTRA), BF16)
    ] * WINDOW
    out_specs = [whole((rows, out_width))] * 2 + [whole((2 * DRAFT, width + EXTRA))] * WINDOW
    return pl.pallas_call(
        functools.partial(front_kernel, count, heads),
        grid=(tiles,),
        in_specs=in_specs,
        out_specs=out_specs,
        out_shape=out_shape,
        scratch_shapes=[
            pltpu.VMEM((rows, depth), BF16),
            pltpu.VMEM((rows, depth), F32),
            pltpu.VMEM((rows, 128), F32),
            pltpu.VMEM((3, 4 * rows + 16, heads), BF16),
            pltpu.VMEM((rows, NSTATE), F32),
            pltpu.VMEM((rows, NSTATE), F32),
            pltpu.VMEM((2, rows, rows), BF16),
            pltpu.VMEM((WINDOW, 2 * DRAFT, TILE), BF16),
            pltpu.VMEM((count, DRAFT, TILE), F32),
        ],
        compiler_params=pltpu.CompilerParams(dimension_semantics=("arbitrary",)),
        cost_estimate=SMALL,
        name="front",
    )(*args)


def pick_kernel(count, peers, destination, states, *outs):
    picked = outs[: len(RAW)]
    table, sems = outs[len(RAW) :]
    here = lax.axis_index("req")
    reach = [
        lax.rem(lax.div(destination[r], count) - here + peers, peers) for r in range(count)
    ]
    index = []
    for k in range(WINDOW):
        index.append(sum((reach[r] == k).astype(jnp.int32) * r for r in range(count)))
        table[3, k] = index[k]
    copies = []
    for n, k in enumerate(RAW):
        copy = pltpu.make_async_copy(states.at[index[k]], picked[n], sems.at[n])
        copy.start()
        copies.append(copy)
    for r in range(count):
        table[0, r] = reach[r]
        table[1, r] = lax.rem(destination[r], count)
        table[2, r] = lax.axis_index("head")
    for copy in copies:
        copy.wait()


def in_hbm():
    return pl.BlockSpec(memory_space=pl.ANY)


def in_vmem():
    return pl.BlockSpec(memory_space=pltpu.VMEM)


def in_smem():
    return pl.BlockSpec(memory_space=pltpu.SMEM)


def pick(count, width, peers, destination, states):
    return pl.pallas_call(
        functools.partial(pick_kernel, count, peers),
        in_specs=[in_smem(), in_hbm()],
        out_specs=[in_vmem()] * len(RAW) + [in_smem()],
        out_shape=[jax.ShapeDtypeStruct((width, NSTATE), BF16)] * len(RAW)
        + [jax.ShapeDtypeStruct((4, max(count, WINDOW)), jnp.int32)],
        scratch_shapes=[pltpu.SemaphoreType.DMA((len(RAW),))],
        cost_estimate=SMALL,
        name="pick",
    )(destination, states)


def advance(corr, state, out):
    width = state.shape[0]
    line = iota((2 * DRAFT, NSTATE), 0)
    bmat = jnp.where(line < DRAFT, corr[:, width:].astype(F32), 0.0)
    ones = jnp.where((line == 11) | (line == 12), 1.0, 0.0)
    right = jnp.concatenate([bmat, ones], axis=1).astype(BF16)
    part = width // PARTS
    for c in range(PARTS):
        span = slice(c * part, (c + 1) * part)
        both = lax.dot_general(
            corr[:, span], right, (((0,), (0,)), ((), ())), preferred_element_type=F32
        )
        out[span] = (both[:, NSTATE:] * state[span].astype(F32) + both[:, :NSTATE]).astype(BF16)


def tail_rows(width):
    pairs = (width // NSTATE + 2) // 2
    return pairs, pairs * 2 * DRAFT


def finish_kernel(offsets, *refs):
    n = len(offsets)
    table, states = refs[:2]
    corr = refs[2 : 2 + n]
    outs = refs[2 + n : 2 + 2 * n]
    loaded, sems = refs[-2:]
    width = loaded.shape[1]
    pairs, _ = tail_rows(width)
    copies = []
    for i, k in enumerate(offsets):
        copy = pltpu.make_async_copy(states.at[table[3, k]], loaded.at[i], sems.at[i])
        copy.start()
        copies.append(copy)
    for i in range(n):
        low = corr[i][...].astype(F32)[DRAFT:]
        low = jnp.concatenate(
            [low, jnp.zeros((DRAFT, 2 * pairs * NSTATE - low.shape[1]), F32)], axis=1
        )
        for t in range(pairs):
            block = jnp.concatenate(
                [
                    low[:, t * NSTATE : (t + 1) * NSTATE],
                    low[:, (t + pairs) * NSTATE : (t + pairs + 1) * NSTATE],
                ],
                axis=0,
            )
            outs[i][width + t * 2 * DRAFT : width + (t + 1) * 2 * DRAFT] = block.astype(BF16)
        copies[i].wait()
        advance(corr[i], loaded.at[i], outs[i])


def finish(offsets, table, states, corr):
    n = len(offsets)
    width = states.shape[1]
    shape = jax.ShapeDtypeStruct((width + tail_rows(width)[1], NSTATE), BF16)
    return pl.pallas_call(
        functools.partial(finish_kernel, offsets),
        in_specs=[in_smem(), in_hbm()] + [in_vmem()] * n,
        out_specs=[in_vmem()] * n,
        out_shape=[shape] * n,
        scratch_shapes=[
            pltpu.VMEM((n, width, NSTATE), BF16),
            pltpu.SemaphoreType.DMA((n,)),
        ],
        cost_estimate=SMALL,
        name="finish",
    )(table, states, *[corr[k] for k in offsets])


def mark_of(low):
    return jnp.max(low[6:7]).astype(jnp.int32) - 1


def merge_kernel(table, states, *refs):
    n = 1 + len(RAW)
    raws = refs[: n - 1]
    corr = refs[n - 1 : 2 * n - 1]
    _, kept, loaded, merged, sem_in, sem_out = refs[2 * n - 1 :]
    width = loaded.shape[0]
    own = pltpu.make_async_copy(states.at[table[3, 0]], loaded, sem_in)
    own.start()
    slots = [mark_of(ref[:, width:].astype(F32)[DRAFT:]) for ref in corr]

    def put(i):
        return pltpu.make_async_copy(merged.at[i], kept.at[slots[i]], sem_out.at[i])

    for i in range(n):
        if i == 0:
            own.wait()

        @pl.when(slots[i] >= 0)
        def _(i=i):
            advance(corr[i], raws[i - 1] if i > 0 else loaded, merged.at[i])
            put(i).start()

    for i in range(n):

        @pl.when(slots[i] >= 0)
        def _(i=i):
            put(i).wait()


def merge(count, table, states, raws, corr, kept):
    width = states.shape[1]
    n = 1 + len(RAW)
    return pl.pallas_call(
        merge_kernel,
        in_specs=[in_smem(), in_hbm()] + [in_vmem()] * (2 * n - 1) + [in_hbm()],
        out_specs=in_hbm(),
        out_shape=jax.ShapeDtypeStruct((count, width, NSTATE), BF16),
        scratch_shapes=[
            pltpu.VMEM((width, NSTATE), BF16),
            pltpu.VMEM((n, width, NSTATE), BF16),
            pltpu.SemaphoreType.DMA,
            pltpu.SemaphoreType.DMA((n,)),
        ],
        input_output_aliases={1 + 2 * n: 0},
        cost_estimate=SMALL,
        name="merge",
    )(table, states, *raws, *corr, kept)


def halves(ref, width):
    parts = [
        ref[row : row + 2 * DRAFT].astype(F32)
        for row in range(width, ref.shape[0], 2 * DRAFT)
    ]
    return [part[:DRAFT] for part in parts] + [part[DRAFT:] for part in parts]


def place_kernel(width, message, *refs):
    kept, sem = refs[-2:]
    slot = mark_of(halves(message, width)[width // NSTATE])

    @pl.when(slot >= 0)
    def _():
        copy = pltpu.make_async_copy(message.at[pl.ds(0, width)], kept.at[slot], sem)
        copy.start()
        copy.wait()


def place(count, width, message, kept=None):
    return pl.pallas_call(
        functools.partial(place_kernel, width),
        in_specs=[in_vmem()] + ([] if kept is None else [in_hbm()]),
        out_specs=in_hbm(),
        out_shape=jax.ShapeDtypeStruct((count, width, NSTATE), BF16),
        input_output_aliases={} if kept is None else {1: 0},
        scratch_shapes=[pltpu.SemaphoreType.DMA],
        cost_estimate=STEP,
        name="place",
    )(message, *([] if kept is None else [kept]))


def close_kernel(n, *refs):
    messages = refs[:n]
    corr = refs[n : n + 1 + len(RAW)]
    _, kept, out_inner, out_ssm, sem = refs[n + 1 + len(RAW) :]
    width = out_inner.shape[2]
    tiles = width // NSTATE
    marks = []
    for ref in messages:
        lows = halves(ref, width)
        marks.append((mark_of(lows[tiles]), lows))
    last = marks[0][0]

    def put():
        return pltpu.make_async_copy(messages[0].at[pl.ds(0, width)], kept.at[last], sem)

    @pl.when(last >= 0)
    def _():
        put().start()

    def write_edges(slot, inner, low):
        out_inner[slot] = inner[: KCONV - 1].astype(BF16)
        high = pltpu.roll(low, DRAFT - 3, 0)
        out_ssm[slot] = jnp.concatenate([low[:3], high[:3]], axis=1).astype(BF16)

    for ref in corr:
        low = ref[...].astype(F32)[DRAFT:]
        slot = mark_of(low[:, width:])

        @pl.when(slot >= 0)
        def _(slot=slot, low=low):
            write_edges(slot, low[:, :width], low[:, width:])

    for slot, lows in marks:

        @pl.when(slot >= 0)
        def _(slot=slot, lows=lows):
            write_edges(slot, jnp.concatenate(lows[:tiles], axis=1), lows[tiles])

    @pl.when(last >= 0)
    def _():
        put().wait()


def close(count, width, messages, corr, kept):
    n = len(messages)
    return pl.pallas_call(
        functools.partial(close_kernel, n),
        in_specs=[in_vmem()] * (n + len(corr)) + [in_hbm()],
        out_specs=[in_hbm(), in_vmem(), in_vmem()],
        out_shape=[
            jax.ShapeDtypeStruct((count, width, NSTATE), BF16),
            jax.ShapeDtypeStruct((count, KCONV - 1, width), BF16),
            jax.ShapeDtypeStruct((count, KCONV - 1, 2 * NSTATE), BF16),
        ],
        input_output_aliases={n + len(corr): 0},
        scratch_shapes=[pltpu.SemaphoreType.DMA],
        cost_estimate=SMALL,
        name="close",
    )(*messages, *corr, kept)


def moved(array, by):
    length = lax.axis_size("req")
    return lax.ppermute(array, "req", [(i, (i + by) % length) for i in range(length)])


def local(
    hidden_in,
    norm_gain,
    proj_gate,
    proj_inner,
    proj_ssm,
    proj_step,
    step_bias,
    decay_log,
    skip_gain,
    conv_inner,
    conv_inner_bias,
    conv_ssm,
    conv_ssm_bias,
    gate_gain,
    proj_out,
    states_in,
    edge_inner,
    edge_ssm,
    draft_lengths,
    accepted,
    destination,
):
    count, heads = states_in.shape[:2]
    depth, width = proj_inner.shape
    peers = lax.axis_size("req")
    flat = states_in.reshape(count, width, NSTATE)
    *raws, table = pick(count, width, peers, destination, flat)
    raws = [moved(raw, k) for raw, k in zip(raws, RAW)]
    table, ready, ready_ssm = lax.optimization_barrier((table, hidden_in, proj_ssm))
    vectors = jnp.stack([norm_gain, conv_inner_bias, gate_gain])
    results = front(
        count,
        heads,
        width,
        depth,
        (
            table,
            draft_lengths,
            accepted,
            lax.all_gather(ready, "head", axis=0, tiled=False),
            vectors,
            proj_gate,
            proj_inner,
            proj_out,
            lax.all_gather(ready_ssm, "head", axis=0, tiled=False),
            proj_step.T,
            jnp.stack([step_bias, decay_log, skip_gain]),
            conv_inner,
            vectors,
            conv_ssm,
            conv_ssm_bias.reshape(1, 2 * NSTATE),
            flat,
            edge_inner,
            edge_ssm,
        ),
    )
    mine, theirs = results[:2]
    corr = list(results[2:])
    sixth, fifth, fourth, third = finish((6, 5, 4, 3), table, flat, corr)
    raw7, corr[7], sixth, fifth, fourth, third, later = lax.optimization_barrier(
        (raws[0], corr[7], sixth, fifth, fourth, third, table)
    )
    sixth = moved(sixth, 6)
    fifth = moved(fifth, 5)
    fourth = moved(fourth, 4)
    third = moved(third, 3)
    corr[7] = moved(corr[7], 7)
    second, first = finish((2, 1), later, flat, corr)

    pair = lax.all_gather(theirs, "head", axis=0, tiled=False)
    other = jnp.where(lax.axis_index("head") == 0, pair[1], pair[0])
    total = mine + other
    half = depth // 2
    scale = lax.rsqrt(total[:, half : half + 1] / DINNER + epsilon)
    hidden_out = (hidden_in.astype(F32) + total[:, :half] * scale).astype(BF16)

    sixth, fourth, corr[7], second = lax.optimization_barrier(
        (sixth, fourth, corr[7], second)
    )
    second = moved(second, 2)
    fifth, third, first = lax.optimization_barrier((fifth, third, first))
    first = moved(first, 1)
    sent = [corr[0], corr[7]]
    kept = place(count, width, sixth)
    kept = place(count, width, fourth, kept)
    kept = merge(count, table, flat, [raw7], sent, kept)
    kept = place(count, width, fifth, kept)
    kept = place(count, width, third, kept)
    kept = place(count, width, second, kept)
    kept, kept_inner, kept_ssm = close(
        count, width, (first, second, third, fourth, fifth, sixth), sent, kept
    )
    return (hidden_out, kept.reshape(states_in.shape), kept_inner, kept_ssm)


def solution(mesh):
    in_specs = (
        P("req", "head"),
        P(),
        P(None, "head"),
        P(None, "head"),
        P(None, "head"),
        P(None, "head"),
        P("head"),
        P("head"),
        P("head"),
        P(None, "head"),
        P("head"),
        P(),
        P(),
        P("head"),
        P("head", None),
        P("req", "head", None, None),
        P("req", None, "head"),
        P("req", None, None),
        P("req"),
        P("req"),
        P("req"),
    )
    out_specs = (
        P("req", "head"),
        P("req", "head", None, None),
        P("req", None, "head"),
        P("req", None, None),
    )
    return jax.shard_map(local, mesh=mesh, in_specs=in_specs, out_specs=out_specs, check_vma=False)
```

```python
import functools

import jax
import jax.numpy as jnp
from jax import lax
from jax.experimental import pallas as pl
from jax.experimental.pallas import tpu as pltpu
from jax.sharding import PartitionSpec as P

HEAD_DIM = 64
NSTATE = 128
KCONV = 4
DRAFT = 8
WINDOW = 8
DINNER = 3072
TILE = 256
EXTRA = NSTATE
RAW = (6, 7)
PARTS = 3
SMALL = pl.CostEstimate(flops=1024, bytes_accessed=1024, transcendentals=0)
STEP = pl.CostEstimate(flops=1024, bytes_accessed=8_000_000, transcendentals=0)

epsilon = 1e-05
HIGH = lax.Precision.HIGHEST
F32 = jnp.float32
BF16 = jnp.bfloat16


def iota(shape, axis):
    return lax.broadcasted_iota(jnp.int32, shape, axis)


def mm(a, b, precision=None):
    return jnp.dot(a, b, preferred_element_type=F32, precision=precision)


def mm_t(a, b):
    return lax.dot_general(a, b, (((1,), (1,)), ((), ())), preferred_element_type=F32)


def silu(x):
    return x * (1.0 / (1.0 + jnp.exp(-x)))


def conv_rows(rows, edges, taps, bias):
    slot = iota(rows.shape, 1)
    total = bias + taps[KCONV - 1 : KCONV] * rows
    for back in range(1, KCONV):
        mixed = jnp.where(slot >= DRAFT - back, edges, rows)
        total = total + taps[KCONV - 1 - back : KCONV - back] * pltpu.roll(mixed, back, 1)
    return total


def front_kernel(
    count,
    heads,
    table,
    lengths_in,
    accepted_in,
    hidden,
    vectors,
    w_gate,
    w_inner,
    w_out,
    w_ssm,
    w_step,
    head_rows,
    taps_inner,
    vector_tile,
    taps_ssm,
    bias_ssm,
    states,
    edge_inner,
    edge_ssm,
    mine,
    theirs,
    *rest,
):
    corr = rest[:WINDOW]
    normed, acc, squares, quant, gmat, cmat, select, boxes, edge_pad = rest[WINDOW:]
    step = pl.program_id(0)
    last = pl.num_programs(0) - 1
    rows = count * DRAFT
    width = acc.shape[1]
    half = width // 2

    @pl.when(step == 0)
    def _():
        wide = jnp.concatenate([hidden[0], hidden[1]], axis=1).astype(F32)
        scale = lax.rsqrt(jnp.mean(wide * wide, axis=-1, keepdims=True) + epsilon)
        norm = (wide * scale * vectors[0:1]).astype(BF16)
        normed[...] = norm
        acc[...] = jnp.zeros_like(acc)
        squares[...] = jnp.zeros_like(squares)
        boxes[...] = jnp.zeros_like(boxes)
        edge_pad[...] = jnp.zeros_like(edge_pad)
        edge_pad[:, DRAFT - KCONV + 1 :] = edge_ssm[...].astype(F32)
        row = iota((rows, rows), 0)
        col = iota((rows, rows), 1)
        request = row >> 3
        taken = jnp.zeros((rows, rows), jnp.int32)
        for r in range(count):
            taken = jnp.where(request == r, accepted_in[r], taken)
        same = request == (col >> 3)
        lower = same & ((col & 7) <= (row & 7))
        before = same & ((col & 7) < taken)
        raw = mm_t(norm, w_step[...]).astype(BF16).astype(F32) + head_rows[0:1]
        lengths = jnp.zeros((rows, heads), jnp.int32)
        chosen = jnp.zeros((rows, heads), jnp.int32)
        hrow = iota((rows, heads), 0)
        for r in range(count):
            lengths = jnp.where((hrow >> 3) == r, lengths_in[r], lengths)
            chosen = jnp.where((hrow >> 3) == r, accepted_in[r], chosen)
        soft = jnp.maximum(raw, 0.0) + jnp.log1p(jnp.exp(-jnp.abs(raw)))
        size = jnp.where((hrow & 7) < lengths, soft, 0.0)
        rate = -jnp.exp(head_rows[1:2])
        cum = mm(lower.astype(F32), size, HIGH)
        upto = mm(before.astype(F32), size, HIGH)
        weight = jnp.where(
            (hrow & 7) < chosen, jnp.exp(jnp.minimum(rate * (upto - cum), 0.0)) * size, 0.0
        )
        stacked = jnp.concatenate(
            [
                rate * cum,
                size,
                weight,
                jnp.exp(rate * upto),
                jnp.broadcast_to(head_rows[2:3], (16, heads)),
            ],
            axis=0,
        )
        for part in range(3):
            piece = stacked.astype(BF16)
            quant[part] = piece
            stacked = stacked - piece.astype(F32)
        sel_rows = jnp.where(
            same & ((row & 7) < KCONV - 1),
            ((col & 7) == (row & 7) + taken - 3).astype(F32),
            0.0,
        ).astype(BF16)
        sel_edge = jnp.where(
            same & ((row & 7) < KCONV - 1),
            ((col & 7) == (row & 7) + taken + 5).astype(F32),
            0.0,
        ).astype(BF16)
        select[0] = sel_rows
        select[1] = sel_edge
        ssm = jnp.concatenate([mm(norm, w_ssm[0]), mm(norm, w_ssm[1])], axis=1).astype(BF16)
        before_ssm = edge_pad[...]
        conv = conv_rows(
            ssm.astype(F32).reshape(count, DRAFT, 2 * NSTATE),
            before_ssm,
            taps_ssm[...].astype(F32),
            bias_ssm[...],
        )
        both = silu(conv).reshape(rows, 2 * NSTATE).astype(BF16)
        bmat = both[:, :NSTATE]
        cvec = both[:, NSTATE:]
        cmat[...] = cvec.astype(F32)
        pair = jnp.where(lower, mm_t(cvec, bmat), 0.0)
        fold = ((iota((rows, NSTATE), 0) & 7) == iota((rows, NSTATE), 1)).astype(F32)
        gmat[...] = mm(pair, fold, HIGH)
        kept = mm(sel_rows, ssm) + mm(
            sel_edge, before_ssm.reshape(rows, 2 * NSTATE).astype(BF16)
        )
        wide_b = bmat.astype(F32)
        place = iota((DRAFT, NSTATE), 0)
        for r in range(count):
            own = kept[r * DRAFT : (r + 1) * DRAFT]
            packed = jnp.where(
                place < 3,
                own[:, :NSTATE],
                jnp.where(
                    place < 6,
                    pltpu.roll(own[:, NSTATE:], 3, 0),
                    jnp.full((DRAFT, NSTATE), (table[1, r] + 1).astype(F32)),
                ),
            )
            boxes[table[0, r], :, :NSTATE] = jnp.concatenate(
                [wide_b[r * DRAFT : (r + 1) * DRAFT], packed], axis=0
            ).astype(BF16)
        for k in range(WINDOW):
            corr[k][:, width:] = boxes[k, :, :NSTATE]

    norm = normed[...]
    inner = mm(norm, w_inner[...]).astype(BF16)
    gate = mm(norm, w_gate[...]).astype(BF16).astype(F32)
    edge_pad[:, DRAFT - KCONV + 1 :] = edge_inner[...].astype(F32)
    edges = edge_pad[...]
    conv = conv_rows(
        inner.astype(F32).reshape(count, DRAFT, TILE),
        edges,
        taps_inner[...].astype(F32),
        vector_tile[1:2],
    )
    x = silu(conv).reshape(rows, TILE).astype(BF16).astype(F32)
    first_head = step * (TILE // HEAD_DIM)
    spread = (
        iota((heads, TILE), 0) == first_head + (iota((heads, TILE), 1) >> 6)
    ).astype(BF16)
    expanded = mm(quant[0], spread) + mm(quant[1], spread) + mm(quant[2], spread)
    level = expanded[:rows]
    weighted = expanded[rows : 2 * rows] * x
    past = jnp.concatenate(
        [
            mm_t(cmat[r * DRAFT : (r + 1) * DRAFT].astype(BF16), states[r])
            for r in range(count)
        ],
        axis=0,
    )
    out = jnp.exp(level) * past + expanded[4 * rows : 4 * rows + 1] * x
    level3 = level.reshape(count, DRAFT, TILE)
    weighted3 = weighted.reshape(count, DRAFT, TILE)
    total = jnp.zeros((count, DRAFT, TILE), F32)
    for u in range(DRAFT):
        factor = jnp.exp(jnp.minimum(level3 - level3[:, u : u + 1], 0.0))
        share = gmat[:, u : u + 1].reshape(count, DRAFT, 1)
        total = total + share * factor * weighted3[:, u : u + 1]
    out = (out + total.reshape(rows, TILE)).astype(BF16).astype(F32)
    gated = out * silu(gate)
    squared = gated * gated
    squares[...] += squared[:, :128] + squared[:, 128:]
    acc[...] += mm((gated * vector_tile[2:3]).astype(BF16), w_out[...])
    delta = expanded[2 * rows : 3 * rows] * x
    decay = expanded[3 * rows : 4 * rows]
    decay_hi = decay.astype(BF16).astype(F32)
    second = mm(select[0], inner) + mm(select[1], edges.reshape(rows, TILE).astype(BF16))
    place = iota((rows, TILE), 0) & 7
    second = jnp.where(
        place == 3, decay_hi, jnp.where(place == 4, decay - decay_hi, second)
    )
    for r in range(count):
        span = slice(r * DRAFT, (r + 1) * DRAFT)
        boxes[table[0, r]] = jnp.concatenate([delta[span], second[span]], axis=0).astype(BF16)
    here = pl.ds(pl.multiple_of(step * TILE, TILE), TILE)
    for k in range(WINDOW):
        corr[k][:, here] = boxes[k]

    @pl.when(step == last)
    def _():
        total_square = jnp.broadcast_to(
            jnp.sum(squares[...], axis=1, keepdims=True), squares.shape
        )
        mine[:, half:] = total_square
        theirs[:, half:] = total_square

        @pl.when(table[2, 0] == 0)
        def _():
            mine[:, :half] = acc[:, :half]
            theirs[:, :half] = acc[:, half:]

        @pl.when(table[2, 0] != 0)
        def _():
            mine[:, :half] = acc[:, half:]
            theirs[:, :half] = acc[:, :half]


def front(count, heads, width, depth, args):
    rows = count * DRAFT
    tiles = width // TILE

    def whole(shape):
        return pl.BlockSpec(shape, lambda j: (0,) * len(shape))

    in_specs = [
        *[pl.BlockSpec(memory_space=pltpu.SMEM)] * 3,
        whole((2, rows, depth // 2)),
        whole((3, depth)),
        pl.BlockSpec((depth, TILE), lambda j: (0, j)),
        pl.BlockSpec((depth, TILE), lambda j: (0, j)),
        pl.BlockSpec((TILE, depth), lambda j: (j, 0)),
        whole((2, depth, NSTATE)),
        whole((heads, depth)),
        whole((3, heads)),
        pl.BlockSpec((KCONV, TILE), lambda j: (0, j)),
        pl.BlockSpec((3, TILE), lambda j: (0, j)),
        whole((KCONV, 2 * NSTATE)),
        whole((1, 2 * NSTATE)),
        pl.BlockSpec((count, TILE, NSTATE), lambda j: (0, j, 0)),
        pl.BlockSpec((count, KCONV - 1, TILE), lambda j: (0, 0, j)),
        whole((count, KCONV - 1, 2 * NSTATE)),
    ]
    out_width = depth // 2 + 128
    out_shape = [jax.ShapeDtypeStruct((rows, out_width), F32)] * 2 + [
        jax.ShapeDtypeStruct((2 * DRAFT, width + EXTRA), BF16)
    ] * WINDOW
    out_specs = [whole((rows, out_width))] * 2 + [whole((2 * DRAFT, width + EXTRA))] * WINDOW
    return pl.pallas_call(
        functools.partial(front_kernel, count, heads),
        grid=(tiles,),
        in_specs=in_specs,
        out_specs=out_specs,
        out_shape=out_shape,
        scratch_shapes=[
            pltpu.VMEM((rows, depth), BF16),
            pltpu.VMEM((rows, depth), F32),
            pltpu.VMEM((rows, 128), F32),
            pltpu.VMEM((3, 4 * rows + 16, heads), BF16),
            pltpu.VMEM((rows, NSTATE), F32),
            pltpu.VMEM((rows, NSTATE), F32),
            pltpu.VMEM((2, rows, rows), BF16),
            pltpu.VMEM((WINDOW, 2 * DRAFT, TILE), BF16),
            pltpu.VMEM((count, DRAFT, TILE), F32),
        ],
        compiler_params=pltpu.CompilerParams(dimension_semantics=("arbitrary",)),
        cost_estimate=SMALL,
        name="front",
    )(*args)


def pick_kernel(count, peers, destination, states, *outs):
    picked = outs[: len(RAW)]
    table, sems = outs[len(RAW) :]
    here = lax.axis_index("req")
    reach = [
        lax.rem(lax.div(destination[r], count) - here + peers, peers) for r in range(count)
    ]
    index = []
    for k in range(WINDOW):
        index.append(sum((reach[r] == k).astype(jnp.int32) * r for r in range(count)))
        table[3, k] = index[k]
    copies = []
    for n, k in enumerate(RAW):
        copy = pltpu.make_async_copy(states.at[index[k]], picked[n], sems.at[n])
        copy.start()
        copies.append(copy)
    for r in range(count):
        table[0, r] = reach[r]
        table[1, r] = lax.rem(destination[r], count)
        table[2, r] = lax.axis_index("head")
    for copy in copies:
        copy.wait()


def in_hbm():
    return pl.BlockSpec(memory_space=pl.ANY)


def in_vmem():
    return pl.BlockSpec(memory_space=pltpu.VMEM)


def in_smem():
    return pl.BlockSpec(memory_space=pltpu.SMEM)


def pick(count, width, peers, destination, states):
    return pl.pallas_call(
        functools.partial(pick_kernel, count, peers),
        in_specs=[in_smem(), in_hbm()],
        out_specs=[in_vmem()] * len(RAW) + [in_smem()],
        out_shape=[jax.ShapeDtypeStruct((width, NSTATE), BF16)] * len(RAW)
        + [jax.ShapeDtypeStruct((4, max(count, WINDOW)), jnp.int32)],
        scratch_shapes=[pltpu.SemaphoreType.DMA((len(RAW),))],
        cost_estimate=SMALL,
        name="pick",
    )(destination, states)


def advance(corr, state, out):
    width = state.shape[0]
    line = iota((2 * DRAFT, NSTATE), 0)
    bmat = jnp.where(line < DRAFT, corr[:, width:].astype(F32), 0.0)
    ones = jnp.where((line == 11) | (line == 12), 1.0, 0.0)
    right = jnp.concatenate([bmat, ones], axis=1).astype(BF16)
    part = width // PARTS
    for c in range(PARTS):
        span = slice(c * part, (c + 1) * part)
        both = lax.dot_general(
            corr[:, span], right, (((0,), (0,)), ((), ())), preferred_element_type=F32
        )
        out[span] = (both[:, NSTATE:] * state[span].astype(F32) + both[:, :NSTATE]).astype(BF16)


def tail_rows(width):
    pairs = (width // NSTATE + 2) // 2
    return pairs, pairs * 2 * DRAFT


def finish_kernel(offsets, *refs):
    n = len(offsets)
    table, states = refs[:2]
    corr = refs[2 : 2 + n]
    outs = refs[2 + n : 2 + 2 * n]
    loaded, sems = refs[-2:]
    width = loaded.shape[1]
    pairs, _ = tail_rows(width)
    copies = []
    for i, k in enumerate(offsets):
        copy = pltpu.make_async_copy(states.at[table[3, k]], loaded.at[i], sems.at[i])
        copy.start()
        copies.append(copy)
    for i in range(n):
        low = corr[i][...].astype(F32)[DRAFT:]
        low = jnp.concatenate(
            [low, jnp.zeros((DRAFT, 2 * pairs * NSTATE - low.shape[1]), F32)], axis=1
        )
        for t in range(pairs):
            block = jnp.concatenate(
                [
                    low[:, t * NSTATE : (t + 1) * NSTATE],
                    low[:, (t + pairs) * NSTATE : (t + pairs + 1) * NSTATE],
                ],
                axis=0,
            )
            outs[i][width + t * 2 * DRAFT : width + (t + 1) * 2 * DRAFT] = block.astype(BF16)
        copies[i].wait()
        advance(corr[i], loaded.at[i], outs[i])


def finish(offsets, table, states, corr):
    n = len(offsets)
    width = states.shape[1]
    shape = jax.ShapeDtypeStruct((width + tail_rows(width)[1], NSTATE), BF16)
    return pl.pallas_call(
        functools.partial(finish_kernel, offsets),
        in_specs=[in_smem(), in_hbm()] + [in_vmem()] * n,
        out_specs=[in_vmem()] * n,
        out_shape=[shape] * n,
        scratch_shapes=[
            pltpu.VMEM((n, width, NSTATE), BF16),
            pltpu.SemaphoreType.DMA((n,)),
        ],
        cost_estimate=SMALL,
        name="finish",
    )(table, states, *[corr[k] for k in offsets])


def mark_of(low):
    return jnp.max(low[6:7]).astype(jnp.int32) - 1


def merge_kernel(table, states, *refs):
    n = 1 + len(RAW)
    raws = refs[: n - 1]
    corr = refs[n - 1 : 2 * n - 1]
    _, kept, loaded, merged, sem_in, sem_out = refs[2 * n - 1 :]
    width = loaded.shape[0]
    own = pltpu.make_async_copy(states.at[table[3, 0]], loaded, sem_in)
    own.start()
    slots = [mark_of(ref[:, width:].astype(F32)[DRAFT:]) for ref in corr]

    def put(i):
        return pltpu.make_async_copy(merged.at[i], kept.at[slots[i]], sem_out.at[i])

    for i in range(n):
        if i == 0:
            own.wait()

        @pl.when(slots[i] >= 0)
        def _(i=i):
            advance(corr[i], raws[i - 1] if i > 0 else loaded, merged.at[i])
            put(i).start()

    for i in range(n):

        @pl.when(slots[i] >= 0)
        def _(i=i):
            put(i).wait()


def merge(count, table, states, raws, corr, kept):
    width = states.shape[1]
    n = 1 + len(RAW)
    return pl.pallas_call(
        merge_kernel,
        in_specs=[in_smem(), in_hbm()] + [in_vmem()] * (2 * n - 1) + [in_hbm()],
        out_specs=in_hbm(),
        out_shape=jax.ShapeDtypeStruct((count, width, NSTATE), BF16),
        scratch_shapes=[
            pltpu.VMEM((width, NSTATE), BF16),
            pltpu.VMEM((n, width, NSTATE), BF16),
            pltpu.SemaphoreType.DMA,
            pltpu.SemaphoreType.DMA((n,)),
        ],
        input_output_aliases={1 + 2 * n: 0},
        cost_estimate=SMALL,
        name="merge",
    )(table, states, *raws, *corr, kept)


def halves(ref, width):
    parts = [
        ref[row : row + 2 * DRAFT].astype(F32)
        for row in range(width, ref.shape[0], 2 * DRAFT)
    ]
    return [part[:DRAFT] for part in parts] + [part[DRAFT:] for part in parts]


def place_kernel(width, message, *refs):
    kept, sem = refs[-2:]
    slot = mark_of(halves(message, width)[width // NSTATE])

    @pl.when(slot >= 0)
    def _():
        copy = pltpu.make_async_copy(message.at[pl.ds(0, width)], kept.at[slot], sem)
        copy.start()
        copy.wait()


def place(count, width, message, kept=None):
    return pl.pallas_call(
        functools.partial(place_kernel, width),
        in_specs=[in_vmem()] + ([] if kept is None else [in_hbm()]),
        out_specs=in_hbm(),
        out_shape=jax.ShapeDtypeStruct((count, width, NSTATE), BF16),
        input_output_aliases={} if kept is None else {1: 0},
        scratch_shapes=[pltpu.SemaphoreType.DMA],
        cost_estimate=STEP,
        name="place",
    )(message, *([] if kept is None else [kept]))


def close_kernel(n, *refs):
    messages = refs[:n]
    corr = refs[n : n + 1 + len(RAW)]
    _, kept, out_inner, out_ssm, sem = refs[n + 1 + len(RAW) :]
    width = out_inner.shape[2]
    tiles = width // NSTATE
    marks = []
    for ref in messages:
        lows = halves(ref, width)
        marks.append((mark_of(lows[tiles]), lows))
    last = marks[0][0]

    def put():
        return pltpu.make_async_copy(messages[0].at[pl.ds(0, width)], kept.at[last], sem)

    @pl.when(last >= 0)
    def _():
        put().start()

    def write_edges(slot, inner, low):
        out_inner[slot] = inner[: KCONV - 1].astype(BF16)
        high = pltpu.roll(low, DRAFT - 3, 0)
        out_ssm[slot] = jnp.concatenate([low[:3], high[:3]], axis=1).astype(BF16)

    for ref in corr:
        low = ref[...].astype(F32)[DRAFT:]
        slot = mark_of(low[:, width:])

        @pl.when(slot >= 0)
        def _(slot=slot, low=low):
            write_edges(slot, low[:, :width], low[:, width:])

    for slot, lows in marks:

        @pl.when(slot >= 0)
        def _(slot=slot, lows=lows):
            write_edges(slot, jnp.concatenate(lows[:tiles], axis=1), lows[tiles])

    @pl.when(last >= 0)
    def _():
        put().wait()


def close(count, width, messages, corr, kept):
    n = len(messages)
    return pl.pallas_call(
        functools.partial(close_kernel, n),
        in_specs=[in_vmem()] * (n + len(corr)) + [in_hbm()],
        out_specs=[in_hbm(), in_vmem(), in_vmem()],
        out_shape=[
            jax.ShapeDtypeStruct((count, width, NSTATE), BF16),
            jax.ShapeDtypeStruct((count, KCONV - 1, width), BF16),
            jax.ShapeDtypeStruct((count, KCONV - 1, 2 * NSTATE), BF16),
        ],
        input_output_aliases={n + len(corr): 0},
        scratch_shapes=[pltpu.SemaphoreType.DMA],
        cost_estimate=SMALL,
        name="close",
    )(*messages, *corr, kept)


def moved(array, by):
    length = lax.axis_size("req")
    return lax.ppermute(array, "req", [(i, (i + by) % length) for i in range(length)])


def local(
    hidden_in,
    norm_gain,
    proj_gate,
    proj_inner,
    proj_ssm,
    proj_step,
    step_bias,
    decay_log,
    skip_gain,
    conv_inner,
    conv_inner_bias,
    conv_ssm,
    conv_ssm_bias,
    gate_gain,
    proj_out,
    states_in,
    edge_inner,
    edge_ssm,
    draft_lengths,
    accepted,
    destination,
):
    count, heads = states_in.shape[:2]
    depth, width = proj_inner.shape
    peers = lax.axis_size("req")
    flat = states_in.reshape(count, width, NSTATE)
    *raws, table = pick(count, width, peers, destination, flat)
    raws = [moved(raw, k) for raw, k in zip(raws, RAW)]
    table, ready, ready_ssm = lax.optimization_barrier((table, hidden_in, proj_ssm))
    vectors = jnp.stack([norm_gain, conv_inner_bias, gate_gain])
    results = front(
        count,
        heads,
        width,
        depth,
        (
            table,
            draft_lengths,
            accepted,
            lax.all_gather(ready, "head", axis=0, tiled=False),
            vectors,
            proj_gate,
            proj_inner,
            proj_out,
            lax.all_gather(ready_ssm, "head", axis=0, tiled=False),
            proj_step.T,
            jnp.stack([step_bias, decay_log, skip_gain]),
            conv_inner,
            vectors,
            conv_ssm,
            conv_ssm_bias.reshape(1, 2 * NSTATE),
            flat,
            edge_inner,
            edge_ssm,
        ),
    )
    mine, theirs = results[:2]
    corr = list(results[2:])
    fifth, fourth, third, second = finish((5, 4, 3, 2), table, flat, corr)
    *raws, corr[7], fifth, fourth, third, second, later = lax.optimization_barrier(
        (*raws, corr[7], fifth, fourth, third, second, table)
    )
    fifth = moved(fifth, 5)
    fourth = moved(fourth, 4)
    third = moved(third, 3)
    second = moved(second, 2)
    corr[7] = moved(corr[7], 7)
    (first,) = finish((1,), later, flat, corr)

    pair = lax.all_gather(theirs, "head", axis=0, tiled=False)
    other = jnp.where(lax.axis_index("head") == 0, pair[1], pair[0])
    total = mine + other
    half = depth // 2
    scale = lax.rsqrt(total[:, half : half + 1] / DINNER + epsilon)
    hidden_out = (hidden_in.astype(F32) + total[:, :half] * scale).astype(BF16)

    fifth, fourth, third, second, corr[7], corr[6], first = lax.optimization_barrier(
        (fifth, fourth, third, second, corr[7], corr[6], first)
    )
    first = moved(first, 1)
    corr[6] = moved(corr[6], 6)
    sent = [corr[0], *corr[6:]]
    kept = place(count, width, fifth)
    kept = place(count, width, fourth, kept)
    kept = place(count, width, third, kept)
    kept = place(count, width, second, kept)
    kept = merge(count, table, flat, raws, sent, kept)
    kept, kept_inner, kept_ssm = close(
        count, width, (first, second, third, fourth, fifth), sent, kept
    )
    return (hidden_out, kept.reshape(states_in.shape), kept_inner, kept_ssm)


def solution(mesh):
    in_specs = (
        P("req", "head"),
        P(),
        P(None, "head"),
        P(None, "head"),
        P(None, "head"),
        P(None, "head"),
        P("head"),
        P("head"),
        P("head"),
        P(None, "head"),
        P("head"),
        P(),
        P(),
        P("head"),
        P("head", None),
        P("req", "head", None, None),
        P("req", None, "head"),
        P("req", None, None),
        P("req"),
        P("req"),
        P("req"),
    )
    out_specs = (
        P("req", "head"),
        P("req", "head", None, None),
        P("req", None, "head"),
        P("req", None, None),
    )
    return jax.shard_map(local, mesh=mesh, in_specs=in_specs, out_specs=out_specs, check_vma=False)
```

```python
import functools

import jax
import jax.numpy as jnp
from jax import lax
from jax.experimental import pallas as pl
from jax.experimental.pallas import tpu as pltpu
from jax.sharding import PartitionSpec as P

HEAD_DIM = 64
NSTATE = 128
KCONV = 4
DRAFT = 8
WINDOW = 8
DINNER = 3072
TILE = 256
EXTRA = NSTATE
RAW = (7, 2)
PARTS = 3
SMALL = pl.CostEstimate(flops=1024, bytes_accessed=1024, transcendentals=0)
STEP = pl.CostEstimate(flops=1024, bytes_accessed=8_000_000, transcendentals=0)

epsilon = 1e-05
HIGH = lax.Precision.HIGHEST
F32 = jnp.float32
BF16 = jnp.bfloat16


def iota(shape, axis):
    return lax.broadcasted_iota(jnp.int32, shape, axis)


def mm(a, b, precision=None):
    return jnp.dot(a, b, preferred_element_type=F32, precision=precision)


def mm_t(a, b):
    return lax.dot_general(a, b, (((1,), (1,)), ((), ())), preferred_element_type=F32)


def silu(x):
    return x * (1.0 / (1.0 + jnp.exp(-x)))


def conv_rows(rows, edges, taps, bias):
    slot = iota(rows.shape, 1)
    total = bias + taps[KCONV - 1 : KCONV] * rows
    for back in range(1, KCONV):
        mixed = jnp.where(slot >= DRAFT - back, edges, rows)
        total = total + taps[KCONV - 1 - back : KCONV - back] * pltpu.roll(mixed, back, 1)
    return total


def front_kernel(
    count,
    heads,
    table,
    lengths_in,
    accepted_in,
    hidden,
    vectors,
    w_gate,
    w_inner,
    w_out,
    w_ssm,
    w_step,
    head_rows,
    taps_inner,
    vector_tile,
    taps_ssm,
    bias_ssm,
    states,
    edge_inner,
    edge_ssm,
    mine,
    theirs,
    *rest,
):
    corr = rest[:WINDOW]
    normed, acc, squares, quant, gmat, cmat, select, boxes, edge_pad = rest[WINDOW:]
    step = pl.program_id(0)
    last = pl.num_programs(0) - 1
    rows = count * DRAFT
    width = acc.shape[1]
    half = width // 2

    @pl.when(step == 0)
    def _():
        wide = jnp.concatenate([hidden[0], hidden[1]], axis=1).astype(F32)
        scale = lax.rsqrt(jnp.mean(wide * wide, axis=-1, keepdims=True) + epsilon)
        norm = (wide * scale * vectors[0:1]).astype(BF16)
        normed[...] = norm
        acc[...] = jnp.zeros_like(acc)
        squares[...] = jnp.zeros_like(squares)
        boxes[...] = jnp.zeros_like(boxes)
        edge_pad[...] = jnp.zeros_like(edge_pad)
        edge_pad[:, DRAFT - KCONV + 1 :] = edge_ssm[...].astype(F32)
        row = iota((rows, rows), 0)
        col = iota((rows, rows), 1)
        request = row >> 3
        taken = jnp.zeros((rows, rows), jnp.int32)
        for r in range(count):
            taken = jnp.where(request == r, accepted_in[r], taken)
        same = request == (col >> 3)
        lower = same & ((col & 7) <= (row & 7))
        before = same & ((col & 7) < taken)
        raw = mm_t(norm, w_step[...]).astype(BF16).astype(F32) + head_rows[0:1]
        lengths = jnp.zeros((rows, heads), jnp.int32)
        chosen = jnp.zeros((rows, heads), jnp.int32)
        hrow = iota((rows, heads), 0)
        for r in range(count):
            lengths = jnp.where((hrow >> 3) == r, lengths_in[r], lengths)
            chosen = jnp.where((hrow >> 3) == r, accepted_in[r], chosen)
        soft = jnp.maximum(raw, 0.0) + jnp.log1p(jnp.exp(-jnp.abs(raw)))
        size = jnp.where((hrow & 7) < lengths, soft, 0.0)
        rate = -jnp.exp(head_rows[1:2])
        cum = mm(lower.astype(F32), size, HIGH)
        upto = mm(before.astype(F32), size, HIGH)
        weight = jnp.where(
            (hrow & 7) < chosen, jnp.exp(jnp.minimum(rate * (upto - cum), 0.0)) * size, 0.0
        )
        stacked = jnp.concatenate(
            [
                rate * cum,
                size,
                weight,
                jnp.exp(rate * upto),
                jnp.broadcast_to(head_rows[2:3], (16, heads)),
            ],
            axis=0,
        )
        for part in range(3):
            piece = stacked.astype(BF16)
            quant[part] = piece
            stacked = stacked - piece.astype(F32)
        sel_rows = jnp.where(
            same & ((row & 7) < KCONV - 1),
            ((col & 7) == (row & 7) + taken - 3).astype(F32),
            0.0,
        ).astype(BF16)
        sel_edge = jnp.where(
            same & ((row & 7) < KCONV - 1),
            ((col & 7) == (row & 7) + taken + 5).astype(F32),
            0.0,
        ).astype(BF16)
        select[0] = sel_rows
        select[1] = sel_edge
        ssm = jnp.concatenate([mm(norm, w_ssm[0]), mm(norm, w_ssm[1])], axis=1).astype(BF16)
        before_ssm = edge_pad[...]
        conv = conv_rows(
            ssm.astype(F32).reshape(count, DRAFT, 2 * NSTATE),
            before_ssm,
            taps_ssm[...].astype(F32),
            bias_ssm[...],
        )
        both = silu(conv).reshape(rows, 2 * NSTATE).astype(BF16)
        bmat = both[:, :NSTATE]
        cvec = both[:, NSTATE:]
        cmat[...] = cvec.astype(F32)
        pair = jnp.where(lower, mm_t(cvec, bmat), 0.0)
        fold = ((iota((rows, NSTATE), 0) & 7) == iota((rows, NSTATE), 1)).astype(F32)
        gmat[...] = mm(pair, fold, HIGH)
        kept = mm(sel_rows, ssm) + mm(
            sel_edge, before_ssm.reshape(rows, 2 * NSTATE).astype(BF16)
        )
        wide_b = bmat.astype(F32)
        place = iota((DRAFT, NSTATE), 0)
        for r in range(count):
            own = kept[r * DRAFT : (r + 1) * DRAFT]
            packed = jnp.where(
                place < 3,
                own[:, :NSTATE],
                jnp.where(
                    place < 6,
                    pltpu.roll(own[:, NSTATE:], 3, 0),
                    jnp.full((DRAFT, NSTATE), (table[1, r] + 1).astype(F32)),
                ),
            )
            boxes[table[0, r], :, :NSTATE] = jnp.concatenate(
                [wide_b[r * DRAFT : (r + 1) * DRAFT], packed], axis=0
            ).astype(BF16)
        for k in range(WINDOW):
            corr[k][:, width:] = boxes[k, :, :NSTATE]

    norm = normed[...]
    inner = mm(norm, w_inner[...]).astype(BF16)
    gate = mm(norm, w_gate[...]).astype(BF16).astype(F32)
    edge_pad[:, DRAFT - KCONV + 1 :] = edge_inner[...].astype(F32)
    edges = edge_pad[...]
    conv = conv_rows(
        inner.astype(F32).reshape(count, DRAFT, TILE),
        edges,
        taps_inner[...].astype(F32),
        vector_tile[1:2],
    )
    x = silu(conv).reshape(rows, TILE).astype(BF16).astype(F32)
    first_head = step * (TILE // HEAD_DIM)
    spread = (
        iota((heads, TILE), 0) == first_head + (iota((heads, TILE), 1) >> 6)
    ).astype(BF16)
    expanded = mm(quant[0], spread) + mm(quant[1], spread) + mm(quant[2], spread)
    level = expanded[:rows]
    weighted = expanded[rows : 2 * rows] * x
    past = jnp.concatenate(
        [
            mm_t(cmat[r * DRAFT : (r + 1) * DRAFT].astype(BF16), states[r])
            for r in range(count)
        ],
        axis=0,
    )
    out = jnp.exp(level) * past + expanded[4 * rows : 4 * rows + 1] * x
    level3 = level.reshape(count, DRAFT, TILE)
    weighted3 = weighted.reshape(count, DRAFT, TILE)
    total = jnp.zeros((count, DRAFT, TILE), F32)
    for u in range(DRAFT):
        factor = jnp.exp(jnp.minimum(level3 - level3[:, u : u + 1], 0.0))
        share = gmat[:, u : u + 1].reshape(count, DRAFT, 1)
        total = total + share * factor * weighted3[:, u : u + 1]
    out = (out + total.reshape(rows, TILE)).astype(BF16).astype(F32)
    gated = out * silu(gate)
    squared = gated * gated
    squares[...] += squared[:, :128] + squared[:, 128:]
    acc[...] += mm((gated * vector_tile[2:3]).astype(BF16), w_out[...])
    delta = expanded[2 * rows : 3 * rows] * x
    decay = expanded[3 * rows : 4 * rows]
    decay_hi = decay.astype(BF16).astype(F32)
    second = mm(select[0], inner) + mm(select[1], edges.reshape(rows, TILE).astype(BF16))
    place = iota((rows, TILE), 0) & 7
    second = jnp.where(
        place == 3, decay_hi, jnp.where(place == 4, decay - decay_hi, second)
    )
    for r in range(count):
        span = slice(r * DRAFT, (r + 1) * DRAFT)
        boxes[table[0, r]] = jnp.concatenate([delta[span], second[span]], axis=0).astype(BF16)
    here = pl.ds(pl.multiple_of(step * TILE, TILE), TILE)
    for k in range(WINDOW):
        corr[k][:, here] = boxes[k]

    @pl.when(step == last)
    def _():
        total_square = jnp.broadcast_to(
            jnp.sum(squares[...], axis=1, keepdims=True), squares.shape
        )
        mine[:, half:] = total_square
        theirs[:, half:] = total_square

        @pl.when(table[2, 0] == 0)
        def _():
            mine[:, :half] = acc[:, :half]
            theirs[:, :half] = acc[:, half:]

        @pl.when(table[2, 0] != 0)
        def _():
            mine[:, :half] = acc[:, half:]
            theirs[:, :half] = acc[:, :half]


def front(count, heads, width, depth, args):
    rows = count * DRAFT
    tiles = width // TILE

    def whole(shape):
        return pl.BlockSpec(shape, lambda j: (0,) * len(shape))

    in_specs = [
        *[pl.BlockSpec(memory_space=pltpu.SMEM)] * 3,
        whole((2, rows, depth // 2)),
        whole((3, depth)),
        pl.BlockSpec((depth, TILE), lambda j: (0, j)),
        pl.BlockSpec((depth, TILE), lambda j: (0, j)),
        pl.BlockSpec((TILE, depth), lambda j: (j, 0)),
        whole((2, depth, NSTATE)),
        whole((heads, depth)),
        whole((3, heads)),
        pl.BlockSpec((KCONV, TILE), lambda j: (0, j)),
        pl.BlockSpec((3, TILE), lambda j: (0, j)),
        whole((KCONV, 2 * NSTATE)),
        whole((1, 2 * NSTATE)),
        pl.BlockSpec((count, TILE, NSTATE), lambda j: (0, j, 0)),
        pl.BlockSpec((count, KCONV - 1, TILE), lambda j: (0, 0, j)),
        whole((count, KCONV - 1, 2 * NSTATE)),
    ]
    out_width = depth // 2 + 128
    out_shape = [jax.ShapeDtypeStruct((rows, out_width), F32)] * 2 + [
        jax.ShapeDtypeStruct((2 * DRAFT, width + EXTRA), BF16)
    ] * WINDOW
    out_specs = [whole((rows, out_width))] * 2 + [whole((2 * DRAFT, width + EXTRA))] * WINDOW
    return pl.pallas_call(
        functools.partial(front_kernel, count, heads),
        grid=(tiles,),
        in_specs=in_specs,
        out_specs=out_specs,
        out_shape=out_shape,
        scratch_shapes=[
            pltpu.VMEM((rows, depth), BF16),
            pltpu.VMEM((rows, depth), F32),
            pltpu.VMEM((rows, 128), F32),
            pltpu.VMEM((3, 4 * rows + 16, heads), BF16),
            pltpu.VMEM((rows, NSTATE), F32),
            pltpu.VMEM((rows, NSTATE), F32),
            pltpu.VMEM((2, rows, rows), BF16),
            pltpu.VMEM((WINDOW, 2 * DRAFT, TILE), BF16),
            pltpu.VMEM((count, DRAFT, TILE), F32),
        ],
        compiler_params=pltpu.CompilerParams(dimension_semantics=("arbitrary",)),
        cost_estimate=SMALL,
        name="front",
    )(*args)


def pick_kernel(count, peers, destination, states, *outs):
    picked = outs[: len(RAW)]
    table, sems = outs[len(RAW) :]
    here = lax.axis_index("req")
    reach = [
        lax.rem(lax.div(destination[r], count) - here + peers, peers) for r in range(count)
    ]
    index = []
    for k in range(WINDOW):
        index.append(sum((reach[r] == k).astype(jnp.int32) * r for r in range(count)))
        table[3, k] = index[k]
    copies = []
    for n, k in enumerate(RAW):
        copy = pltpu.make_async_copy(states.at[index[k]], picked[n], sems.at[n])
        copy.start()
        copies.append(copy)
    for r in range(count):
        table[0, r] = reach[r]
        table[1, r] = lax.rem(destination[r], count)
        table[2, r] = lax.axis_index("head")
    for copy in copies:
        copy.wait()


def in_hbm():
    return pl.BlockSpec(memory_space=pl.ANY)


def in_vmem():
    return pl.BlockSpec(memory_space=pltpu.VMEM)


def in_smem():
    return pl.BlockSpec(memory_space=pltpu.SMEM)


def pick(count, width, peers, destination, states):
    return pl.pallas_call(
        functools.partial(pick_kernel, count, peers),
        in_specs=[in_smem(), in_hbm()],
        out_specs=[in_vmem()] * len(RAW) + [in_smem()],
        out_shape=[jax.ShapeDtypeStruct((width, NSTATE), BF16)] * len(RAW)
        + [jax.ShapeDtypeStruct((4, max(count, WINDOW)), jnp.int32)],
        scratch_shapes=[pltpu.SemaphoreType.DMA((len(RAW),))],
        cost_estimate=SMALL,
        name="pick",
    )(destination, states)


def advance(corr, state, out):
    width = state.shape[0]
    line = iota((2 * DRAFT, NSTATE), 0)
    bmat = jnp.where(line < DRAFT, corr[:, width:].astype(F32), 0.0)
    ones = jnp.where((line == 11) | (line == 12), 1.0, 0.0)
    right = jnp.concatenate([bmat, ones], axis=1).astype(BF16)
    part = width // PARTS
    for c in range(PARTS):
        span = slice(c * part, (c + 1) * part)
        both = lax.dot_general(
            corr[:, span], right, (((0,), (0,)), ((), ())), preferred_element_type=F32
        )
        out[span] = (both[:, NSTATE:] * state[span].astype(F32) + both[:, :NSTATE]).astype(BF16)


def tail_rows(width):
    pairs = (width // NSTATE + 2) // 2
    return pairs, pairs * 2 * DRAFT


def finish_kernel(offsets, *refs):
    n = len(offsets)
    table, states = refs[:2]
    corr = refs[2 : 2 + n]
    outs = refs[2 + n : 2 + 2 * n]
    loaded, sems = refs[-2:]
    width = loaded.shape[1]
    pairs, _ = tail_rows(width)
    copies = []
    for i, k in enumerate(offsets):
        copy = pltpu.make_async_copy(states.at[table[3, k]], loaded.at[i], sems.at[i])
        copy.start()
        copies.append(copy)
    for i in range(n):
        low = corr[i][...].astype(F32)[DRAFT:]
        low = jnp.concatenate(
            [low, jnp.zeros((DRAFT, 2 * pairs * NSTATE - low.shape[1]), F32)], axis=1
        )
        for t in range(pairs):
            block = jnp.concatenate(
                [
                    low[:, t * NSTATE : (t + 1) * NSTATE],
                    low[:, (t + pairs) * NSTATE : (t + pairs + 1) * NSTATE],
                ],
                axis=0,
            )
            outs[i][width + t * 2 * DRAFT : width + (t + 1) * 2 * DRAFT] = block.astype(BF16)
        copies[i].wait()
        advance(corr[i], loaded.at[i], outs[i])


def finish(offsets, table, states, corr):
    n = len(offsets)
    width = states.shape[1]
    shape = jax.ShapeDtypeStruct((width + tail_rows(width)[1], NSTATE), BF16)
    return pl.pallas_call(
        functools.partial(finish_kernel, offsets),
        in_specs=[in_smem(), in_hbm()] + [in_vmem()] * n,
        out_specs=[in_vmem()] * n,
        out_shape=[shape] * n,
        scratch_shapes=[
            pltpu.VMEM((n, width, NSTATE), BF16),
            pltpu.SemaphoreType.DMA((n,)),
        ],
        cost_estimate=SMALL,
        name="finish",
    )(table, states, *[corr[k] for k in offsets])


def mark_of(low):
    return jnp.max(low[6:7]).astype(jnp.int32) - 1


def merge_kernel(table, states, *refs):
    n = 1 + len(RAW)
    raws = refs[: n - 1]
    corr = refs[n - 1 : 2 * n - 1]
    _, kept, loaded, merged, sem_in, sem_out = refs[2 * n - 1 :]
    width = loaded.shape[0]
    own = pltpu.make_async_copy(states.at[table[3, 0]], loaded, sem_in)
    own.start()
    slots = [mark_of(ref[:, width:].astype(F32)[DRAFT:]) for ref in corr]

    def put(i):
        return pltpu.make_async_copy(merged.at[i], kept.at[slots[i]], sem_out.at[i])

    for i in range(n):
        if i == 0:
            own.wait()

        @pl.when(slots[i] >= 0)
        def _(i=i):
            advance(corr[i], raws[i - 1] if i > 0 else loaded, merged.at[i])
            put(i).start()

    for i in range(n):

        @pl.when(slots[i] >= 0)
        def _(i=i):
            put(i).wait()


def merge(count, table, states, raws, corr, kept):
    width = states.shape[1]
    n = 1 + len(RAW)
    return pl.pallas_call(
        merge_kernel,
        in_specs=[in_smem(), in_hbm()] + [in_vmem()] * (2 * n - 1) + [in_hbm()],
        out_specs=in_hbm(),
        out_shape=jax.ShapeDtypeStruct((count, width, NSTATE), BF16),
        scratch_shapes=[
            pltpu.VMEM((width, NSTATE), BF16),
            pltpu.VMEM((n, width, NSTATE), BF16),
            pltpu.SemaphoreType.DMA,
            pltpu.SemaphoreType.DMA((n,)),
        ],
        input_output_aliases={1 + 2 * n: 0},
        cost_estimate=SMALL,
        name="merge",
    )(table, states, *raws, *corr, kept)


def halves(ref, width):
    parts = [
        ref[row : row + 2 * DRAFT].astype(F32)
        for row in range(width, ref.shape[0], 2 * DRAFT)
    ]
    return [part[:DRAFT] for part in parts] + [part[DRAFT:] for part in parts]


def place_kernel(width, message, *refs):
    kept, sem = refs[-2:]
    slot = mark_of(halves(message, width)[width // NSTATE])

    @pl.when(slot >= 0)
    def _():
        copy = pltpu.make_async_copy(message.at[pl.ds(0, width)], kept.at[slot], sem)
        copy.start()
        copy.wait()


def place(count, width, message, kept=None):
    return pl.pallas_call(
        functools.partial(place_kernel, width),
        in_specs=[in_vmem()] + ([] if kept is None else [in_hbm()]),
        out_specs=in_hbm(),
        out_shape=jax.ShapeDtypeStruct((count, width, NSTATE), BF16),
        input_output_aliases={} if kept is None else {1: 0},
        scratch_shapes=[pltpu.SemaphoreType.DMA],
        cost_estimate=STEP,
        name="place",
    )(message, *([] if kept is None else [kept]))


def close_kernel(n, *refs):
    messages = refs[:n]
    corr = refs[n : n + 1 + len(RAW)]
    _, kept, out_inner, out_ssm, sem = refs[n + 1 + len(RAW) :]
    width = out_inner.shape[2]
    tiles = width // NSTATE
    marks = []
    for ref in messages:
        lows = halves(ref, width)
        marks.append((mark_of(lows[tiles]), lows))
    last = marks[0][0]

    def put():
        return pltpu.make_async_copy(messages[0].at[pl.ds(0, width)], kept.at[last], sem)

    @pl.when(last >= 0)
    def _():
        put().start()

    def write_edges(slot, inner, low):
        out_inner[slot] = inner[: KCONV - 1].astype(BF16)
        high = pltpu.roll(low, DRAFT - 3, 0)
        out_ssm[slot] = jnp.concatenate([low[:3], high[:3]], axis=1).astype(BF16)

    for ref in corr:
        low = ref[...].astype(F32)[DRAFT:]
        slot = mark_of(low[:, width:])

        @pl.when(slot >= 0)
        def _(slot=slot, low=low):
            write_edges(slot, low[:, :width], low[:, width:])

    for slot, lows in marks:

        @pl.when(slot >= 0)
        def _(slot=slot, lows=lows):
            write_edges(slot, jnp.concatenate(lows[:tiles], axis=1), lows[tiles])

    @pl.when(last >= 0)
    def _():
        put().wait()


def close(count, width, messages, corr, kept):
    n = len(messages)
    return pl.pallas_call(
        functools.partial(close_kernel, n),
        in_specs=[in_vmem()] * (n + len(corr)) + [in_hbm()],
        out_specs=[in_hbm(), in_vmem(), in_vmem()],
        out_shape=[
            jax.ShapeDtypeStruct((count, width, NSTATE), BF16),
            jax.ShapeDtypeStruct((count, KCONV - 1, width), BF16),
            jax.ShapeDtypeStruct((count, KCONV - 1, 2 * NSTATE), BF16),
        ],
        input_output_aliases={n + len(corr): 0},
        scratch_shapes=[pltpu.SemaphoreType.DMA],
        cost_estimate=SMALL,
        name="close",
    )(*messages, *corr, kept)


def moved(array, by):
    length = lax.axis_size("req")
    return lax.ppermute(array, "req", [(i, (i + by) % length) for i in range(length)])


def local(
    hidden_in,
    norm_gain,
    proj_gate,
    proj_inner,
    proj_ssm,
    proj_step,
    step_bias,
    decay_log,
    skip_gain,
    conv_inner,
    conv_inner_bias,
    conv_ssm,
    conv_ssm_bias,
    gate_gain,
    proj_out,
    states_in,
    edge_inner,
    edge_ssm,
    draft_lengths,
    accepted,
    destination,
):
    count, heads = states_in.shape[:2]
    depth, width = proj_inner.shape
    peers = lax.axis_size("req")
    flat = states_in.reshape(count, width, NSTATE)
    *raws, table = pick(count, width, peers, destination, flat)
    raws = [moved(raw, k) for raw, k in zip(raws, RAW)]
    table, ready, ready_ssm = lax.optimization_barrier((table, hidden_in, proj_ssm))
    vectors = jnp.stack([norm_gain, conv_inner_bias, gate_gain])
    results = front(
        count,
        heads,
        width,
        depth,
        (
            table,
            draft_lengths,
            accepted,
            lax.all_gather(ready, "head", axis=0, tiled=False),
            vectors,
            proj_gate,
            proj_inner,
            proj_out,
            lax.all_gather(ready_ssm, "head", axis=0, tiled=False),
            proj_step.T,
            jnp.stack([step_bias, decay_log, skip_gain]),
            conv_inner,
            vectors,
            conv_ssm,
            conv_ssm_bias.reshape(1, 2 * NSTATE),
            flat,
            edge_inner,
            edge_ssm,
        ),
    )
    mine, theirs = results[:2]
    corr = list(results[2:])
    sixth, fifth, fourth, third = finish((6, 5, 4, 3), table, flat, corr)
    *raws, corr[7], sixth, fifth, fourth, third, later = lax.optimization_barrier(
        (*raws, corr[7], sixth, fifth, fourth, third, table)
    )
    sixth = moved(sixth, 6)
    fifth = moved(fifth, 5)
    fourth = moved(fourth, 4)
    third = moved(third, 3)
    corr[7] = moved(corr[7], 7)
    (first,) = finish((1,), later, flat, corr)

    pair = lax.all_gather(theirs, "head", axis=0, tiled=False)
    other = jnp.where(lax.axis_index("head") == 0, pair[1], pair[0])
    total = mine + other
    half = depth // 2
    scale = lax.rsqrt(total[:, half : half + 1] / DINNER + epsilon)
    hidden_out = (hidden_in.astype(F32) + total[:, :half] * scale).astype(BF16)

    sixth, fifth, fourth, third, corr[7], corr[2], first = lax.optimization_barrier(
        (sixth, fifth, fourth, third, corr[7], corr[2], first)
    )
    corr[2] = moved(corr[2], 2)
    first = moved(first, 1)
    sent = [corr[0], *(corr[k] for k in RAW)]
    kept = place(count, width, sixth)
    kept = place(count, width, fifth, kept)
    kept = place(count, width, fourth, kept)
    kept = place(count, width, third, kept)
    kept = merge(count, table, flat, raws, sent, kept)
    kept, kept_inner, kept_ssm = close(
        count, width, (first, third, fourth, fifth, sixth), sent, kept
    )
    return (hidden_out, kept.reshape(states_in.shape), kept_inner, kept_ssm)


def solution(mesh):
    in_specs = (
        P("req", "head"),
        P(),
        P(None, "head"),
        P(None, "head"),
        P(None, "head"),
        P(None, "head"),
        P("head"),
        P("head"),
        P("head"),
        P(None, "head"),
        P("head"),
        P(),
        P(),
        P("head"),
        P("head", None),
        P("req", "head", None, None),
        P("req", None, "head"),
        P("req", None, None),
        P("req"),
        P("req"),
        P("req"),
    )
    out_specs = (
        P("req", "head"),
        P("req", "head", None, None),
        P("req", None, "head"),
        P("req", None, None),
    )
    return jax.shard_map(local, mesh=mesh, in_specs=in_specs, out_specs=out_specs, check_vma=False)
```

```python
import functools

import jax
import jax.numpy as jnp
from jax import lax
from jax.experimental import pallas as pl
from jax.experimental.pallas import tpu as pltpu
from jax.sharding import PartitionSpec as P

HEAD_DIM = 64
NSTATE = 128
KCONV = 4
DRAFT = 8
WINDOW = 8
DINNER = 3072
TILE = 256
EXTRA = NSTATE
RAW = (7, 2)
PARTS = 3
SMALL = pl.CostEstimate(flops=1024, bytes_accessed=1024, transcendentals=0)

epsilon = 1e-05
HIGH = lax.Precision.HIGHEST
F32 = jnp.float32
BF16 = jnp.bfloat16


def iota(shape, axis):
    return lax.broadcasted_iota(jnp.int32, shape, axis)


def mm(a, b, precision=None):
    return jnp.dot(a, b, preferred_element_type=F32, precision=precision)


def mm_t(a, b):
    return lax.dot_general(a, b, (((1,), (1,)), ((), ())), preferred_element_type=F32)


def silu(x):
    return x * (1.0 / (1.0 + jnp.exp(-x)))


def conv_rows(rows, edges, taps, bias):
    slot = iota(rows.shape, 1)
    total = bias + taps[KCONV - 1 : KCONV] * rows
    for back in range(1, KCONV):
        mixed = jnp.where(slot >= DRAFT - back, edges, rows)
        total = total + taps[KCONV - 1 - back : KCONV - back] * pltpu.roll(mixed, back, 1)
    return total


def front_kernel(
    count,
    heads,
    table,
    lengths_in,
    accepted_in,
    hidden,
    vectors,
    w_gate,
    w_inner,
    w_out,
    w_ssm,
    w_step,
    head_rows,
    taps_inner,
    vector_tile,
    taps_ssm,
    bias_ssm,
    states,
    edge_inner,
    edge_ssm,
    mine,
    theirs,
    *rest,
):
    corr = rest[:WINDOW]
    normed, acc, squares, quant, gmat, cmat, select, boxes, edge_pad = rest[WINDOW:]
    step = pl.program_id(0)
    last = pl.num_programs(0) - 1
    rows = count * DRAFT
    width = acc.shape[1]
    half = width // 2

    @pl.when(step == 0)
    def _():
        wide = jnp.concatenate([hidden[0], hidden[1]], axis=1).astype(F32)
        scale = lax.rsqrt(jnp.mean(wide * wide, axis=-1, keepdims=True) + epsilon)
        norm = (wide * scale * vectors[0:1]).astype(BF16)
        normed[...] = norm
        acc[...] = jnp.zeros_like(acc)
        squares[...] = jnp.zeros_like(squares)
        boxes[...] = jnp.zeros_like(boxes)
        edge_pad[...] = jnp.zeros_like(edge_pad)
        edge_pad[:, DRAFT - KCONV + 1 :] = edge_ssm[...].astype(F32)
        row = iota((rows, rows), 0)
        col = iota((rows, rows), 1)
        request = row >> 3
        taken = jnp.zeros((rows, rows), jnp.int32)
        for r in range(count):
            taken = jnp.where(request == r, accepted_in[r], taken)
        same = request == (col >> 3)
        lower = same & ((col & 7) <= (row & 7))
        before = same & ((col & 7) < taken)
        raw = mm_t(norm, w_step[...]).astype(BF16).astype(F32) + head_rows[0:1]
        lengths = jnp.zeros((rows, heads), jnp.int32)
        chosen = jnp.zeros((rows, heads), jnp.int32)
        hrow = iota((rows, heads), 0)
        for r in range(count):
            lengths = jnp.where((hrow >> 3) == r, lengths_in[r], lengths)
            chosen = jnp.where((hrow >> 3) == r, accepted_in[r], chosen)
        soft = jnp.maximum(raw, 0.0) + jnp.log1p(jnp.exp(-jnp.abs(raw)))
        size = jnp.where((hrow & 7) < lengths, soft, 0.0)
        rate = -jnp.exp(head_rows[1:2])
        cum = mm(lower.astype(F32), size, HIGH)
        upto = mm(before.astype(F32), size, HIGH)
        weight = jnp.where(
            (hrow & 7) < chosen, jnp.exp(jnp.minimum(rate * (upto - cum), 0.0)) * size, 0.0
        )
        stacked = jnp.concatenate(
            [
                rate * cum,
                size,
                weight,
                jnp.exp(rate * upto),
                jnp.broadcast_to(head_rows[2:3], (16, heads)),
            ],
            axis=0,
        )
        for part in range(3):
            piece = stacked.astype(BF16)
            quant[part] = piece
            stacked = stacked - piece.astype(F32)
        sel_rows = jnp.where(
            same & ((row & 7) < KCONV - 1),
            ((col & 7) == (row & 7) + taken - 3).astype(F32),
            0.0,
        ).astype(BF16)
        sel_edge = jnp.where(
            same & ((row & 7) < KCONV - 1),
            ((col & 7) == (row & 7) + taken + 5).astype(F32),
            0.0,
        ).astype(BF16)
        select[0] = sel_rows
        select[1] = sel_edge
        ssm = jnp.concatenate([mm(norm, w_ssm[0]), mm(norm, w_ssm[1])], axis=1).astype(BF16)
        before_ssm = edge_pad[...]
        conv = conv_rows(
            ssm.astype(F32).reshape(count, DRAFT, 2 * NSTATE),
            before_ssm,
            taps_ssm[...].astype(F32),
            bias_ssm[...],
        )
        both = silu(conv).reshape(rows, 2 * NSTATE).astype(BF16)
        bmat = both[:, :NSTATE]
        cvec = both[:, NSTATE:]
        cmat[...] = cvec.astype(F32)
        pair = jnp.where(lower, mm_t(cvec, bmat), 0.0)
        fold = ((iota((rows, NSTATE), 0) & 7) == iota((rows, NSTATE), 1)).astype(F32)
        gmat[...] = mm(pair, fold, HIGH)
        kept = mm(sel_rows, ssm) + mm(
            sel_edge, before_ssm.reshape(rows, 2 * NSTATE).astype(BF16)
        )
        wide_b = bmat.astype(F32)
        place = iota((DRAFT, NSTATE), 0)
        for r in range(count):
            own = kept[r * DRAFT : (r + 1) * DRAFT]
            packed = jnp.where(
                place < 3,
                own[:, :NSTATE],
                jnp.where(
                    place < 6,
                    pltpu.roll(own[:, NSTATE:], 3, 0),
                    jnp.full((DRAFT, NSTATE), (table[1, r] + 1).astype(F32)),
                ),
            )
            boxes[table[0, r], :, :NSTATE] = jnp.concatenate(
                [wide_b[r * DRAFT : (r + 1) * DRAFT], packed], axis=0
            ).astype(BF16)
        for k in range(WINDOW):
            corr[k][:, width:] = boxes[k, :, :NSTATE]

    norm = normed[...]
    inner = mm(norm, w_inner[...]).astype(BF16)
    gate = mm(norm, w_gate[...]).astype(BF16).astype(F32)
    edge_pad[:, DRAFT - KCONV + 1 :] = edge_inner[...].astype(F32)
    edges = edge_pad[...]
    conv = conv_rows(
        inner.astype(F32).reshape(count, DRAFT, TILE),
        edges,
        taps_inner[...].astype(F32),
        vector_tile[1:2],
    )
    x = silu(conv).reshape(rows, TILE).astype(BF16).astype(F32)
    first_head = step * (TILE // HEAD_DIM)
    spread = (
        iota((heads, TILE), 0) == first_head + (iota((heads, TILE), 1) >> 6)
    ).astype(BF16)
    expanded = mm(quant[0], spread) + mm(quant[1], spread) + mm(quant[2], spread)
    level = expanded[:rows]
    weighted = expanded[rows : 2 * rows] * x
    past = jnp.concatenate(
        [
            mm_t(cmat[r * DRAFT : (r + 1) * DRAFT].astype(BF16), states[r])
            for r in range(count)
        ],
        axis=0,
    )
    out = jnp.exp(level) * past + expanded[4 * rows : 4 * rows + 1] * x
    level3 = level.reshape(count, DRAFT, TILE)
    weighted3 = weighted.reshape(count, DRAFT, TILE)
    total = jnp.zeros((count, DRAFT, TILE), F32)
    for u in range(DRAFT):
        factor = jnp.exp(jnp.minimum(level3 - level3[:, u : u + 1], 0.0))
        share = gmat[:, u : u + 1].reshape(count, DRAFT, 1)
        total = total + share * factor * weighted3[:, u : u + 1]
    out = (out + total.reshape(rows, TILE)).astype(BF16).astype(F32)
    gated = out * silu(gate)
    squared = gated * gated
    squares[...] += squared[:, :128] + squared[:, 128:]
    acc[...] += mm((gated * vector_tile[2:3]).astype(BF16), w_out[...])
    delta = expanded[2 * rows : 3 * rows] * x
    decay = expanded[3 * rows : 4 * rows]
    decay_hi = decay.astype(BF16).astype(F32)
    second = mm(select[0], inner) + mm(select[1], edges.reshape(rows, TILE).astype(BF16))
    place = iota((rows, TILE), 0) & 7
    second = jnp.where(
        place == 3, decay_hi, jnp.where(place == 4, decay - decay_hi, second)
    )
    for r in range(count):
        span = slice(r * DRAFT, (r + 1) * DRAFT)
        boxes[table[0, r]] = jnp.concatenate([delta[span], second[span]], axis=0).astype(BF16)
    here = pl.ds(pl.multiple_of(step * TILE, TILE), TILE)
    for k in range(WINDOW):
        corr[k][:, here] = boxes[k]

    @pl.when(step == last)
    def _():
        total_square = jnp.broadcast_to(
            jnp.sum(squares[...], axis=1, keepdims=True), squares.shape
        )
        mine[:, half:] = total_square
        theirs[:, half:] = total_square

        @pl.when(table[2, 0] == 0)
        def _():
            mine[:, :half] = acc[:, :half]
            theirs[:, :half] = acc[:, half:]

        @pl.when(table[2, 0] != 0)
        def _():
            mine[:, :half] = acc[:, half:]
            theirs[:, :half] = acc[:, :half]


def front(count, heads, width, depth, args):
    rows = count * DRAFT
    tiles = width // TILE

    def whole(shape):
        return pl.BlockSpec(shape, lambda j: (0,) * len(shape))

    in_specs = [
        *[pl.BlockSpec(memory_space=pltpu.SMEM)] * 3,
        whole((2, rows, depth // 2)),
        whole((3, depth)),
        pl.BlockSpec((depth, TILE), lambda j: (0, j)),
        pl.BlockSpec((depth, TILE), lambda j: (0, j)),
        pl.BlockSpec((TILE, depth), lambda j: (j, 0)),
        whole((2, depth, NSTATE)),
        whole((heads, depth)),
        whole((3, heads)),
        pl.BlockSpec((KCONV, TILE), lambda j: (0, j)),
        pl.BlockSpec((3, TILE), lambda j: (0, j)),
        whole((KCONV, 2 * NSTATE)),
        whole((1, 2 * NSTATE)),
        pl.BlockSpec((count, TILE, NSTATE), lambda j: (0, j, 0)),
        pl.BlockSpec((count, KCONV - 1, TILE), lambda j: (0, 0, j)),
        whole((count, KCONV - 1, 2 * NSTATE)),
    ]
    out_width = depth // 2 + 128
    out_shape = [jax.ShapeDtypeStruct((rows, out_width), F32)] * 2 + [
        jax.ShapeDtypeStruct((2 * DRAFT, width + EXTRA), BF16)
    ] * WINDOW
    out_specs = [whole((rows, out_width))] * 2 + [whole((2 * DRAFT, width + EXTRA))] * WINDOW
    return pl.pallas_call(
        functools.partial(front_kernel, count, heads),
        grid=(tiles,),
        in_specs=in_specs,
        out_specs=out_specs,
        out_shape=out_shape,
        scratch_shapes=[
            pltpu.VMEM((rows, depth), BF16),
            pltpu.VMEM((rows, depth), F32),
            pltpu.VMEM((rows, 128), F32),
            pltpu.VMEM((3, 4 * rows + 16, heads), BF16),
            pltpu.VMEM((rows, NSTATE), F32),
            pltpu.VMEM((rows, NSTATE), F32),
            pltpu.VMEM((2, rows, rows), BF16),
            pltpu.VMEM((WINDOW, 2 * DRAFT, TILE), BF16),
            pltpu.VMEM((count, DRAFT, TILE), F32),
        ],
        compiler_params=pltpu.CompilerParams(dimension_semantics=("arbitrary",)),
        cost_estimate=SMALL,
        name="front",
    )(*args)


def pick_kernel(count, peers, destination, states, *outs):
    picked = outs[: len(RAW)]
    table, sems = outs[len(RAW) :]
    here = lax.axis_index("req")
    reach = [
        lax.rem(lax.div(destination[r], count) - here + peers, peers) for r in range(count)
    ]
    index = []
    for k in range(WINDOW):
        index.append(sum((reach[r] == k).astype(jnp.int32) * r for r in range(count)))
        table[3, k] = index[k]
    copies = []
    for n, k in enumerate(RAW):
        copy = pltpu.make_async_copy(states.at[index[k]], picked[n], sems.at[n])
        copy.start()
        copies.append(copy)
    for r in range(count):
        table[0, r] = reach[r]
        table[1, r] = lax.rem(destination[r], count)
        table[2, r] = lax.axis_index("head")
    for copy in copies:
        copy.wait()


def in_hbm():
    return pl.BlockSpec(memory_space=pl.ANY)


def in_vmem():
    return pl.BlockSpec(memory_space=pltpu.VMEM)


def in_smem():
    return pl.BlockSpec(memory_space=pltpu.SMEM)


def pick(count, width, peers, destination, states):
    return pl.pallas_call(
        functools.partial(pick_kernel, count, peers),
        in_specs=[in_smem(), in_hbm()],
        out_specs=[in_vmem()] * len(RAW) + [in_smem()],
        out_shape=[jax.ShapeDtypeStruct((width, NSTATE), BF16)] * len(RAW)
        + [jax.ShapeDtypeStruct((4, max(count, WINDOW)), jnp.int32)],
        scratch_shapes=[pltpu.SemaphoreType.DMA((len(RAW),))],
        cost_estimate=SMALL,
        name="pick",
    )(destination, states)


def advance(corr, state, out):
    width = state.shape[0]
    line = iota((2 * DRAFT, NSTATE), 0)
    bmat = jnp.where(line < DRAFT, corr[:, width:].astype(F32), 0.0)
    ones = jnp.where((line == 11) | (line == 12), 1.0, 0.0)
    right = jnp.concatenate([bmat, ones], axis=1).astype(BF16)
    part = width // PARTS
    for c in range(PARTS):
        span = slice(c * part, (c + 1) * part)
        both = lax.dot_general(
            corr[:, span], right, (((0,), (0,)), ((), ())), preferred_element_type=F32
        )
        out[span] = (both[:, NSTATE:] * state[span].astype(F32) + both[:, :NSTATE]).astype(BF16)


def tail_rows(width):
    tiles = width // NSTATE
    groups = tiles // 2 + 1
    return groups, (groups + groups % 2) * DRAFT


def finish_kernel(offsets, *refs):
    n = len(offsets)
    table, states = refs[:2]
    corr = refs[2 : 2 + n]
    outs = refs[2 + n : 2 + 2 * n]
    loaded, sems = refs[-2:]
    width = loaded.shape[1]
    groups, _ = tail_rows(width)
    copies = []
    for i, k in enumerate(offsets):
        copy = pltpu.make_async_copy(states.at[table[3, k]], loaded.at[i], sems.at[i])
        copy.start()
        copies.append(copy)
    for i in range(n):
        low = corr[i][...].astype(F32)[DRAFT:]
        half = iota((DRAFT, NSTATE), 0) < DRAFT // 2
        tiles = [low[:, t * NSTATE : (t + 1) * NSTATE] for t in range(width // NSTATE + 1)]
        packed = [
            jnp.where(half, tiles[2 * g], pltpu.roll(tiles[2 * g + 1], DRAFT // 2, 0))
            for g in range(groups - 1)
        ]
        packed.append(tiles[-1])
        if groups % 2:
            packed.append(jnp.zeros((DRAFT, NSTATE), F32))
        for g in range(0, len(packed), 2):
            block = jnp.concatenate(packed[g : g + 2], axis=0)
            outs[i][width + g * DRAFT : width + (g + 2) * DRAFT] = block.astype(BF16)
        copies[i].wait()
        advance(corr[i], loaded.at[i], outs[i])


def finish(offsets, table, states, corr):
    n = len(offsets)
    width = states.shape[1]
    shape = jax.ShapeDtypeStruct((width + tail_rows(width)[1], NSTATE), BF16)
    return pl.pallas_call(
        functools.partial(finish_kernel, offsets),
        in_specs=[in_smem(), in_hbm()] + [in_vmem()] * n,
        out_specs=[in_vmem()] * n,
        out_shape=[shape] * n,
        scratch_shapes=[
            pltpu.VMEM((n, width, NSTATE), BF16),
            pltpu.SemaphoreType.DMA((n,)),
        ],
        cost_estimate=SMALL,
        name="finish",
    )(table, states, *[corr[k] for k in offsets])


def mark_of(low):
    return jnp.max(low[6:7]).astype(jnp.int32) - 1


def merge_kernel(own, *refs):
    table, states = refs[:2]
    raw = refs[2]
    corr = refs[3 : 4 + own]
    _, kept, loaded, merged, sem_in, sem_out = refs[4 + own :]
    width = loaded.shape[0]
    if own:
        copy = pltpu.make_async_copy(states.at[table[3, 0]], loaded, sem_in)
        copy.start()
    slots = [mark_of(ref[:, width:].astype(F32)[DRAFT:]) for ref in corr]

    def put(i):
        return pltpu.make_async_copy(merged.at[i], kept.at[slots[i]], sem_out.at[i])

    for i in range(1 + own):
        if i == 1:
            copy.wait()

        @pl.when(slots[i] >= 0)
        def _(i=i):
            advance(corr[i], loaded if i == 1 else raw, merged.at[i])
            put(i).start()

    for i in range(1 + own):

        @pl.when(slots[i] >= 0)
        def _(i=i):
            put(i).wait()


def merge(count, table, states, raw, corr, kept):
    width = states.shape[1]
    n = len(corr)
    return pl.pallas_call(
        functools.partial(merge_kernel, n - 1),
        in_specs=[in_smem(), in_hbm()] + [in_vmem()] * (1 + n) + [in_hbm()],
        out_specs=in_hbm(),
        out_shape=jax.ShapeDtypeStruct((count, width, NSTATE), BF16),
        scratch_shapes=[
            pltpu.VMEM((width, NSTATE), BF16),
            pltpu.VMEM((n, width, NSTATE), BF16),
            pltpu.SemaphoreType.DMA,
            pltpu.SemaphoreType.DMA((n,)),
        ],
        input_output_aliases={3 + n: 0},
        cost_estimate=SMALL,
        name="merge",
    )(table, states, raw, *corr, kept)


def halves(ref, width):
    groups, _ = tail_rows(width)
    tiles = []
    for row in range(width, ref.shape[0], 2 * DRAFT):
        block = ref[row : row + 2 * DRAFT].astype(F32)
        for part in (block[:DRAFT], block[DRAFT:]):
            if len(tiles) < 2 * (groups - 1):
                tiles += [part, pltpu.roll(part, DRAFT // 2, 0)]
            else:
                tiles.append(part)
    return tiles[: 2 * groups - 1]


def place_kernel(n, earlier, *refs):
    messages = refs[:n]
    out = len(refs) - 4
    corr = refs[n : out - 3 * earlier]
    kept, out_inner, out_ssm, sems = refs[out:]
    width = out_inner.shape[2]
    tiles = width // NSTATE
    if earlier:
        out_inner[...] = refs[out - 2][...]
        out_ssm[...] = refs[out - 1][...]
    lows = [halves(ref, width) for ref in messages]
    slots = [mark_of(low[tiles]) for low in lows]

    def put(i):
        return pltpu.make_async_copy(
            messages[i].at[pl.ds(0, width)], kept.at[slots[i]], sems.at[i]
        )

    for i in range(n):

        @pl.when(slots[i] >= 0)
        def _(i=i):
            put(i).start()

    def write_edges(slot, inner, low):
        out_inner[slot] = inner[: KCONV - 1].astype(BF16)
        high = pltpu.roll(low, DRAFT - 3, 0)
        out_ssm[slot] = jnp.concatenate([low[:3], high[:3]], axis=1).astype(BF16)

    for ref in corr:
        low = ref[...].astype(F32)[DRAFT:]
        slot = mark_of(low[:, width:])

        @pl.when(slot >= 0)
        def _(slot=slot, low=low):
            write_edges(slot, low[:, :width], low[:, width:])

    for i in range(n):

        @pl.when(slots[i] >= 0)
        def _(i=i):
            write_edges(slots[i], jnp.concatenate(lows[i][:tiles], axis=1), lows[i][tiles])

    for i in range(n):

        @pl.when(slots[i] >= 0)
        def _(i=i):
            put(i).wait()


def place(count, width, messages, corr, earlier=()):
    n = len(messages)
    inputs = [*messages, *corr]
    return pl.pallas_call(
        functools.partial(place_kernel, n, 1 if earlier else 0),
        in_specs=[in_vmem()] * len(inputs)
        + ([in_hbm(), in_vmem(), in_vmem()] if earlier else []),
        out_specs=[in_hbm(), in_vmem(), in_vmem()],
        out_shape=[
            jax.ShapeDtypeStruct((count, width, NSTATE), BF16),
            jax.ShapeDtypeStruct((count, KCONV - 1, width), BF16),
            jax.ShapeDtypeStruct((count, KCONV - 1, 2 * NSTATE), BF16),
        ],
        input_output_aliases={len(inputs): 0} if earlier else {},
        scratch_shapes=[pltpu.SemaphoreType.DMA((n,))],
        cost_estimate=SMALL,
        name="place",
    )(*inputs, *earlier)


def moved(array, by):
    length = lax.axis_size("req")
    return lax.ppermute(array, "req", [(i, (i + by) % length) for i in range(length)])


def local(
    hidden_in,
    norm_gain,
    proj_gate,
    proj_inner,
    proj_ssm,
    proj_step,
    step_bias,
    decay_log,
    skip_gain,
    conv_inner,
    conv_inner_bias,
    conv_ssm,
    conv_ssm_bias,
    gate_gain,
    proj_out,
    states_in,
    edge_inner,
    edge_ssm,
    draft_lengths,
    accepted,
    destination,
):
    count, heads = states_in.shape[:2]
    depth, width = proj_inner.shape
    peers = lax.axis_size("req")
    flat = states_in.reshape(count, width, NSTATE)
    *raws, table = pick(count, width, peers, destination, flat)
    raws = [moved(raw, k) for raw, k in zip(raws, RAW)]
    table, ready, ready_ssm = lax.optimization_barrier((table, hidden_in, proj_ssm))
    vectors = jnp.stack([norm_gain, conv_inner_bias, gate_gain])
    results = front(
        count,
        heads,
        width,
        depth,
        (
            table,
            draft_lengths,
            accepted,
            lax.all_gather(ready, "head", axis=0, tiled=False),
            vectors,
            proj_gate,
            proj_inner,
            proj_out,
            lax.all_gather(ready_ssm, "head", axis=0, tiled=False),
            proj_step.T,
            jnp.stack([step_bias, decay_log, skip_gain]),
            conv_inner,
            vectors,
            conv_ssm,
            conv_ssm_bias.reshape(1, 2 * NSTATE),
            flat,
            edge_inner,
            edge_ssm,
        ),
    )
    mine, theirs = results[:2]
    corr = list(results[2:])
    sixth, fifth, fourth, third = finish((6, 5, 4, 3), table, flat, corr)
    *raws, corr[7], sixth, fifth, fourth, third, later = lax.optimization_barrier(
        (*raws, corr[7], sixth, fifth, fourth, third, table)
    )
    sixth = moved(sixth, 6)
    fifth = moved(fifth, 5)
    fourth = moved(fourth, 4)
    third = moved(third, 3)
    corr[7] = moved(corr[7], 7)
    (first,) = finish((1,), later, flat, corr)

    pair = lax.all_gather(theirs, "head", axis=0, tiled=False)
    other = jnp.where(lax.axis_index("head") == 0, pair[1], pair[0])
    total = mine + other
    half = depth // 2
    scale = lax.rsqrt(total[:, half : half + 1] / DINNER + epsilon)
    hidden_out = (hidden_in.astype(F32) + total[:, :half] * scale).astype(BF16)

    sixth, fifth, fourth, third, corr[7], corr[2], first = lax.optimization_barrier(
        (sixth, fifth, fourth, third, corr[7], corr[2], first)
    )
    corr[2] = moved(corr[2], 2)
    first = moved(first, 1)
    kept, edges, edges_ssm = place(
        count, width, (sixth, fifth, fourth, third), (corr[0], corr[7])
    )
    kept = merge(count, table, flat, raws[0], (corr[7], corr[0]), kept)
    kept = merge(count, table, flat, raws[1], (corr[2],), kept)
    kept, kept_inner, kept_ssm = place(
        count, width, (first,), (corr[2],), (kept, edges, edges_ssm)
    )
    return (hidden_out, kept.reshape(states_in.shape), kept_inner, kept_ssm)


def solution(mesh):
    in_specs = (
        P("req", "head"),
        P(),
        P(None, "head"),
        P(None, "head"),
        P(None, "head"),
        P(None, "head"),
        P("head"),
        P("head"),
        P("head"),
        P(None, "head"),
        P("head"),
        P(),
        P(),
        P("head"),
        P("head", None),
        P("req", "head", None, None),
        P("req", None, "head"),
        P("req", None, None),
        P("req"),
        P("req"),
        P("req"),
    )
    out_specs = (
        P("req", "head"),
        P("req", "head", None, None),
        P("req", None, "head"),
        P("req", None, None),
    )
    return jax.shard_map(local, mesh=mesh, in_specs=in_specs, out_specs=out_specs, check_vma=False)
```

```python
import functools

import jax
import jax.numpy as jnp
from jax import lax
from jax.experimental import pallas as pl
from jax.experimental.pallas import tpu as pltpu
from jax.sharding import PartitionSpec as P

HEAD_DIM = 64
NSTATE = 128
KCONV = 4
DRAFT = 8
WINDOW = 8
DINNER = 3072
TILE = 256
EXTRA = NSTATE
RAW = (7, 2)
PARTS = 3
ROOM = 12 * 1024 * 1024
SMALL = pl.CostEstimate(flops=1024, bytes_accessed=1024, transcendentals=0)

epsilon = 1e-05
HIGH = lax.Precision.HIGHEST
F32 = jnp.float32
BF16 = jnp.bfloat16


def iota(shape, axis):
    return lax.broadcasted_iota(jnp.int32, shape, axis)


def mm(a, b, precision=None):
    return jnp.dot(a, b, preferred_element_type=F32, precision=precision)


def mm_t(a, b):
    return lax.dot_general(a, b, (((1,), (1,)), ((), ())), preferred_element_type=F32)


def silu(x):
    return x * (1.0 / (1.0 + jnp.exp(-x)))


def conv_rows(rows, edges, taps, bias):
    slot = iota(rows.shape, 1)
    total = bias + taps[KCONV - 1 : KCONV] * rows
    for back in range(1, KCONV):
        mixed = jnp.where(slot >= DRAFT - back, edges, rows)
        total = total + taps[KCONV - 1 - back : KCONV - back] * pltpu.roll(mixed, back, 1)
    return total


def front_kernel(
    count,
    heads,
    table,
    lengths_in,
    accepted_in,
    hidden,
    vectors,
    w_gate,
    w_inner,
    w_out,
    w_ssm,
    w_step,
    head_rows,
    taps_inner,
    vector_tile,
    taps_ssm,
    bias_ssm,
    states,
    edge_inner,
    edge_ssm,
    mine,
    theirs,
    *rest,
):
    corr = rest[:WINDOW]
    normed, acc, squares, quant, gmat, cmat, select, boxes, edge_pad = rest[WINDOW:]
    step = pl.program_id(0)
    last = pl.num_programs(0) - 1
    rows = count * DRAFT
    width = acc.shape[1]
    half = width // 2

    @pl.when(step == 0)
    def _():
        wide = jnp.concatenate([hidden[0], hidden[1]], axis=1).astype(F32)
        scale = lax.rsqrt(jnp.mean(wide * wide, axis=-1, keepdims=True) + epsilon)
        norm = (wide * scale * vectors[0:1]).astype(BF16)
        normed[...] = norm
        acc[...] = jnp.zeros_like(acc)
        squares[...] = jnp.zeros_like(squares)
        boxes[...] = jnp.zeros_like(boxes)
        edge_pad[...] = jnp.zeros_like(edge_pad)
        edge_pad[:, DRAFT - KCONV + 1 :] = edge_ssm[...].astype(F32)
        row = iota((rows, rows), 0)
        col = iota((rows, rows), 1)
        request = row >> 3
        taken = jnp.zeros((rows, rows), jnp.int32)
        for r in range(count):
            taken = jnp.where(request == r, accepted_in[r], taken)
        same = request == (col >> 3)
        lower = same & ((col & 7) <= (row & 7))
        before = same & ((col & 7) < taken)
        raw = mm_t(norm, w_step[...]).astype(BF16).astype(F32) + head_rows[0:1]
        lengths = jnp.zeros((rows, heads), jnp.int32)
        chosen = jnp.zeros((rows, heads), jnp.int32)
        hrow = iota((rows, heads), 0)
        for r in range(count):
            lengths = jnp.where((hrow >> 3) == r, lengths_in[r], lengths)
            chosen = jnp.where((hrow >> 3) == r, accepted_in[r], chosen)
        soft = jnp.maximum(raw, 0.0) + jnp.log1p(jnp.exp(-jnp.abs(raw)))
        size = jnp.where((hrow & 7) < lengths, soft, 0.0)
        rate = -jnp.exp(head_rows[1:2])
        cum = mm(lower.astype(F32), size, HIGH)
        upto = mm(before.astype(F32), size, HIGH)
        weight = jnp.where(
            (hrow & 7) < chosen, jnp.exp(jnp.minimum(rate * (upto - cum), 0.0)) * size, 0.0
        )
        stacked = jnp.concatenate(
            [
                rate * cum,
                size,
                weight,
                jnp.exp(rate * upto),
                jnp.broadcast_to(head_rows[2:3], (16, heads)),
            ],
            axis=0,
        )
        for part in range(3):
            piece = stacked.astype(BF16)
            quant[part] = piece
            stacked = stacked - piece.astype(F32)
        sel_rows = jnp.where(
            same & ((row & 7) < KCONV - 1),
            ((col & 7) == (row & 7) + taken - 3).astype(F32),
            0.0,
        ).astype(BF16)
        sel_edge = jnp.where(
            same & ((row & 7) < KCONV - 1),
            ((col & 7) == (row & 7) + taken + 5).astype(F32),
            0.0,
        ).astype(BF16)
        select[0] = sel_rows
        select[1] = sel_edge
        ssm = jnp.concatenate([mm(norm, w_ssm[0]), mm(norm, w_ssm[1])], axis=1).astype(BF16)
        before_ssm = edge_pad[...]
        conv = conv_rows(
            ssm.astype(F32).reshape(count, DRAFT, 2 * NSTATE),
            before_ssm,
            taps_ssm[...].astype(F32),
            bias_ssm[...],
        )
        both = silu(conv).reshape(rows, 2 * NSTATE).astype(BF16)
        bmat = both[:, :NSTATE]
        cvec = both[:, NSTATE:]
        cmat[...] = cvec.astype(F32)
        pair = jnp.where(lower, mm_t(cvec, bmat), 0.0)
        fold = ((iota((rows, NSTATE), 0) & 7) == iota((rows, NSTATE), 1)).astype(F32)
        gmat[...] = mm(pair, fold, HIGH)
        kept = mm(sel_rows, ssm) + mm(
            sel_edge, before_ssm.reshape(rows, 2 * NSTATE).astype(BF16)
        )
        wide_b = bmat.astype(F32)
        place = iota((DRAFT, NSTATE), 0)
        for r in range(count):
            own = kept[r * DRAFT : (r + 1) * DRAFT]
            packed = jnp.where(
                place < 3,
                own[:, :NSTATE],
                jnp.where(
                    place < 6,
                    pltpu.roll(own[:, NSTATE:], 3, 0),
                    jnp.full((DRAFT, NSTATE), (table[1, r] + 1).astype(F32)),
                ),
            )
            boxes[table[0, r], :, :NSTATE] = jnp.concatenate(
                [wide_b[r * DRAFT : (r + 1) * DRAFT], packed], axis=0
            ).astype(BF16)
        for k in range(WINDOW):
            corr[k][:, width:] = boxes[k, :, :NSTATE]

    norm = normed[...]
    inner = mm(norm, w_inner[...]).astype(BF16)
    gate = mm(norm, w_gate[...]).astype(BF16).astype(F32)
    edge_pad[:, DRAFT - KCONV + 1 :] = edge_inner[...].astype(F32)
    edges = edge_pad[...]
    conv = conv_rows(
        inner.astype(F32).reshape(count, DRAFT, TILE),
        edges,
        taps_inner[...].astype(F32),
        vector_tile[1:2],
    )
    x = silu(conv).reshape(rows, TILE).astype(BF16).astype(F32)
    first_head = step * (TILE // HEAD_DIM)
    spread = (
        iota((heads, TILE), 0) == first_head + (iota((heads, TILE), 1) >> 6)
    ).astype(BF16)
    expanded = mm(quant[0], spread) + mm(quant[1], spread) + mm(quant[2], spread)
    level = expanded[:rows]
    weighted = expanded[rows : 2 * rows] * x
    past = jnp.concatenate(
        [
            mm_t(cmat[r * DRAFT : (r + 1) * DRAFT].astype(BF16), states[r])
            for r in range(count)
        ],
        axis=0,
    )
    out = jnp.exp(level) * past + expanded[4 * rows : 4 * rows + 1] * x
    level3 = level.reshape(count, DRAFT, TILE)
    weighted3 = weighted.reshape(count, DRAFT, TILE)
    total = jnp.zeros((count, DRAFT, TILE), F32)
    for u in range(DRAFT):
        factor = jnp.exp(jnp.minimum(level3 - level3[:, u : u + 1], 0.0))
        share = gmat[:, u : u + 1].reshape(count, DRAFT, 1)
        total = total + share * factor * weighted3[:, u : u + 1]
    out = (out + total.reshape(rows, TILE)).astype(BF16).astype(F32)
    gated = out * silu(gate)
    squared = gated * gated
    squares[...] += squared[:, :128] + squared[:, 128:]
    acc[...] += mm((gated * vector_tile[2:3]).astype(BF16), w_out[...])
    delta = expanded[2 * rows : 3 * rows] * x
    decay = expanded[3 * rows : 4 * rows]
    decay_hi = decay.astype(BF16).astype(F32)
    second = mm(select[0], inner) + mm(select[1], edges.reshape(rows, TILE).astype(BF16))
    place = iota((rows, TILE), 0) & 7
    second = jnp.where(
        place == 3, decay_hi, jnp.where(place == 4, decay - decay_hi, second)
    )
    for r in range(count):
        span = slice(r * DRAFT, (r + 1) * DRAFT)
        boxes[table[0, r]] = jnp.concatenate([delta[span], second[span]], axis=0).astype(BF16)
    here = pl.ds(pl.multiple_of(step * TILE, TILE), TILE)
    for k in range(WINDOW):
        corr[k][:, here] = boxes[k]

    @pl.when(step == last)
    def _():
        total_square = jnp.broadcast_to(
            jnp.sum(squares[...], axis=1, keepdims=True), squares.shape
        )
        mine[:, half:] = total_square
        theirs[:, half:] = total_square

        @pl.when(table[2, 0] == 0)
        def _():
            mine[:, :half] = acc[:, :half]
            theirs[:, :half] = acc[:, half:]

        @pl.when(table[2, 0] != 0)
        def _():
            mine[:, :half] = acc[:, half:]
            theirs[:, :half] = acc[:, :half]


def front(count, heads, width, depth, args):
    rows = count * DRAFT
    tiles = width // TILE

    def whole(shape):
        return pl.BlockSpec(shape, lambda j: (0,) * len(shape))

    in_specs = [
        *[pl.BlockSpec(memory_space=pltpu.SMEM)] * 3,
        whole((2, rows, depth // 2)),
        whole((3, depth)),
        pl.BlockSpec((depth, TILE), lambda j: (0, j)),
        pl.BlockSpec((depth, TILE), lambda j: (0, j)),
        pl.BlockSpec((TILE, depth), lambda j: (j, 0)),
        whole((2, depth, NSTATE)),
        whole((heads, depth)),
        whole((3, heads)),
        pl.BlockSpec((KCONV, TILE), lambda j: (0, j)),
        pl.BlockSpec((3, TILE), lambda j: (0, j)),
        whole((KCONV, 2 * NSTATE)),
        whole((1, 2 * NSTATE)),
        pl.BlockSpec((count, TILE, NSTATE), lambda j: (0, j, 0)),
        pl.BlockSpec((count, KCONV - 1, TILE), lambda j: (0, 0, j)),
        whole((count, KCONV - 1, 2 * NSTATE)),
    ]
    out_width = depth // 2 + 128
    out_shape = [jax.ShapeDtypeStruct((rows, out_width), F32)] * 2 + [
        jax.ShapeDtypeStruct((2 * DRAFT, width + EXTRA), BF16)
    ] * WINDOW
    out_specs = [whole((rows, out_width))] * 2 + [whole((2 * DRAFT, width + EXTRA))] * WINDOW
    return pl.pallas_call(
        functools.partial(front_kernel, count, heads),
        grid=(tiles,),
        in_specs=in_specs,
        out_specs=out_specs,
        out_shape=out_shape,
        scratch_shapes=[
            pltpu.VMEM((rows, depth), BF16),
            pltpu.VMEM((rows, depth), F32),
            pltpu.VMEM((rows, 128), F32),
            pltpu.VMEM((3, 4 * rows + 16, heads), BF16),
            pltpu.VMEM((rows, NSTATE), F32),
            pltpu.VMEM((rows, NSTATE), F32),
            pltpu.VMEM((2, rows, rows), BF16),
            pltpu.VMEM((WINDOW, 2 * DRAFT, TILE), BF16),
            pltpu.VMEM((count, DRAFT, TILE), F32),
        ],
        compiler_params=pltpu.CompilerParams(dimension_semantics=("arbitrary",)),
        cost_estimate=SMALL,
        name="front",
    )(*args)


def pick_kernel(count, peers, destination, states, *outs):
    picked = outs[: len(RAW)]
    table, sems = outs[len(RAW) :]
    here = lax.axis_index("req")
    reach = [
        lax.rem(lax.div(destination[r], count) - here + peers, peers) for r in range(count)
    ]
    index = []
    for k in range(WINDOW):
        index.append(sum((reach[r] == k).astype(jnp.int32) * r for r in range(count)))
        table[3, k] = index[k]
    copies = []
    for n, k in enumerate(RAW):
        copy = pltpu.make_async_copy(states.at[index[k]], picked[n], sems.at[n])
        copy.start()
        copies.append(copy)
    for r in range(count):
        table[0, r] = reach[r]
        table[1, r] = lax.rem(destination[r], count)
        table[2, r] = lax.axis_index("head")
    for copy in copies:
        copy.wait()


def in_hbm():
    return pl.BlockSpec(memory_space=pl.ANY)


def in_vmem():
    return pl.BlockSpec(memory_space=pltpu.VMEM)


def in_smem():
    return pl.BlockSpec(memory_space=pltpu.SMEM)


def pick(count, width, peers, destination, states):
    return pl.pallas_call(
        functools.partial(pick_kernel, count, peers),
        in_specs=[in_smem(), in_hbm()],
        out_specs=[in_vmem()] * len(RAW) + [in_smem()],
        out_shape=[jax.ShapeDtypeStruct((width, NSTATE), BF16)] * len(RAW)
        + [jax.ShapeDtypeStruct((4, max(count, WINDOW)), jnp.int32)],
        scratch_shapes=[pltpu.SemaphoreType.DMA((len(RAW),))],
        cost_estimate=SMALL,
        name="pick",
    )(destination, states)


def advance(corr, state, out):
    width = state.shape[0]
    line = iota((2 * DRAFT, NSTATE), 0)
    bmat = jnp.where(line < DRAFT, corr[:, width:].astype(F32), 0.0)
    ones = jnp.where((line == 11) | (line == 12), 1.0, 0.0)
    right = jnp.concatenate([bmat, ones], axis=1).astype(BF16)
    part = width // PARTS
    for c in range(PARTS):
        span = slice(c * part, (c + 1) * part)
        both = lax.dot_general(
            corr[:, span], right, (((0,), (0,)), ((), ())), preferred_element_type=F32
        )
        out[span] = (both[:, NSTATE:] * state[span].astype(F32) + both[:, :NSTATE]).astype(BF16)


def tail_rows(width):
    tiles = width // NSTATE
    groups = tiles // 2 + 1
    return groups, (groups + groups % 2) * DRAFT


def finish_kernel(offsets, *refs):
    n = len(offsets)
    table, states = refs[:2]
    corr = refs[2 : 2 + n]
    outs = refs[2 + n : 2 + 2 * n]
    loaded, sems = refs[-2:]
    width = loaded.shape[1]
    groups, _ = tail_rows(width)
    copies = []
    for i, k in enumerate(offsets):
        copy = pltpu.make_async_copy(states.at[table[3, k]], loaded.at[i], sems.at[i])
        copy.start()
        copies.append(copy)
    for i in range(n):
        low = corr[i][...].astype(F32)[DRAFT:]
        half = iota((DRAFT, NSTATE), 0) < DRAFT // 2
        tiles = [low[:, t * NSTATE : (t + 1) * NSTATE] for t in range(width // NSTATE + 1)]
        packed = [
            jnp.where(half, tiles[2 * g], pltpu.roll(tiles[2 * g + 1], DRAFT // 2, 0))
            for g in range(groups - 1)
        ]
        packed.append(tiles[-1])
        if groups % 2:
            packed.append(jnp.zeros((DRAFT, NSTATE), F32))
        for g in range(0, len(packed), 2):
            block = jnp.concatenate(packed[g : g + 2], axis=0)
            outs[i][width + g * DRAFT : width + (g + 2) * DRAFT] = block.astype(BF16)
        copies[i].wait()
        advance(corr[i], loaded.at[i], outs[i])


def finish(offsets, table, states, corr):
    n = len(offsets)
    width = states.shape[1]
    shape = jax.ShapeDtypeStruct((width + tail_rows(width)[1], NSTATE), BF16)
    return pl.pallas_call(
        functools.partial(finish_kernel, offsets),
        in_specs=[in_smem(), in_hbm()] + [in_vmem()] * n,
        out_specs=[in_vmem()] * n,
        out_shape=[shape] * n,
        scratch_shapes=[
            pltpu.VMEM((n, width, NSTATE), BF16),
            pltpu.SemaphoreType.DMA((n,)),
        ],
        cost_estimate=SMALL,
        compiler_params=pltpu.CompilerParams(vmem_limit_bytes=ROOM),
        name="finish",
    )(table, states, *[corr[k] for k in offsets])


def mark_of(low):
    return jnp.max(low[6:7]).astype(jnp.int32) - 1


def merge_kernel(own, *refs):
    table, states = refs[:2]
    raw = refs[2]
    corr = refs[3 : 4 + own]
    _, kept, loaded, merged, sem_in, sem_out = refs[4 + own :]
    width = loaded.shape[0]
    if own:
        copy = pltpu.make_async_copy(states.at[table[3, 0]], loaded, sem_in)
        copy.start()
    slots = [mark_of(ref[:, width:].astype(F32)[DRAFT:]) for ref in corr]

    def put(i):
        return pltpu.make_async_copy(merged.at[i], kept.at[slots[i]], sem_out.at[i])

    for i in range(1 + own):
        if i == 1:
            copy.wait()

        @pl.when(slots[i] >= 0)
        def _(i=i):
            advance(corr[i], loaded if i == 1 else raw, merged.at[i])
            put(i).start()

    for i in range(1 + own):

        @pl.when(slots[i] >= 0)
        def _(i=i):
            put(i).wait()


def merge(count, table, states, raw, corr, kept):
    width = states.shape[1]
    n = len(corr)
    return pl.pallas_call(
        functools.partial(merge_kernel, n - 1),
        in_specs=[in_smem(), in_hbm()] + [in_vmem()] * (1 + n) + [in_hbm()],
        out_specs=in_hbm(),
        out_shape=jax.ShapeDtypeStruct((count, width, NSTATE), BF16),
        scratch_shapes=[
            pltpu.VMEM((width, NSTATE), BF16),
            pltpu.VMEM((n, width, NSTATE), BF16),
            pltpu.SemaphoreType.DMA,
            pltpu.SemaphoreType.DMA((n,)),
        ],
        input_output_aliases={3 + n: 0},
        cost_estimate=SMALL,
        compiler_params=pltpu.CompilerParams(vmem_limit_bytes=ROOM),
        name="merge",
    )(table, states, raw, *corr, kept)


def halves(ref, width):
    groups, _ = tail_rows(width)
    tiles = []
    for row in range(width, ref.shape[0], 2 * DRAFT):
        block = ref[row : row + 2 * DRAFT].astype(F32)
        for part in (block[:DRAFT], block[DRAFT:]):
            if len(tiles) < 2 * (groups - 1):
                tiles += [part, pltpu.roll(part, DRAFT // 2, 0)]
            else:
                tiles.append(part)
    return tiles[: 2 * groups - 1]


def place_kernel(n, earlier, *refs):
    messages = refs[:n]
    out = len(refs) - 4
    corr = refs[n : out - 3 * earlier]
    kept, out_inner, out_ssm, sems = refs[out:]
    width = out_inner.shape[2]
    tiles = width // NSTATE
    if earlier:
        out_inner[...] = refs[out - 2][...]
        out_ssm[...] = refs[out - 1][...]
    lows = [halves(ref, width) for ref in messages]
    slots = [mark_of(low[tiles]) for low in lows]

    def put(i):
        return pltpu.make_async_copy(
            messages[i].at[pl.ds(0, width)], kept.at[slots[i]], sems.at[i]
        )

    for i in range(n):

        @pl.when(slots[i] >= 0)
        def _(i=i):
            put(i).start()

    def write_edges(slot, inner, low):
        out_inner[slot] = inner[: KCONV - 1].astype(BF16)
        high = pltpu.roll(low, DRAFT - 3, 0)
        out_ssm[slot] = jnp.concatenate([low[:3], high[:3]], axis=1).astype(BF16)

    for ref in corr:
        low = ref[...].astype(F32)[DRAFT:]
        slot = mark_of(low[:, width:])

        @pl.when(slot >= 0)
        def _(slot=slot, low=low):
            write_edges(slot, low[:, :width], low[:, width:])

    for i in range(n):

        @pl.when(slots[i] >= 0)
        def _(i=i):
            write_edges(slots[i], jnp.concatenate(lows[i][:tiles], axis=1), lows[i][tiles])

    for i in range(n):

        @pl.when(slots[i] >= 0)
        def _(i=i):
            put(i).wait()


def place(count, width, messages, corr, earlier=()):
    n = len(messages)
    inputs = [*messages, *corr]
    return pl.pallas_call(
        functools.partial(place_kernel, n, 1 if earlier else 0),
        in_specs=[in_vmem()] * len(inputs)
        + ([in_hbm(), in_vmem(), in_vmem()] if earlier else []),
        out_specs=[in_hbm(), in_vmem(), in_vmem()],
        out_shape=[
            jax.ShapeDtypeStruct((count, width, NSTATE), BF16),
            jax.ShapeDtypeStruct((count, KCONV - 1, width), BF16),
            jax.ShapeDtypeStruct((count, KCONV - 1, 2 * NSTATE), BF16),
        ],
        input_output_aliases={len(inputs): 0} if earlier else {},
        scratch_shapes=[pltpu.SemaphoreType.DMA((n,))],
        cost_estimate=SMALL,
        compiler_params=pltpu.CompilerParams(vmem_limit_bytes=ROOM),
        name="place",
    )(*inputs, *earlier)


def moved(array, by):
    length = lax.axis_size("req")
    return lax.ppermute(array, "req", [(i, (i + by) % length) for i in range(length)])


def local(
    hidden_in,
    norm_gain,
    proj_gate,
    proj_inner,
    proj_ssm,
    proj_step,
    step_bias,
    decay_log,
    skip_gain,
    conv_inner,
    conv_inner_bias,
    conv_ssm,
    conv_ssm_bias,
    gate_gain,
    proj_out,
    states_in,
    edge_inner,
    edge_ssm,
    draft_lengths,
    accepted,
    destination,
):
    count, heads = states_in.shape[:2]
    depth, width = proj_inner.shape
    peers = lax.axis_size("req")
    flat = states_in.reshape(count, width, NSTATE)
    *raws, table = pick(count, width, peers, destination, flat)
    raws = [moved(raw, k) for raw, k in zip(raws, RAW)]
    table, ready, ready_ssm = lax.optimization_barrier((table, hidden_in, proj_ssm))
    vectors = jnp.stack([norm_gain, conv_inner_bias, gate_gain])
    results = front(
        count,
        heads,
        width,
        depth,
        (
            table,
            draft_lengths,
            accepted,
            lax.all_gather(ready, "head", axis=0, tiled=False),
            vectors,
            proj_gate,
            proj_inner,
            proj_out,
            lax.all_gather(ready_ssm, "head", axis=0, tiled=False),
            proj_step.T,
            jnp.stack([step_bias, decay_log, skip_gain]),
            conv_inner,
            vectors,
            conv_ssm,
            conv_ssm_bias.reshape(1, 2 * NSTATE),
            flat,
            edge_inner,
            edge_ssm,
        ),
    )
    mine, theirs = results[:2]
    corr = list(results[2:])
    sixth, fifth, fourth, third = finish((6, 5, 4, 3), table, flat, corr)
    *raws, corr[7], sixth, fifth, fourth, third, later = lax.optimization_barrier(
        (*raws, corr[7], sixth, fifth, fourth, third, table)
    )
    sixth = moved(sixth, 6)
    fifth = moved(fifth, 5)
    fourth = moved(fourth, 4)
    third = moved(third, 3)
    corr[7] = moved(corr[7], 7)
    (first,) = finish((1,), later, flat, corr)

    pair = lax.all_gather(theirs, "head", axis=0, tiled=False)
    other = jnp.where(lax.axis_index("head") == 0, pair[1], pair[0])
    total = mine + other
    half = depth // 2
    scale = lax.rsqrt(total[:, half : half + 1] / DINNER + epsilon)
    hidden_out = (hidden_in.astype(F32) + total[:, :half] * scale).astype(BF16)

    corr[7], corr[2] = lax.optimization_barrier((corr[7], corr[2]))
    corr[2] = moved(corr[2], 2)
    sixth, fifth, fourth, third, corr[7], first = lax.optimization_barrier(
        (sixth, fifth, fourth, third, corr[7], first)
    )
    first = moved(first, 1)
    kept, edges, edges_ssm = place(
        count, width, (sixth, fifth, fourth, third), (corr[0], corr[7])
    )
    kept = merge(count, table, flat, raws[0], (corr[7], corr[0]), kept)
    kept = merge(count, table, flat, raws[1], (corr[2],), kept)
    kept, kept_inner, kept_ssm = place(
        count, width, (first,), (corr[2],), (kept, edges, edges_ssm)
    )
    return (hidden_out, kept.reshape(states_in.shape), kept_inner, kept_ssm)


def solution(mesh):
    in_specs = (
        P("req", "head"),
        P(),
        P(None, "head"),
        P(None, "head"),
        P(None, "head"),
        P(None, "head"),
        P("head"),
        P("head"),
        P("head"),
        P(None, "head"),
        P("head"),
        P(),
        P(),
        P("head"),
        P("head", None),
        P("req", "head", None, None),
        P("req", None, "head"),
        P("req", None, None),
        P("req"),
        P("req"),
        P("req"),
    )
    out_specs = (
        P("req", "head"),
        P("req", "head", None, None),
        P("req", None, "head"),
        P("req", None, None),
    )
    return jax.shard_map(local, mesh=mesh, in_specs=in_specs, out_specs=out_specs, check_vma=False)
```

```python
import functools

import jax
import jax.numpy as jnp
from jax import lax
from jax.experimental import pallas as pl
from jax.experimental.pallas import tpu as pltpu
from jax.sharding import PartitionSpec as P

HEAD_DIM = 64
NSTATE = 128
KCONV = 4
DRAFT = 8
WINDOW = 8
DINNER = 3072
TILE = 256
EXTRA = NSTATE
RAW = (7, 2)
PARTS = 3
ROOM = 12 * 1024 * 1024
SMALL = pl.CostEstimate(flops=1024, bytes_accessed=1024, transcendentals=0)

epsilon = 1e-05
HIGH = lax.Precision.HIGHEST
F32 = jnp.float32
BF16 = jnp.bfloat16


def iota(shape, axis):
    return lax.broadcasted_iota(jnp.int32, shape, axis)


def mm(a, b, precision=None):
    return jnp.dot(a, b, preferred_element_type=F32, precision=precision)


def mm_t(a, b):
    return lax.dot_general(a, b, (((1,), (1,)), ((), ())), preferred_element_type=F32)


def silu(x):
    return x * (1.0 / (1.0 + jnp.exp(-x)))


def conv_rows(rows, edges, taps, bias):
    slot = iota(rows.shape, 1)
    total = bias + taps[KCONV - 1 : KCONV] * rows
    for back in range(1, KCONV):
        mixed = jnp.where(slot >= DRAFT - back, edges, rows)
        total = total + taps[KCONV - 1 - back : KCONV - back] * pltpu.roll(mixed, back, 1)
    return total


def front_kernel(
    count,
    heads,
    table,
    lengths_in,
    accepted_in,
    hidden,
    vectors,
    w_gate,
    w_inner,
    w_out,
    w_ssm,
    w_step,
    head_rows,
    taps_inner,
    vector_tile,
    taps_ssm,
    bias_ssm,
    states,
    edge_inner,
    edge_ssm,
    mine,
    theirs,
    *rest,
):
    corr = rest[:WINDOW]
    normed, acc, squares, quant, gmat, cmat, select, boxes, edge_pad = rest[WINDOW:]
    step = pl.program_id(0)
    last = pl.num_programs(0) - 1
    rows = count * DRAFT
    width = acc.shape[1]
    half = width // 2

    @pl.when(step == 0)
    def _():
        wide = jnp.concatenate([hidden[0], hidden[1]], axis=1).astype(F32)
        scale = lax.rsqrt(jnp.mean(wide * wide, axis=-1, keepdims=True) + epsilon)
        norm = (wide * scale * vectors[0:1]).astype(BF16)
        normed[...] = norm
        acc[...] = jnp.zeros_like(acc)
        squares[...] = jnp.zeros_like(squares)
        boxes[...] = jnp.zeros_like(boxes)
        edge_pad[...] = jnp.zeros_like(edge_pad)
        edge_pad[:, DRAFT - KCONV + 1 :] = edge_ssm[...].astype(F32)
        row = iota((rows, rows), 0)
        col = iota((rows, rows), 1)
        request = row >> 3
        taken = jnp.zeros((rows, rows), jnp.int32)
        for r in range(count):
            taken = jnp.where(request == r, accepted_in[r], taken)
        same = request == (col >> 3)
        lower = same & ((col & 7) <= (row & 7))
        before = same & ((col & 7) < taken)
        raw = mm_t(norm, w_step[...]).astype(BF16).astype(F32) + head_rows[0:1]
        lengths = jnp.zeros((rows, heads), jnp.int32)
        chosen = jnp.zeros((rows, heads), jnp.int32)
        hrow = iota((rows, heads), 0)
        for r in range(count):
            lengths = jnp.where((hrow >> 3) == r, lengths_in[r], lengths)
            chosen = jnp.where((hrow >> 3) == r, accepted_in[r], chosen)
        soft = jnp.maximum(raw, 0.0) + jnp.log1p(jnp.exp(-jnp.abs(raw)))
        size = jnp.where((hrow & 7) < lengths, soft, 0.0)
        rate = -jnp.exp(head_rows[1:2])
        cum = mm(lower.astype(F32), size, HIGH)
        upto = mm(before.astype(F32), size, HIGH)
        weight = jnp.where(
            (hrow & 7) < chosen, jnp.exp(jnp.minimum(rate * (upto - cum), 0.0)) * size, 0.0
        )
        stacked = jnp.concatenate(
            [
                rate * cum,
                size,
                weight,
                jnp.exp(rate * upto),
                jnp.broadcast_to(head_rows[2:3], (16, heads)),
            ],
            axis=0,
        )
        for part in range(3):
            piece = stacked.astype(BF16)
            quant[part] = piece
            stacked = stacked - piece.astype(F32)
        sel_rows = jnp.where(
            same & ((row & 7) < KCONV - 1),
            ((col & 7) == (row & 7) + taken - 3).astype(F32),
            0.0,
        ).astype(BF16)
        sel_edge = jnp.where(
            same & ((row & 7) < KCONV - 1),
            ((col & 7) == (row & 7) + taken + 5).astype(F32),
            0.0,
        ).astype(BF16)
        select[0] = sel_rows
        select[1] = sel_edge
        ssm = jnp.concatenate([mm(norm, w_ssm[0]), mm(norm, w_ssm[1])], axis=1).astype(BF16)
        before_ssm = edge_pad[...]
        conv = conv_rows(
            ssm.astype(F32).reshape(count, DRAFT, 2 * NSTATE),
            before_ssm,
            taps_ssm[...].astype(F32),
            bias_ssm[...],
        )
        both = silu(conv).reshape(rows, 2 * NSTATE).astype(BF16)
        bmat = both[:, :NSTATE]
        cvec = both[:, NSTATE:]
        cmat[...] = cvec.astype(F32)
        pair = jnp.where(lower, mm_t(cvec, bmat), 0.0)
        fold = ((iota((rows, NSTATE), 0) & 7) == iota((rows, NSTATE), 1)).astype(F32)
        gmat[...] = mm(pair, fold, HIGH)
        kept = mm(sel_rows, ssm) + mm(
            sel_edge, before_ssm.reshape(rows, 2 * NSTATE).astype(BF16)
        )
        wide_b = bmat.astype(F32)
        place = iota((DRAFT, NSTATE), 0)
        for r in range(count):
            own = kept[r * DRAFT : (r + 1) * DRAFT]
            packed = jnp.where(
                place < 3,
                own[:, :NSTATE],
                jnp.where(
                    place < 6,
                    pltpu.roll(own[:, NSTATE:], 3, 0),
                    jnp.full((DRAFT, NSTATE), (table[1, r] + 1).astype(F32)),
                ),
            )
            boxes[table[0, r], :, :NSTATE] = jnp.concatenate(
                [wide_b[r * DRAFT : (r + 1) * DRAFT], packed], axis=0
            ).astype(BF16)
        for k in range(WINDOW):
            corr[k][:, width:] = boxes[k, :, :NSTATE]

    norm = normed[...]
    inner = mm(norm, w_inner[...]).astype(BF16)
    gate = mm(norm, w_gate[...]).astype(BF16).astype(F32)
    edge_pad[:, DRAFT - KCONV + 1 :] = edge_inner[...].astype(F32)
    edges = edge_pad[...]
    conv = conv_rows(
        inner.astype(F32).reshape(count, DRAFT, TILE),
        edges,
        taps_inner[...].astype(F32),
        vector_tile[1:2],
    )
    x = silu(conv).reshape(rows, TILE).astype(BF16).astype(F32)
    first_head = step * (TILE // HEAD_DIM)
    spread = (
        iota((heads, TILE), 0) == first_head + (iota((heads, TILE), 1) >> 6)
    ).astype(BF16)
    expanded = mm(quant[0], spread) + mm(quant[1], spread) + mm(quant[2], spread)
    level = expanded[:rows]
    weighted = expanded[rows : 2 * rows] * x
    past = jnp.concatenate(
        [
            mm_t(cmat[r * DRAFT : (r + 1) * DRAFT].astype(BF16), states[r])
            for r in range(count)
        ],
        axis=0,
    )
    out = jnp.exp(level) * past + expanded[4 * rows : 4 * rows + 1] * x
    level3 = level.reshape(count, DRAFT, TILE)
    weighted3 = weighted.reshape(count, DRAFT, TILE)
    total = jnp.zeros((count, DRAFT, TILE), F32)
    for u in range(DRAFT):
        factor = jnp.exp(jnp.minimum(level3 - level3[:, u : u + 1], 0.0))
        share = gmat[:, u : u + 1].reshape(count, DRAFT, 1)
        total = total + share * factor * weighted3[:, u : u + 1]
    out = (out + total.reshape(rows, TILE)).astype(BF16).astype(F32)
    gated = out * silu(gate)
    squared = gated * gated
    squares[...] += squared[:, :128] + squared[:, 128:]
    acc[...] += mm((gated * vector_tile[2:3]).astype(BF16), w_out[...])
    delta = expanded[2 * rows : 3 * rows] * x
    decay = expanded[3 * rows : 4 * rows]
    decay_hi = decay.astype(BF16).astype(F32)
    second = mm(select[0], inner) + mm(select[1], edges.reshape(rows, TILE).astype(BF16))
    place = iota((rows, TILE), 0) & 7
    second = jnp.where(
        place == 3, decay_hi, jnp.where(place == 4, decay - decay_hi, second)
    )
    for r in range(count):
        span = slice(r * DRAFT, (r + 1) * DRAFT)
        boxes[table[0, r]] = jnp.concatenate([delta[span], second[span]], axis=0).astype(BF16)
    here = pl.ds(pl.multiple_of(step * TILE, TILE), TILE)
    for k in range(WINDOW):
        corr[k][:, here] = boxes[k]

    @pl.when(step == last)
    def _():
        total_square = jnp.broadcast_to(
            jnp.sum(squares[...], axis=1, keepdims=True), squares.shape
        )
        mine[:, half:] = total_square
        theirs[:, half:] = total_square

        @pl.when(table[2, 0] == 0)
        def _():
            mine[:, :half] = acc[:, :half]
            theirs[:, :half] = acc[:, half:]

        @pl.when(table[2, 0] != 0)
        def _():
            mine[:, :half] = acc[:, half:]
            theirs[:, :half] = acc[:, :half]


def front(count, heads, width, depth, args):
    rows = count * DRAFT
    tiles = width // TILE

    def whole(shape):
        return pl.BlockSpec(shape, lambda j: (0,) * len(shape))

    in_specs = [
        *[pl.BlockSpec(memory_space=pltpu.SMEM)] * 3,
        whole((2, rows, depth // 2)),
        whole((3, depth)),
        pl.BlockSpec((depth, TILE), lambda j: (0, j)),
        pl.BlockSpec((depth, TILE), lambda j: (0, j)),
        pl.BlockSpec((TILE, depth), lambda j: (j, 0)),
        whole((2, depth, NSTATE)),
        whole((heads, depth)),
        whole((3, heads)),
        pl.BlockSpec((KCONV, TILE), lambda j: (0, j)),
        pl.BlockSpec((3, TILE), lambda j: (0, j)),
        whole((KCONV, 2 * NSTATE)),
        whole((1, 2 * NSTATE)),
        pl.BlockSpec((count, TILE, NSTATE), lambda j: (0, j, 0)),
        pl.BlockSpec((count, KCONV - 1, TILE), lambda j: (0, 0, j)),
        whole((count, KCONV - 1, 2 * NSTATE)),
    ]
    out_width = depth // 2 + 128
    out_shape = [jax.ShapeDtypeStruct((rows, out_width), F32)] * 2 + [
        jax.ShapeDtypeStruct((2 * DRAFT, width + EXTRA), BF16)
    ] * WINDOW
    out_specs = [whole((rows, out_width))] * 2 + [whole((2 * DRAFT, width + EXTRA))] * WINDOW
    return pl.pallas_call(
        functools.partial(front_kernel, count, heads),
        grid=(tiles,),
        in_specs=in_specs,
        out_specs=out_specs,
        out_shape=out_shape,
        scratch_shapes=[
            pltpu.VMEM((rows, depth), BF16),
            pltpu.VMEM((rows, depth), F32),
            pltpu.VMEM((rows, 128), F32),
            pltpu.VMEM((3, 4 * rows + 16, heads), BF16),
            pltpu.VMEM((rows, NSTATE), F32),
            pltpu.VMEM((rows, NSTATE), F32),
            pltpu.VMEM((2, rows, rows), BF16),
            pltpu.VMEM((WINDOW, 2 * DRAFT, TILE), BF16),
            pltpu.VMEM((count, DRAFT, TILE), F32),
        ],
        compiler_params=pltpu.CompilerParams(dimension_semantics=("arbitrary",)),
        cost_estimate=SMALL,
        name="front",
    )(*args)


def pick_kernel(count, peers, destination, states, *outs):
    picked = outs[: len(RAW)]
    table, sems = outs[len(RAW) :]
    here = lax.axis_index("req")
    reach = [
        lax.rem(lax.div(destination[r], count) - here + peers, peers) for r in range(count)
    ]
    index = []
    for k in range(WINDOW):
        index.append(sum((reach[r] == k).astype(jnp.int32) * r for r in range(count)))
        table[3, k] = index[k]
    copies = []
    for n, k in enumerate(RAW):
        copy = pltpu.make_async_copy(states.at[index[k]], picked[n], sems.at[n])
        copy.start()
        copies.append(copy)
    for r in range(count):
        table[0, r] = reach[r]
        table[1, r] = lax.rem(destination[r], count)
        table[2, r] = lax.axis_index("head")
    for copy in copies:
        copy.wait()


def in_hbm():
    return pl.BlockSpec(memory_space=pl.ANY)


def in_vmem():
    return pl.BlockSpec(memory_space=pltpu.VMEM)


def in_smem():
    return pl.BlockSpec(memory_space=pltpu.SMEM)


def pick(count, width, peers, destination, states):
    return pl.pallas_call(
        functools.partial(pick_kernel, count, peers),
        in_specs=[in_smem(), in_hbm()],
        out_specs=[in_vmem()] * len(RAW) + [in_smem()],
        out_shape=[jax.ShapeDtypeStruct((width, NSTATE), BF16)] * len(RAW)
        + [jax.ShapeDtypeStruct((4, max(count, WINDOW)), jnp.int32)],
        scratch_shapes=[pltpu.SemaphoreType.DMA((len(RAW),))],
        cost_estimate=SMALL,
        name="pick",
    )(destination, states)


def advance(corr, state, out):
    width = state.shape[0]
    line = iota((2 * DRAFT, NSTATE), 0)
    bmat = jnp.where(line < DRAFT, corr[:, width:].astype(F32), 0.0)
    ones = jnp.where((line == 11) | (line == 12), 1.0, 0.0)
    right = jnp.concatenate([bmat, ones], axis=1).astype(BF16)
    part = width // PARTS
    for c in range(PARTS):
        span = slice(c * part, (c + 1) * part)
        both = lax.dot_general(
            corr[:, span], right, (((0,), (0,)), ((), ())), preferred_element_type=F32
        )
        out[span] = (both[:, NSTATE:] * state[span].astype(F32) + both[:, :NSTATE]).astype(BF16)


def tail_rows(width):
    tiles = width // NSTATE
    groups = tiles // 2 + 1
    return groups, (groups + groups % 2) * DRAFT


def finish_kernel(offsets, *refs):
    n = len(offsets)
    table, states = refs[:2]
    corr = refs[2 : 2 + n]
    outs = refs[2 + n : 2 + 2 * n]
    loaded, sems = refs[-2:]
    width = loaded.shape[1]
    groups, _ = tail_rows(width)
    copies = []
    for i, k in enumerate(offsets):
        copy = pltpu.make_async_copy(states.at[table[3, k]], loaded.at[i], sems.at[i])
        copy.start()
        copies.append(copy)
    for i in range(n):
        low = corr[i][...].astype(F32)[DRAFT:]
        half = iota((DRAFT, NSTATE), 0) < DRAFT // 2
        tiles = [low[:, t * NSTATE : (t + 1) * NSTATE] for t in range(width // NSTATE + 1)]
        packed = [
            jnp.where(half, tiles[2 * g], pltpu.roll(tiles[2 * g + 1], DRAFT // 2, 0))
            for g in range(groups - 1)
        ]
        packed.append(tiles[-1])
        if groups % 2:
            packed.append(jnp.zeros((DRAFT, NSTATE), F32))
        for g in range(0, len(packed), 2):
            block = jnp.concatenate(packed[g : g + 2], axis=0)
            outs[i][width + g * DRAFT : width + (g + 2) * DRAFT] = block.astype(BF16)
        copies[i].wait()
        advance(corr[i], loaded.at[i], outs[i])


def finish(offsets, table, states, corr):
    n = len(offsets)
    width = states.shape[1]
    shape = jax.ShapeDtypeStruct((width + tail_rows(width)[1], NSTATE), BF16)
    return pl.pallas_call(
        functools.partial(finish_kernel, offsets),
        in_specs=[in_smem(), in_hbm()] + [in_vmem()] * n,
        out_specs=[in_vmem()] * n,
        out_shape=[shape] * n,
        scratch_shapes=[
            pltpu.VMEM((n, width, NSTATE), BF16),
            pltpu.SemaphoreType.DMA((n,)),
        ],
        cost_estimate=SMALL,
        name="finish",
    )(table, states, *[corr[k] for k in offsets])


def mark_of(low):
    return jnp.max(low[6:7]).astype(jnp.int32) - 1


def merge_kernel(own, *refs):
    table, states = refs[:2]
    raw = refs[2]
    corr = refs[3 : 4 + own]
    _, kept, loaded, merged, sem_in, sem_out = refs[4 + own :]
    width = loaded.shape[0]
    if own:
        copy = pltpu.make_async_copy(states.at[table[3, 0]], loaded, sem_in)
        copy.start()
    slots = [mark_of(ref[:, width:].astype(F32)[DRAFT:]) for ref in corr]

    def put(i):
        return pltpu.make_async_copy(merged.at[i], kept.at[slots[i]], sem_out.at[i])

    for i in range(1 + own):
        if i == 1:
            copy.wait()

        @pl.when(slots[i] >= 0)
        def _(i=i):
            advance(corr[i], loaded if i == 1 else raw, merged.at[i])
            put(i).start()

    for i in range(1 + own):

        @pl.when(slots[i] >= 0)
        def _(i=i):
            put(i).wait()


def merge(count, table, states, raw, corr, kept):
    width = states.shape[1]
    n = len(corr)
    return pl.pallas_call(
        functools.partial(merge_kernel, n - 1),
        in_specs=[in_smem(), in_hbm()] + [in_vmem()] * (1 + n) + [in_hbm()],
        out_specs=in_hbm(),
        out_shape=jax.ShapeDtypeStruct((count, width, NSTATE), BF16),
        scratch_shapes=[
            pltpu.VMEM((width, NSTATE), BF16),
            pltpu.VMEM((n, width, NSTATE), BF16),
            pltpu.SemaphoreType.DMA,
            pltpu.SemaphoreType.DMA((n,)),
        ],
        input_output_aliases={3 + n: 0},
        cost_estimate=SMALL,
        compiler_params=pltpu.CompilerParams(vmem_limit_bytes=ROOM),
        name="merge",
    )(table, states, raw, *corr, kept)


def halves(ref, width):
    groups, _ = tail_rows(width)
    tiles = []
    for row in range(width, ref.shape[0], 2 * DRAFT):
        block = ref[row : row + 2 * DRAFT].astype(F32)
        for part in (block[:DRAFT], block[DRAFT:]):
            if len(tiles) < 2 * (groups - 1):
                tiles += [part, pltpu.roll(part, DRAFT // 2, 0)]
            else:
                tiles.append(part)
    return tiles[: 2 * groups - 1]


def place_kernel(n, earlier, *refs):
    messages = refs[:n]
    out = len(refs) - 4
    corr = refs[n : out - 3 * earlier]
    kept, out_inner, out_ssm, sems = refs[out:]
    width = out_inner.shape[2]
    tiles = width // NSTATE
    if earlier:
        out_inner[...] = refs[out - 2][...]
        out_ssm[...] = refs[out - 1][...]
    lows = [halves(ref, width) for ref in messages]
    slots = [mark_of(low[tiles]) for low in lows]

    def put(i):
        return pltpu.make_async_copy(
            messages[i].at[pl.ds(0, width)], kept.at[slots[i]], sems.at[i]
        )

    for i in range(n):

        @pl.when(slots[i] >= 0)
        def _(i=i):
            put(i).start()

    def write_edges(slot, inner, low):
        out_inner[slot] = inner[: KCONV - 1].astype(BF16)
        high = pltpu.roll(low, DRAFT - 3, 0)
        out_ssm[slot] = jnp.concatenate([low[:3], high[:3]], axis=1).astype(BF16)

    for ref in corr:
        low = ref[...].astype(F32)[DRAFT:]
        slot = mark_of(low[:, width:])

        @pl.when(slot >= 0)
        def _(slot=slot, low=low):
            write_edges(slot, low[:, :width], low[:, width:])

    for i in range(n):

        @pl.when(slots[i] >= 0)
        def _(i=i):
            write_edges(slots[i], jnp.concatenate(lows[i][:tiles], axis=1), lows[i][tiles])

    for i in range(n):

        @pl.when(slots[i] >= 0)
        def _(i=i):
            put(i).wait()


def place(count, width, messages, corr, earlier=()):
    n = len(messages)
    inputs = [*messages, *corr]
    return pl.pallas_call(
        functools.partial(place_kernel, n, 1 if earlier else 0),
        in_specs=[in_vmem()] * len(inputs)
        + ([in_hbm(), in_vmem(), in_vmem()] if earlier else []),
        out_specs=[in_hbm(), in_vmem(), in_vmem()],
        out_shape=[
            jax.ShapeDtypeStruct((count, width, NSTATE), BF16),
            jax.ShapeDtypeStruct((count, KCONV - 1, width), BF16),
            jax.ShapeDtypeStruct((count, KCONV - 1, 2 * NSTATE), BF16),
        ],
        input_output_aliases={len(inputs): 0} if earlier else {},
        scratch_shapes=[pltpu.SemaphoreType.DMA((n,))],
        cost_estimate=SMALL,
        compiler_params=pltpu.CompilerParams(vmem_limit_bytes=ROOM),
        name="place",
    )(*inputs, *earlier)


def moved(array, by):
    length = lax.axis_size("req")
    return lax.ppermute(array, "req", [(i, (i + by) % length) for i in range(length)])


def local(
    hidden_in,
    norm_gain,
    proj_gate,
    proj_inner,
    proj_ssm,
    proj_step,
    step_bias,
    decay_log,
    skip_gain,
    conv_inner,
    conv_inner_bias,
    conv_ssm,
    conv_ssm_bias,
    gate_gain,
    proj_out,
    states_in,
    edge_inner,
    edge_ssm,
    draft_lengths,
    accepted,
    destination,
):
    count, heads = states_in.shape[:2]
    depth, width = proj_inner.shape
    peers = lax.axis_size("req")
    flat = states_in.reshape(count, width, NSTATE)
    *raws, table = pick(count, width, peers, destination, flat)
    raws = [moved(raw, k) for raw, k in zip(raws, RAW)]
    table, ready, ready_ssm = lax.optimization_barrier((table, hidden_in, proj_ssm))
    vectors = jnp.stack([norm_gain, conv_inner_bias, gate_gain])
    results = front(
        count,
        heads,
        width,
        depth,
        (
            table,
            draft_lengths,
            accepted,
            lax.all_gather(ready, "head", axis=0, tiled=False),
            vectors,
            proj_gate,
            proj_inner,
            proj_out,
            lax.all_gather(ready_ssm, "head", axis=0, tiled=False),
            proj_step.T,
            jnp.stack([step_bias, decay_log, skip_gain]),
            conv_inner,
            vectors,
            conv_ssm,
            conv_ssm_bias.reshape(1, 2 * NSTATE),
            flat,
            edge_inner,
            edge_ssm,
        ),
    )
    mine, theirs = results[:2]
    corr = list(results[2:])
    sixth, fifth, fourth, third = finish((6, 5, 4, 3), table, flat, corr)
    *raws, corr[7], sixth, fifth, fourth, third, later = lax.optimization_barrier(
        (*raws, corr[7], sixth, fifth, fourth, third, table)
    )
    sixth = moved(sixth, 6)
    fifth = moved(fifth, 5)
    fourth = moved(fourth, 4)
    third = moved(third, 3)
    corr[7] = moved(corr[7], 7)
    (first,) = finish((1,), later, flat, corr)

    pair = lax.all_gather(theirs, "head", axis=0, tiled=False)
    other = jnp.where(lax.axis_index("head") == 0, pair[1], pair[0])
    total = mine + other
    half = depth // 2
    scale = lax.rsqrt(total[:, half : half + 1] / DINNER + epsilon)
    hidden_out = (hidden_in.astype(F32) + total[:, :half] * scale).astype(BF16)

    corr[7], corr[2] = lax.optimization_barrier((corr[7], corr[2]))
    corr[2] = moved(corr[2], 2)
    sixth, fifth, fourth, third, corr[7], first = lax.optimization_barrier(
        (sixth, fifth, fourth, third, corr[7], first)
    )
    first = moved(first, 1)
    kept, edges, edges_ssm = place(
        count, width, (sixth, fifth, fourth, third), (corr[0], corr[7])
    )
    kept = merge(count, table, flat, raws[0], (corr[7], corr[0]), kept)
    kept = merge(count, table, flat, raws[1], (corr[2],), kept)
    kept, kept_inner, kept_ssm = place(
        count, width, (first,), (corr[2],), (kept, edges, edges_ssm)
    )
    return (hidden_out, kept.reshape(states_in.shape), kept_inner, kept_ssm)


def solution(mesh):
    in_specs = (
        P("req", "head"),
        P(),
        P(None, "head"),
        P(None, "head"),
        P(None, "head"),
        P(None, "head"),
        P("head"),
        P("head"),
        P("head"),
        P(None, "head"),
        P("head"),
        P(),
        P(),
        P("head"),
        P("head", None),
        P("req", "head", None, None),
        P("req", None, "head"),
        P("req", None, None),
        P("req"),
        P("req"),
        P("req"),
    )
    out_specs = (
        P("req", "head"),
        P("req", "head", None, None),
        P("req", None, "head"),
        P("req", None, None),
    )
    return jax.shard_map(local, mesh=mesh, in_specs=in_specs, out_specs=out_specs, check_vma=False)
```

```python
import functools

import jax
import jax.numpy as jnp
from jax import lax
from jax.experimental import pallas as pl
from jax.experimental.pallas import tpu as pltpu
from jax.sharding import PartitionSpec as P

HEAD_DIM = 64
NSTATE = 128
KCONV = 4
DRAFT = 8
WINDOW = 8
DINNER = 3072
TILE = 256
EXTRA = NSTATE
RAW = (7, 2)
PARTS = 3
ROOM = 12 * 1024 * 1024
SMALL = pl.CostEstimate(flops=1024, bytes_accessed=1024, transcendentals=0)

epsilon = 1e-05
HIGH = lax.Precision.HIGHEST
F32 = jnp.float32
BF16 = jnp.bfloat16


def iota(shape, axis):
    return lax.broadcasted_iota(jnp.int32, shape, axis)


def mm(a, b, precision=None):
    return jnp.dot(a, b, preferred_element_type=F32, precision=precision)


def mm_t(a, b):
    return lax.dot_general(a, b, (((1,), (1,)), ((), ())), preferred_element_type=F32)


def silu(x):
    return x * (1.0 / (1.0 + jnp.exp(-x)))


def conv_rows(rows, edges, taps, bias):
    slot = iota(rows.shape, 1)
    total = bias + taps[KCONV - 1 : KCONV] * rows
    for back in range(1, KCONV):
        mixed = jnp.where(slot >= DRAFT - back, edges, rows)
        total = total + taps[KCONV - 1 - back : KCONV - back] * pltpu.roll(mixed, back, 1)
    return total


def front_kernel(
    count,
    heads,
    table,
    lengths_in,
    accepted_in,
    hidden,
    vectors,
    w_gate,
    w_inner,
    w_out,
    w_ssm,
    w_step,
    head_rows,
    taps_inner,
    vector_tile,
    taps_ssm,
    bias_ssm,
    states,
    edge_inner,
    edge_ssm,
    mine,
    theirs,
    *rest,
):
    corr = rest[:WINDOW]
    normed, acc, squares, quant, gmat, cmat, select, boxes, edge_pad = rest[WINDOW:]
    step = pl.program_id(0)
    last = pl.num_programs(0) - 1
    rows = count * DRAFT
    width = acc.shape[1]
    half = width // 2

    @pl.when(step == 0)
    def _():
        wide = jnp.concatenate([hidden[0], hidden[1]], axis=1).astype(F32)
        scale = lax.rsqrt(jnp.mean(wide * wide, axis=-1, keepdims=True) + epsilon)
        norm = (wide * scale * vectors[0:1]).astype(BF16)
        normed[...] = norm
        acc[...] = jnp.zeros_like(acc)
        squares[...] = jnp.zeros_like(squares)
        boxes[...] = jnp.zeros_like(boxes)
        edge_pad[...] = jnp.zeros_like(edge_pad)
        edge_pad[:, DRAFT - KCONV + 1 :] = edge_ssm[...].astype(F32)
        row = iota((rows, rows), 0)
        col = iota((rows, rows), 1)
        request = row >> 3
        taken = jnp.zeros((rows, rows), jnp.int32)
        for r in range(count):
            taken = jnp.where(request == r, accepted_in[r], taken)
        same = request == (col >> 3)
        lower = same & ((col & 7) <= (row & 7))
        before = same & ((col & 7) < taken)
        raw = mm_t(norm, w_step[...]).astype(BF16).astype(F32) + head_rows[0:1]
        lengths = jnp.zeros((rows, heads), jnp.int32)
        chosen = jnp.zeros((rows, heads), jnp.int32)
        hrow = iota((rows, heads), 0)
        for r in range(count):
            lengths = jnp.where((hrow >> 3) == r, lengths_in[r], lengths)
            chosen = jnp.where((hrow >> 3) == r, accepted_in[r], chosen)
        soft = jnp.maximum(raw, 0.0) + jnp.log1p(jnp.exp(-jnp.abs(raw)))
        size = jnp.where((hrow & 7) < lengths, soft, 0.0)
        rate = -jnp.exp(head_rows[1:2])
        cum = mm(lower.astype(F32), size, HIGH)
        upto = mm(before.astype(F32), size, HIGH)
        weight = jnp.where(
            (hrow & 7) < chosen, jnp.exp(jnp.minimum(rate * (upto - cum), 0.0)) * size, 0.0
        )
        stacked = jnp.concatenate(
            [
                rate * cum,
                size,
                weight,
                jnp.exp(rate * upto),
                jnp.broadcast_to(head_rows[2:3], (16, heads)),
            ],
            axis=0,
        )
        for part in range(3):
            piece = stacked.astype(BF16)
            quant[part] = piece
            stacked = stacked - piece.astype(F32)
        sel_rows = jnp.where(
            same & ((row & 7) < KCONV - 1),
            ((col & 7) == (row & 7) + taken - 3).astype(F32),
            0.0,
        ).astype(BF16)
        sel_edge = jnp.where(
            same & ((row & 7) < KCONV - 1),
            ((col & 7) == (row & 7) + taken + 5).astype(F32),
            0.0,
        ).astype(BF16)
        select[0] = sel_rows
        select[1] = sel_edge
        ssm = jnp.concatenate([mm(norm, w_ssm[0]), mm(norm, w_ssm[1])], axis=1).astype(BF16)
        before_ssm = edge_pad[...]
        conv = conv_rows(
            ssm.astype(F32).reshape(count, DRAFT, 2 * NSTATE),
            before_ssm,
            taps_ssm[...].astype(F32),
            bias_ssm[...],
        )
        both = silu(conv).reshape(rows, 2 * NSTATE).astype(BF16)
        bmat = both[:, :NSTATE]
        cvec = both[:, NSTATE:]
        cmat[...] = cvec.astype(F32)
        pair = jnp.where(lower, mm_t(cvec, bmat), 0.0)
        fold = ((iota((rows, NSTATE), 0) & 7) == iota((rows, NSTATE), 1)).astype(F32)
        gmat[...] = mm(pair, fold, HIGH)
        kept = mm(sel_rows, ssm) + mm(
            sel_edge, before_ssm.reshape(rows, 2 * NSTATE).astype(BF16)
        )
        wide_b = bmat.astype(F32)
        place = iota((DRAFT, NSTATE), 0)
        for r in range(count):
            own = kept[r * DRAFT : (r + 1) * DRAFT]
            packed = jnp.where(
                place < 3,
                own[:, :NSTATE],
                jnp.where(
                    place < 6,
                    pltpu.roll(own[:, NSTATE:], 3, 0),
                    jnp.full((DRAFT, NSTATE), (table[1, r] + 1).astype(F32)),
                ),
            )
            boxes[table[0, r], :, :NSTATE] = jnp.concatenate(
                [wide_b[r * DRAFT : (r + 1) * DRAFT], packed], axis=0
            ).astype(BF16)
        for k in range(WINDOW):
            corr[k][:, width:] = boxes[k, :, :NSTATE]

    norm = normed[...]
    inner = mm(norm, w_inner[...]).astype(BF16)
    gate = mm(norm, w_gate[...]).astype(BF16).astype(F32)
    edge_pad[:, DRAFT - KCONV + 1 :] = edge_inner[...].astype(F32)
    edges = edge_pad[...]
    conv = conv_rows(
        inner.astype(F32).reshape(count, DRAFT, TILE),
        edges,
        taps_inner[...].astype(F32),
        vector_tile[1:2],
    )
    x = silu(conv).reshape(rows, TILE).astype(BF16).astype(F32)
    first_head = step * (TILE // HEAD_DIM)
    spread = (
        iota((heads, TILE), 0) == first_head + (iota((heads, TILE), 1) >> 6)
    ).astype(BF16)
    expanded = mm(quant[0], spread) + mm(quant[1], spread) + mm(quant[2], spread)
    level = expanded[:rows]
    weighted = expanded[rows : 2 * rows] * x
    past = jnp.concatenate(
        [
            mm_t(cmat[r * DRAFT : (r + 1) * DRAFT].astype(BF16), states[r])
            for r in range(count)
        ],
        axis=0,
    )
    out = jnp.exp(level) * past + expanded[4 * rows : 4 * rows + 1] * x
    level3 = level.reshape(count, DRAFT, TILE)
    weighted3 = weighted.reshape(count, DRAFT, TILE)
    total = jnp.zeros((count, DRAFT, TILE), F32)
    for u in range(DRAFT):
        factor = jnp.exp(jnp.minimum(level3 - level3[:, u : u + 1], 0.0))
        share = gmat[:, u : u + 1].reshape(count, DRAFT, 1)
        total = total + share * factor * weighted3[:, u : u + 1]
    out = (out + total.reshape(rows, TILE)).astype(BF16).astype(F32)
    gated = out * silu(gate)
    squared = gated * gated
    squares[...] += squared[:, :128] + squared[:, 128:]
    acc[...] += mm((gated * vector_tile[2:3]).astype(BF16), w_out[...])
    delta = expanded[2 * rows : 3 * rows] * x
    decay = expanded[3 * rows : 4 * rows]
    decay_hi = decay.astype(BF16).astype(F32)
    second = mm(select[0], inner) + mm(select[1], edges.reshape(rows, TILE).astype(BF16))
    place = iota((rows, TILE), 0) & 7
    second = jnp.where(
        place == 3, decay_hi, jnp.where(place == 4, decay - decay_hi, second)
    )
    for r in range(count):
        span = slice(r * DRAFT, (r + 1) * DRAFT)
        boxes[table[0, r]] = jnp.concatenate([delta[span], second[span]], axis=0).astype(BF16)
    here = pl.ds(pl.multiple_of(step * TILE, TILE), TILE)
    for k in range(WINDOW):
        corr[k][:, here] = boxes[k]

    @pl.when(step == last)
    def _():
        total_square = jnp.broadcast_to(
            jnp.sum(squares[...], axis=1, keepdims=True), squares.shape
        )
        mine[:, half:] = total_square
        theirs[:, half:] = total_square

        @pl.when(table[2, 0] == 0)
        def _():
            mine[:, :half] = acc[:, :half]
            theirs[:, :half] = acc[:, half:]

        @pl.when(table[2, 0] != 0)
        def _():
            mine[:, :half] = acc[:, half:]
            theirs[:, :half] = acc[:, :half]


def front(count, heads, width, depth, args):
    rows = count * DRAFT
    tiles = width // TILE

    def whole(shape):
        return pl.BlockSpec(shape, lambda j: (0,) * len(shape))

    in_specs = [
        *[pl.BlockSpec(memory_space=pltpu.SMEM)] * 3,
        whole((2, rows, depth // 2)),
        whole((3, depth)),
        pl.BlockSpec((depth, TILE), lambda j: (0, j)),
        pl.BlockSpec((depth, TILE), lambda j: (0, j)),
        pl.BlockSpec((TILE, depth), lambda j: (j, 0)),
        whole((2, depth, NSTATE)),
        whole((heads, depth)),
        whole((3, heads)),
        pl.BlockSpec((KCONV, TILE), lambda j: (0, j)),
        pl.BlockSpec((3, TILE), lambda j: (0, j)),
        whole((KCONV, 2 * NSTATE)),
        whole((1, 2 * NSTATE)),
        pl.BlockSpec((count, TILE, NSTATE), lambda j: (0, j, 0)),
        pl.BlockSpec((count, KCONV - 1, TILE), lambda j: (0, 0, j)),
        whole((count, KCONV - 1, 2 * NSTATE)),
    ]
    out_width = depth // 2 + 128
    out_shape = [jax.ShapeDtypeStruct((rows, out_width), F32)] * 2 + [
        jax.ShapeDtypeStruct((2 * DRAFT, width + EXTRA), BF16)
    ] * WINDOW
    out_specs = [whole((rows, out_width))] * 2 + [whole((2 * DRAFT, width + EXTRA))] * WINDOW
    return pl.pallas_call(
        functools.partial(front_kernel, count, heads),
        grid=(tiles,),
        in_specs=in_specs,
        out_specs=out_specs,
        out_shape=out_shape,
        scratch_shapes=[
            pltpu.VMEM((rows, depth), BF16),
            pltpu.VMEM((rows, depth), F32),
            pltpu.VMEM((rows, 128), F32),
            pltpu.VMEM((3, 4 * rows + 16, heads), BF16),
            pltpu.VMEM((rows, NSTATE), F32),
            pltpu.VMEM((rows, NSTATE), F32),
            pltpu.VMEM((2, rows, rows), BF16),
            pltpu.VMEM((WINDOW, 2 * DRAFT, TILE), BF16),
            pltpu.VMEM((count, DRAFT, TILE), F32),
        ],
        compiler_params=pltpu.CompilerParams(dimension_semantics=("arbitrary",)),
        cost_estimate=SMALL,
        name="front",
    )(*args)


def pick_kernel(count, peers, destination, states, *outs):
    picked = outs[: len(RAW)]
    table, sems = outs[len(RAW) :]
    here = lax.axis_index("req")
    reach = [
        lax.rem(lax.div(destination[r], count) - here + peers, peers) for r in range(count)
    ]
    index = []
    for k in range(WINDOW):
        index.append(sum((reach[r] == k).astype(jnp.int32) * r for r in range(count)))
        table[3, k] = index[k]
    copies = []
    for n, k in enumerate(RAW):
        copy = pltpu.make_async_copy(states.at[index[k]], picked[n], sems.at[n])
        copy.start()
        copies.append(copy)
    for r in range(count):
        table[0, r] = reach[r]
        table[1, r] = lax.rem(destination[r], count)
        table[2, r] = lax.axis_index("head")
    for copy in copies:
        copy.wait()


def in_hbm():
    return pl.BlockSpec(memory_space=pl.ANY)


def in_vmem():
    return pl.BlockSpec(memory_space=pltpu.VMEM)


def in_smem():
    return pl.BlockSpec(memory_space=pltpu.SMEM)


def pick(count, width, peers, destination, states):
    return pl.pallas_call(
        functools.partial(pick_kernel, count, peers),
        in_specs=[in_smem(), in_hbm()],
        out_specs=[in_vmem()] * len(RAW) + [in_smem()],
        out_shape=[jax.ShapeDtypeStruct((width, NSTATE), BF16)] * len(RAW)
        + [jax.ShapeDtypeStruct((4, max(count, WINDOW)), jnp.int32)],
        scratch_shapes=[pltpu.SemaphoreType.DMA((len(RAW),))],
        cost_estimate=SMALL,
        name="pick",
    )(destination, states)


def advance(corr, state, out):
    width = state.shape[0]
    line = iota((2 * DRAFT, NSTATE), 0)
    bmat = jnp.where(line < DRAFT, corr[:, width:].astype(F32), 0.0)
    ones = jnp.where((line == 11) | (line == 12), 1.0, 0.0)
    right = jnp.concatenate([bmat, ones], axis=1).astype(BF16)
    part = width // PARTS
    for c in range(PARTS):
        span = slice(c * part, (c + 1) * part)
        both = lax.dot_general(
            corr[:, span], right, (((0,), (0,)), ((), ())), preferred_element_type=F32
        )
        out[span] = (both[:, NSTATE:] * state[span].astype(F32) + both[:, :NSTATE]).astype(BF16)


def tail_rows(width):
    tiles = width // NSTATE
    groups = tiles // 2 + 1
    return groups, (groups + groups % 2) * DRAFT


def finish_kernel(offsets, *refs):
    n = len(offsets)
    table, states = refs[:2]
    corr = refs[2 : 2 + n]
    outs = refs[2 + n : 2 + 2 * n]
    loaded, sems = refs[-2:]
    width = loaded.shape[1]
    groups, _ = tail_rows(width)
    copies = []
    for i, k in enumerate(offsets):
        copy = pltpu.make_async_copy(states.at[table[3, k]], loaded.at[i], sems.at[i])
        copy.start()
        copies.append(copy)
    for i in range(n):
        low = corr[i][...].astype(F32)[DRAFT:]
        half = iota((DRAFT, NSTATE), 0) < DRAFT // 2
        tiles = [low[:, t * NSTATE : (t + 1) * NSTATE] for t in range(width // NSTATE + 1)]
        packed = [
            jnp.where(half, tiles[2 * g], pltpu.roll(tiles[2 * g + 1], DRAFT // 2, 0))
            for g in range(groups - 1)
        ]
        packed.append(tiles[-1])
        if groups % 2:
            packed.append(jnp.zeros((DRAFT, NSTATE), F32))
        for g in range(0, len(packed), 2):
            block = jnp.concatenate(packed[g : g + 2], axis=0)
            outs[i][width + g * DRAFT : width + (g + 2) * DRAFT] = block.astype(BF16)
        copies[i].wait()
        advance(corr[i], loaded.at[i], outs[i])


def finish(offsets, table, states, corr):
    n = len(offsets)
    width = states.shape[1]
    shape = jax.ShapeDtypeStruct((width + tail_rows(width)[1], NSTATE), BF16)
    return pl.pallas_call(
        functools.partial(finish_kernel, offsets),
        in_specs=[in_smem(), in_hbm()] + [in_vmem()] * n,
        out_specs=[in_vmem()] * n,
        out_shape=[shape] * n,
        scratch_shapes=[
            pltpu.VMEM((n, width, NSTATE), BF16),
            pltpu.SemaphoreType.DMA((n,)),
        ],
        cost_estimate=SMALL,
        compiler_params=pltpu.CompilerParams(vmem_limit_bytes=ROOM if n == 1 else None),
        name="finish",
    )(table, states, *[corr[k] for k in offsets])


def mark_of(low):
    return jnp.max(low[6:7]).astype(jnp.int32) - 1


def merge_kernel(own, *refs):
    table, states = refs[:2]
    raw = refs[2]
    corr = refs[3 : 4 + own]
    _, kept, loaded, merged, sem_in, sem_out = refs[4 + own :]
    width = loaded.shape[0]
    if own:
        copy = pltpu.make_async_copy(states.at[table[3, 0]], loaded, sem_in)
        copy.start()
    slots = [mark_of(ref[:, width:].astype(F32)[DRAFT:]) for ref in corr]

    def put(i):
        return pltpu.make_async_copy(merged.at[i], kept.at[slots[i]], sem_out.at[i])

    for i in range(1 + own):
        if i == 1:
            copy.wait()

        @pl.when(slots[i] >= 0)
        def _(i=i):
            advance(corr[i], loaded if i == 1 else raw, merged.at[i])
            put(i).start()

    for i in range(1 + own):

        @pl.when(slots[i] >= 0)
        def _(i=i):
            put(i).wait()


def merge(count, table, states, raw, corr, kept):
    width = states.shape[1]
    n = len(corr)
    return pl.pallas_call(
        functools.partial(merge_kernel, n - 1),
        in_specs=[in_smem(), in_hbm()] + [in_vmem()] * (1 + n) + [in_hbm()],
        out_specs=in_hbm(),
        out_shape=jax.ShapeDtypeStruct((count, width, NSTATE), BF16),
        scratch_shapes=[
            pltpu.VMEM((width, NSTATE), BF16),
            pltpu.VMEM((n, width, NSTATE), BF16),
            pltpu.SemaphoreType.DMA,
            pltpu.SemaphoreType.DMA((n,)),
        ],
        input_output_aliases={3 + n: 0},
        cost_estimate=SMALL,
        compiler_params=pltpu.CompilerParams(vmem_limit_bytes=ROOM),
        name="merge",
    )(table, states, raw, *corr, kept)


def halves(ref, width):
    groups, _ = tail_rows(width)
    tiles = []
    for row in range(width, ref.shape[0], 2 * DRAFT):
        block = ref[row : row + 2 * DRAFT].astype(F32)
        for part in (block[:DRAFT], block[DRAFT:]):
            if len(tiles) < 2 * (groups - 1):
                tiles += [part, pltpu.roll(part, DRAFT // 2, 0)]
            else:
                tiles.append(part)
    return tiles[: 2 * groups - 1]


def place_kernel(n, earlier, *refs):
    messages = refs[:n]
    out = len(refs) - 4
    corr = refs[n : out - 3 * earlier]
    kept, out_inner, out_ssm, sems = refs[out:]
    width = out_inner.shape[2]
    tiles = width // NSTATE
    if earlier:
        out_inner[...] = refs[out - 2][...]
        out_ssm[...] = refs[out - 1][...]
    lows = [halves(ref, width) for ref in messages]
    slots = [mark_of(low[tiles]) for low in lows]

    def put(i):
        return pltpu.make_async_copy(
            messages[i].at[pl.ds(0, width)], kept.at[slots[i]], sems.at[i]
        )

    for i in range(n):

        @pl.when(slots[i] >= 0)
        def _(i=i):
            put(i).start()

    def write_edges(slot, inner, low):
        out_inner[slot] = inner[: KCONV - 1].astype(BF16)
        high = pltpu.roll(low, DRAFT - 3, 0)
        out_ssm[slot] = jnp.concatenate([low[:3], high[:3]], axis=1).astype(BF16)

    for ref in corr:
        low = ref[...].astype(F32)[DRAFT:]
        slot = mark_of(low[:, width:])

        @pl.when(slot >= 0)
        def _(slot=slot, low=low):
            write_edges(slot, low[:, :width], low[:, width:])

    for i in range(n):

        @pl.when(slots[i] >= 0)
        def _(i=i):
            write_edges(slots[i], jnp.concatenate(lows[i][:tiles], axis=1), lows[i][tiles])

    for i in range(n):

        @pl.when(slots[i] >= 0)
        def _(i=i):
            put(i).wait()


def place(count, width, messages, corr, earlier=()):
    n = len(messages)
    inputs = [*messages, *corr]
    return pl.pallas_call(
        functools.partial(place_kernel, n, 1 if earlier else 0),
        in_specs=[in_vmem()] * len(inputs)
        + ([in_hbm(), in_vmem(), in_vmem()] if earlier else []),
        out_specs=[in_hbm(), in_vmem(), in_vmem()],
        out_shape=[
            jax.ShapeDtypeStruct((count, width, NSTATE), BF16),
            jax.ShapeDtypeStruct((count, KCONV - 1, width), BF16),
            jax.ShapeDtypeStruct((count, KCONV - 1, 2 * NSTATE), BF16),
        ],
        input_output_aliases={len(inputs): 0} if earlier else {},
        scratch_shapes=[pltpu.SemaphoreType.DMA((n,))],
        cost_estimate=SMALL,
        compiler_params=pltpu.CompilerParams(vmem_limit_bytes=ROOM),
        name="place",
    )(*inputs, *earlier)


def moved(array, by):
    length = lax.axis_size("req")
    return lax.ppermute(array, "req", [(i, (i + by) % length) for i in range(length)])


def local(
    hidden_in,
    norm_gain,
    proj_gate,
    proj_inner,
    proj_ssm,
    proj_step,
    step_bias,
    decay_log,
    skip_gain,
    conv_inner,
    conv_inner_bias,
    conv_ssm,
    conv_ssm_bias,
    gate_gain,
    proj_out,
    states_in,
    edge_inner,
    edge_ssm,
    draft_lengths,
    accepted,
    destination,
):
    count, heads = states_in.shape[:2]
    depth, width = proj_inner.shape
    peers = lax.axis_size("req")
    flat = states_in.reshape(count, width, NSTATE)
    *raws, table = pick(count, width, peers, destination, flat)
    raws = [moved(raw, k) for raw, k in zip(raws, RAW)]
    table, ready, ready_ssm = lax.optimization_barrier((table, hidden_in, proj_ssm))
    vectors = jnp.stack([norm_gain, conv_inner_bias, gate_gain])
    results = front(
        count,
        heads,
        width,
        depth,
        (
            table,
            draft_lengths,
            accepted,
            lax.all_gather(ready, "head", axis=0, tiled=False),
            vectors,
            proj_gate,
            proj_inner,
            proj_out,
            lax.all_gather(ready_ssm, "head", axis=0, tiled=False),
            proj_step.T,
            jnp.stack([step_bias, decay_log, skip_gain]),
            conv_inner,
            vectors,
            conv_ssm,
            conv_ssm_bias.reshape(1, 2 * NSTATE),
            flat,
            edge_inner,
            edge_ssm,
        ),
    )
    mine, theirs = results[:2]
    corr = list(results[2:])
    sixth, fifth, fourth, third = finish((6, 5, 4, 3), table, flat, corr)
    *raws, corr[7], sixth, fifth, fourth, third, later = lax.optimization_barrier(
        (*raws, corr[7], sixth, fifth, fourth, third, table)
    )
    sixth = moved(sixth, 6)
    fifth = moved(fifth, 5)
    fourth = moved(fourth, 4)
    third = moved(third, 3)
    corr[7] = moved(corr[7], 7)
    (first,) = finish((1,), later, flat, corr)

    pair = lax.all_gather(theirs, "head", axis=0, tiled=False)
    other = jnp.where(lax.axis_index("head") == 0, pair[1], pair[0])
    total = mine + other
    half = depth // 2
    scale = lax.rsqrt(total[:, half : half + 1] / DINNER + epsilon)
    hidden_out = (hidden_in.astype(F32) + total[:, :half] * scale).astype(BF16)

    corr[7], corr[2] = lax.optimization_barrier((corr[7], corr[2]))
    corr[2] = moved(corr[2], 2)
    sixth, fifth, fourth, third, corr[7], first = lax.optimization_barrier(
        (sixth, fifth, fourth, third, corr[7], first)
    )
    first = moved(first, 1)
    kept, edges, edges_ssm = place(
        count, width, (sixth, fifth, fourth, third), (corr[0], corr[7])
    )
    kept = merge(count, table, flat, raws[0], (corr[7], corr[0]), kept)
    kept = merge(count, table, flat, raws[1], (corr[2],), kept)
    kept, kept_inner, kept_ssm = place(
        count, width, (first,), (corr[2],), (kept, edges, edges_ssm)
    )
    return (hidden_out, kept.reshape(states_in.shape), kept_inner, kept_ssm)


def solution(mesh):
    in_specs = (
        P("req", "head"),
        P(),
        P(None, "head"),
        P(None, "head"),
        P(None, "head"),
        P(None, "head"),
        P("head"),
        P("head"),
        P("head"),
        P(None, "head"),
        P("head"),
        P(),
        P(),
        P("head"),
        P("head", None),
        P("req", "head", None, None),
        P("req", None, "head"),
        P("req", None, None),
        P("req"),
        P("req"),
        P("req"),
    )
    out_specs = (
        P("req", "head"),
        P("req", "head", None, None),
        P("req", None, "head"),
        P("req", None, None),
    )
    return jax.shard_map(local, mesh=mesh, in_specs=in_specs, out_specs=out_specs, check_vma=False)
```
